32 devices in a mesh: rep: 4 (over x, core), fsdp: 8 (over z, y).
Axes of the slice: x: 2, y: 2, z: 4, core: 2. Of those that a mesh axis runs over, the one named last changes fastest.
Arguments:
- patches: bfloat16 [32, 1024, 768], P(('rep', 'fsdp')), may hold values from -6 to 6
- lengths: int32 [32], P(('rep', 'fsdp')), may hold values from 256 to 1024, as said below
- tasks: int32 [32], P(('rep', 'fsdp')), may hold values from 0 to 2
- w_query: bfloat16 [768, 768], P('fsdp'), may hold values from -0.21875 to 0.21875
- w_key: bfloat16 [768, 768], P('fsdp'), may hold values from -0.21875 to 0.21875
- w_value: bfloat16 [768, 768], P('fsdp'), may hold values from -0.21875 to 0.21875
- w_out: bfloat16 [768, 768], P('fsdp'), may hold values from -1.25 to 1.25
- w_gate: bfloat16 [768, 2048], P('fsdp'), may hold values from -0.21875 to 0.21875
- w_up: bfloat16 [768, 2048], P('fsdp'), may hold values from -0.21875 to 0.21875
- w_down: bfloat16 [2048, 768], P('fsdp'), may hold values from -0.125 to 0.125
- gain_attn: bfloat16 [768], P('fsdp'), may hold values from 0.5 to 1.5
- gain_mlp: bfloat16 [768], P('fsdp'), may hold values from 0.5 to 1.5
- task_table: bfloat16 [768, 3], P('fsdp'), may hold values from -4 to 4
- cotangent: bfloat16 [32, 1024, 768], P(('rep', 'fsdp')), may hold values from -8 to 8
Outputs:
- output: bfloat16 [32, 1024, 768], P(('rep', 'fsdp'))
- grad_patches: float32 [32, 1024, 768], P(('rep', 'fsdp'))
- grad_query: float32 [768, 768], P('fsdp')
- grad_key: float32 [768, 768], P('fsdp')
- grad_value: float32 [768, 768], P('fsdp')
- grad_out: float32 [768, 768], P('fsdp')
- grad_gate: float32 [768, 2048], P('fsdp')
- grad_up: float32 [768, 2048], P('fsdp')
- grad_down: float32 [2048, 768], P('fsdp')
- grad_gain_attn: float32 [768], P('fsdp')
- grad_gain_mlp: float32 [768], P('fsdp')
- grad_table: float32 [768, 3], P('fsdp')
The draws below stay inside these ranges and needn't reach their ends.
Inputs may be any that keep to these rules, and one draw needn't show every extreme that they name: `lengths`: in every draw some chart has all 1024 patches valid.
All inputs are finite; a program needn't handle non-finite values.
Results may differ from the reference program's by a relative error of at most 0.017.
Values may be sent and summed in bfloat16 or wider, within the bound.
A program may use at most 320 MiB of HBM per device.

```python
import jax
import jax.numpy as jnp
from jax import lax

D = 768
HEADS = 12
HEAD_DIM = 64
FF = 2048
TASKS = 3
SEQ = 1024
CHARTS = 32


def draw_lengths(key, part):
    key = jax.random.fold_in(key, 11)
    first, second = jax.random.split(key)
    drawn = jax.random.randint(first, (CHARTS,), SEQ // 4, SEQ + 1)
    chosen = jax.random.randint(second, (), 0, CHARTS)
    return jnp.where(jnp.arange(CHARTS) == chosen, SEQ, drawn).astype(jnp.int32)


def draw_cotangent(key, part):
    key = jax.random.fold_in(key, 23)
    ramp = jnp.arange(CHARTS, dtype=jnp.float32) / max(CHARTS - 1, 1)
    base = jnp.clip(jax.random.normal(key, (CHARTS, SEQ, D), jnp.float32), -4.0, 4.0)
    factor = 0.6 + 1.2 * ramp
    return (base * factor[:, None, None]).astype(jnp.bfloat16)


def with_ends(entries, stream_key, smallest, high):
    longest = entries.shape.index(max(entries.shape))
    spots = []
    for shift in (0, 1):
        where = [jax.random.randint(jax.random.fold_in(stream_key, axis), (), 0, length) for axis, length in enumerate(entries.shape)]
        where[longest] = (where[longest] + shift) % entries.shape[longest]
        spots.append(tuple(where))
    return entries.at[spots[0]].set(smallest).at[spots[1]].set(high)


def shard_levels(key, extent, cuts, smallest, largest):
    def one(axis_at, blocks):
        draws = jax.random.uniform(jax.random.fold_in(jax.random.fold_in(key, 6), axis_at), (blocks,), jnp.float32, smallest / len(cuts), largest / len(cuts))
        return jnp.repeat(jnp.exp(draws), extent[axis_at] // blocks).reshape((-1,) + (1,) * (len(extent) - axis_at - 1))

    level = one(*cuts[0])
    for cut in cuts[1:]:
        level = level * one(*cut)
    return level


def centred(stream_key, shape, deviation, reach, shards=(), kind=jnp.bfloat16):
    values = jax.random.normal(stream_key, shape, jnp.float32) * deviation
    if len(shards) > 0:
        values = shard_levels(stream_key, shape, shards, -0.22, 0.18) * values
    return jnp.clip(values, min=-reach, max=reach).astype(kind)


def setup_inputs(seed: int = 0) -> dict:
    key_of = jax.random.split(jax.random.key(seed), 15)
    return {
        "patches": centred(key_of[0], (CHARTS, SEQ, D), 1.0, 6.0, ((0, 32),)),
        "lengths": draw_lengths(jax.random.fold_in(key_of[14], 71), 0),
        "tasks": with_ends(jax.random.randint(key_of[2], (CHARTS,), 0, TASKS), jax.random.fold_in(key_of[2], 1), 0, TASKS - 1).astype(jnp.int32),
        "w_query": centred(key_of[3], (D, D), D ** -0.5, 0.21875, ((0, 8),)),
        "w_key": centred(key_of[4], (D, D), D ** -0.5, 0.21875, ((0, 8),)),
        "w_value": centred(key_of[5], (D, D), D ** -0.5, 0.21875, ((0, 8),)),
        "w_out": centred(key_of[6], (D, D), (D * 32 // SEQ) ** -0.5, 1.25, ((0, 8),)),
        "w_gate": centred(key_of[7], (D, FF), D ** -0.5, 0.21875, ((0, 8),)),
        "w_up": centred(key_of[8], (D, FF), D ** -0.5, 0.21875, ((0, 8),)),
        "w_down": centred(key_of[9], (FF, D), FF ** -0.5, 0.125, ((0, 8),)),
        "gain_attn": jnp.clip(1.0 + 0.1 * jax.random.normal(key_of[10], (D,), jnp.float32), 0.5, 1.5).astype(jnp.bfloat16),
        "gain_mlp": jnp.clip(1.0 + 0.1 * jax.random.normal(key_of[11], (D,), jnp.float32), 0.5, 1.5).astype(jnp.bfloat16),
        "task_table": centred(key_of[12], (D, TASKS), 1.0, 4.0, ((0, 8),)),
        "cotangent": draw_cotangent(jax.random.fold_in(key_of[14], 71), 0),
    }


EPS = 1e-06

@jax.custom_vjp
def low(v):
    return lax.optimization_barrier(v.astype(jnp.bfloat16)).astype(jnp.float32)

@jax.custom_vjp
def low_back(v):
    return v

def low_keep(v):
    return (low(v), None)

def low_pass(kept, grad):
    return (grad,)

def back_keep(v):
    return (v, None)

def back_low(kept, grad):
    return (low(grad),)
low.defvjp(low_keep, low_pass)
low_back.defvjp(back_keep, back_low)

def product(left, right):
    return jnp.dot(left, right, precision=lax.Precision.HIGHEST)

def normalize(resid, gain):
    return resid * lax.rsqrt(lax.optimization_barrier(jnp.mean(resid * resid, axis=-1, keepdims=True)) + EPS) * gain

def chart_layer(source, length, task, w_query, w_key, w_value, w_out, w_gate, w_up, w_down, gain_attn, gain_mlp, task_table):
    picked = (jnp.arange(TASKS) == task).astype(jnp.float32)
    resid = source + product(task_table, picked)[None, :]
    normed = low(normalize(resid, gain_attn))
    query = low(low_back(product(normed, w_query))).reshape(SEQ, HEADS, HEAD_DIM)
    keys = low(low_back(product(normed, w_key))).reshape(SEQ, HEADS, HEAD_DIM)
    values = low(low_back(product(normed, w_value))).reshape(SEQ, HEADS, HEAD_DIM)
    valid = (jnp.arange(SEQ) < length)[None, None, :]
    span = min(512, SEQ)
    scale = HEAD_DIM ** (-0.5)

    def attend(rows):
        raw = jnp.einsum('qhd,khd->hqk', rows, keys, precision=lax.Precision.HIGHEST) * scale
        scores = jnp.where(valid, low_back(raw), -1e+30)
        top = lax.optimization_barrier(jnp.max(scores, axis=-1, keepdims=True))
        expd = jnp.exp(scores - top)
        probs = low(expd / lax.optimization_barrier(jnp.sum(expd, axis=-1, keepdims=True)))
        return jnp.einsum('hqk,khd->qhd', probs, values, precision=lax.Precision.HIGHEST)
    context = lax.map(jax.checkpoint(attend), query.reshape(SEQ // span, span, HEADS, HEAD_DIM))
    context = low(low_back(context.reshape(SEQ, D)))
    mixed = resid + low_back(product(context, w_out))
    normed_two = low(normalize(mixed, gain_mlp))
    gate = low_back(product(normed_two, w_gate))
    up = low_back(product(normed_two, w_up))
    hidden = low(jax.nn.gelu(gate, approximate=True) * up)
    return mixed + low_back(product(hidden, w_down))

def reference(patches, lengths, tasks, w_query, w_key, w_value, w_out, w_gate, w_up, w_down, gain_attn, gain_mlp, task_table, cotangent):
    params = tuple((w.astype(jnp.float32) for w in (w_query, w_key, w_value, w_out, w_gate, w_up, w_down, gain_attn, gain_mlp, task_table)))

    def forward(source, *weights):

        def advance(carry, item):
            return (carry, chart_layer(item[0], item[1], item[2], *weights))
        _, result = lax.scan(jax.checkpoint(advance), jnp.zeros((), jnp.float32), (source, lengths, tasks))
        return result
    result, pull = jax.vjp(forward, patches.astype(jnp.float32), *params)
    grads = pull(cotangent.astype(jnp.float32))
    return (result.astype(jnp.bfloat16), grads[0], grads[1], grads[2], grads[3], grads[4], grads[5], grads[6], grads[7], grads[8], grads[9], grads[10])
```

```python
import functools

import jax
import jax.numpy as jnp
from jax import lax
from jax.experimental import pallas as pl
from jax.experimental.pallas import tpu as pltpu
from jax.sharding import PartitionSpec as P

HEADS = 12
HEAD_DIM = 64


EPS = 1e-06
FAR = -1e30


def normalize(resid, gain):
    return resid * lax.rsqrt(jnp.mean(resid * resid, axis=-1, keepdims=True) + EPS) * gain


def gated(gate, up):
    return jax.nn.gelu(gate, approximate=True) * up


def matmul(left, right):
    return jnp.dot(left, right, preferred_element_type=jnp.float32)


def matmul_back(left, right):
    return lax.dot_general(
        left, right, (((1,), (1,)), ((), ())), preferred_element_type=jnp.float32
    )


def outer_sum(left, right):
    return lax.dot_general(
        left, right, (((0,), (0,)), ((), ())), preferred_element_type=jnp.float32
    )


def plain(
    patches,
    lengths,
    tasks,
    w_query,
    w_key,
    w_value,
    w_out,
    w_gate,
    w_up,
    w_down,
    gain_attn,
    gain_mlp,
    task_table,
    cotangent,
):
    gathered = (
        lax.all_gather(w_query, "fsdp", axis=0, tiled=True),
        lax.all_gather(w_key, "fsdp", axis=0, tiled=True),
        lax.all_gather(w_value, "fsdp", axis=0, tiled=True),
        lax.all_gather(w_out, "fsdp", axis=0, tiled=True),
        lax.all_gather(w_gate, "fsdp", axis=0, tiled=True),
        lax.all_gather(w_up, "fsdp", axis=0, tiled=True),
        lax.all_gather(w_down, "fsdp", axis=0, tiled=True),
        lax.all_gather(gain_attn, "fsdp", axis=0, tiled=True),
        lax.all_gather(gain_mlp, "fsdp", axis=0, tiled=True),
        lax.all_gather(task_table, "fsdp", axis=0, tiled=True),
    )
    query_w, key_w, value_w, out_w, gate_w, up_w, down_w, gain_one, gain_two, table = gathered
    source = patches[0].astype(jnp.float32)
    count, width = source.shape
    scale = HEAD_DIM ** (-0.5)
    span = min(512, count)
    blocks = count // span
    gain_one = gain_one.astype(jnp.float32)
    gain_two = gain_two.astype(jnp.float32)
    picked = (jnp.arange(table.shape[1]) == tasks[0]).astype(jnp.float32)
    resid = source + jnp.sum(table.astype(jnp.float32) * picked[None, :], axis=1)[None, :]
    normed = normalize(resid, gain_one).astype(jnp.bfloat16)
    query = matmul(normed, query_w).astype(jnp.bfloat16).reshape(count, HEADS, HEAD_DIM)
    keys = matmul(normed, key_w).astype(jnp.bfloat16).reshape(count, HEADS, HEAD_DIM)
    values = matmul(normed, value_w).astype(jnp.bfloat16).reshape(count, HEADS, HEAD_DIM)
    valid = (jnp.arange(count) < lengths[0])[None, None, :]

    def scores_of(rows):
        raw = jnp.einsum("qhd,khd->hqk", rows, keys, preferred_element_type=jnp.float32) * scale
        return jnp.where(valid, raw, FAR)

    contexts = []
    logsums = []
    for index in range(blocks):
        rows = query[index * span : (index + 1) * span]
        scores = scores_of(rows)
        top = jnp.max(scores, axis=-1, keepdims=True)
        expd = jnp.exp(scores - top)
        total = jnp.sum(expd, axis=-1, keepdims=True)
        probs = (expd / total).astype(jnp.bfloat16)
        block_out = jnp.einsum("hqk,khd->qhd", probs, values, preferred_element_type=jnp.float32)
        contexts.append(block_out.reshape(span, width).astype(jnp.bfloat16))
        logsums.append(top + jnp.log(total))
    context = jnp.concatenate(contexts, axis=0)
    mixed = resid + matmul(context, out_w)
    normed_two = normalize(mixed, gain_two).astype(jnp.bfloat16)
    gate = matmul(normed_two, gate_w)
    up = matmul(normed_two, up_w)
    hidden = gated(gate, up).astype(jnp.bfloat16)
    output = (mixed + matmul(hidden, down_w)).astype(jnp.bfloat16)[None]
    fetched = (
        lax.all_gather(w_query, "fsdp", axis=0, tiled=True),
        lax.all_gather(w_key, "fsdp", axis=0, tiled=True),
        lax.all_gather(w_value, "fsdp", axis=0, tiled=True),
        lax.all_gather(w_out, "fsdp", axis=0, tiled=True),
        lax.all_gather(w_gate, "fsdp", axis=0, tiled=True),
        lax.all_gather(w_up, "fsdp", axis=0, tiled=True),
        lax.all_gather(w_down, "fsdp", axis=0, tiled=True),
        lax.all_gather(gain_attn, "fsdp", axis=0, tiled=True),
        lax.all_gather(gain_mlp, "fsdp", axis=0, tiled=True),
        lax.all_gather(task_table, "fsdp", axis=0, tiled=True),
    )
    query_w, key_w, value_w, out_w, gate_w, up_w, down_w, gain_one, gain_two, table = fetched
    gain_one = gain_one.astype(jnp.float32)
    gain_two = gain_two.astype(jnp.float32)
    upstream = cotangent[0].astype(jnp.float32)
    branch_grad = upstream.astype(jnp.bfloat16)
    grad_down = outer_sum(hidden, branch_grad)
    hidden_grad = matmul_back(branch_grad, down_w)
    _, pull_gated = jax.vjp(gated, gate, up)
    gate_grad, up_grad = pull_gated(hidden_grad)
    gate_grad = gate_grad.astype(jnp.bfloat16)
    up_grad = up_grad.astype(jnp.bfloat16)
    grad_gate = outer_sum(normed_two, gate_grad)
    grad_up = outer_sum(normed_two, up_grad)
    second_grad = matmul_back(gate_grad, gate_w) + matmul_back(up_grad, up_w)
    _, pull_second = jax.vjp(normalize, mixed, gain_two)
    mixed_grad, grad_gain_two = pull_second(second_grad)
    mixed_grad = mixed_grad + upstream
    attn_grad = mixed_grad.astype(jnp.bfloat16)
    grad_out = outer_sum(context, attn_grad)
    context_grad = (
        matmul_back(attn_grad, out_w).astype(jnp.bfloat16).reshape(count, HEADS, HEAD_DIM)
    )
    key_grad = jnp.zeros((count, HEADS, HEAD_DIM), jnp.float32)
    value_grad = jnp.zeros((count, HEADS, HEAD_DIM), jnp.float32)
    query_parts = []
    for index in range(blocks):
        rows = query[index * span : (index + 1) * span]
        back_rows = context_grad[index * span : (index + 1) * span]
        probs = jnp.exp(scores_of(rows) - logsums[index])
        probs_low = probs.astype(jnp.bfloat16)
        prob_grad = jnp.einsum(
            "qhd,khd->hqk", back_rows, values, preferred_element_type=jnp.float32
        )
        weighted = jnp.sum(probs * prob_grad, axis=-1, keepdims=True)
        score_grad = (probs * (prob_grad - weighted)).astype(jnp.bfloat16)
        query_parts.append(
            jnp.einsum("hqk,khd->qhd", score_grad, keys, preferred_element_type=jnp.float32) * scale
        )
        key_grad = (
            key_grad
            + jnp.einsum("hqk,qhd->khd", score_grad, rows, preferred_element_type=jnp.float32)
            * scale
        )
        value_grad = value_grad + jnp.einsum(
            "hqk,qhd->khd", probs_low, back_rows, preferred_element_type=jnp.float32
        )
    query_grad = jnp.concatenate(query_parts, axis=0).reshape(count, width).astype(jnp.bfloat16)
    key_grad = key_grad.reshape(count, width).astype(jnp.bfloat16)
    value_grad = value_grad.reshape(count, width).astype(jnp.bfloat16)
    grad_query = outer_sum(normed, query_grad)
    grad_key = outer_sum(normed, key_grad)
    grad_value = outer_sum(normed, value_grad)
    first_grad = (
        matmul_back(query_grad, query_w)
        + matmul_back(key_grad, key_w)
        + matmul_back(value_grad, value_w)
    )
    _, pull_first = jax.vjp(normalize, resid, gain_one)
    resid_grad, grad_gain_one = pull_first(first_grad)
    resid_grad = resid_grad + mixed_grad
    grad_table = jnp.sum(resid_grad, axis=0)[:, None] * picked[None, :]
    shares = (
        lax.psum_scatter(grad_query, "fsdp", scatter_dimension=0, tiled=True),
        lax.psum_scatter(grad_key, "fsdp", scatter_dimension=0, tiled=True),
        lax.psum_scatter(grad_value, "fsdp", scatter_dimension=0, tiled=True),
        lax.psum_scatter(grad_out, "fsdp", scatter_dimension=0, tiled=True),
        lax.psum_scatter(grad_gate, "fsdp", scatter_dimension=0, tiled=True),
        lax.psum_scatter(grad_up, "fsdp", scatter_dimension=0, tiled=True),
        lax.psum_scatter(grad_down, "fsdp", scatter_dimension=0, tiled=True),
        lax.psum_scatter(grad_gain_one, "fsdp", scatter_dimension=0, tiled=True),
        lax.psum_scatter(grad_gain_two, "fsdp", scatter_dimension=0, tiled=True),
        lax.psum_scatter(grad_table, "fsdp", scatter_dimension=0, tiled=True),
    )
    (
        share_query,
        share_key,
        share_value,
        share_out,
        share_gate,
        share_up,
        share_down,
        share_one,
        share_two,
        share_table,
    ) = shares
    summed = (
        lax.psum(share_query.astype(jnp.bfloat16), "rep").astype(jnp.float32),
        lax.psum(share_key.astype(jnp.bfloat16), "rep").astype(jnp.float32),
        lax.psum(share_value.astype(jnp.bfloat16), "rep").astype(jnp.float32),
        lax.psum(share_out.astype(jnp.bfloat16), "rep").astype(jnp.float32),
        lax.psum(share_gate.astype(jnp.bfloat16), "rep").astype(jnp.float32),
        lax.psum(share_up.astype(jnp.bfloat16), "rep").astype(jnp.float32),
        lax.psum(share_down.astype(jnp.bfloat16), "rep").astype(jnp.float32),
        lax.psum(share_one.astype(jnp.bfloat16), "rep").astype(jnp.float32),
        lax.psum(share_two.astype(jnp.bfloat16), "rep").astype(jnp.float32),
        lax.psum(share_table.astype(jnp.bfloat16), "rep").astype(jnp.float32),
    )
    return (
        output,
        resid_grad[None],
        summed[0],
        summed[1],
        summed[2],
        summed[3],
        summed[4],
        summed[5],
        summed[6],
        summed[7],
        summed[8],
        summed[9],
    )


EVENTS = {
    "pre": [("Y", 0), ("Z", 2), ("X", 0), ("Y", 1), ("Z", 3), ("C", 0), ("D", 0)],
    "forward": {
        0: [("X", 1), ("Y", 2), ("Z", 4)],
        1: [("C", 1), ("X", 2), ("Y", 3), ("Z", 5)],
        3: [("X", 3), ("C", 2), ("Y", 4), ("Z", 6)],
        4: [("D", 1), ("C", 3), ("X", 4), ("Y", 5), ("Z", 7)],
        7: [("Y", 6), ("X", 5), ("C", 4), ("Z", 8)],
        8: [("D", 2), ("Y", 7), ("X", 6), ("C", 5), ("Z", 9)],
        11: [("Y", 8), ("X", 7), ("C", 6)],
    },
    "attended": [("D", 3), ("F", 0), ("F", 1), ("F", 2)],
    "normed": [("Y", 9), ("X", 8), ("C", 7)],
    "tile": {
        0: [("D", 4), ("D", 5), ("D", 6), ("F", 4), ("F", 5), ("F", 6)],
        1: [("C", 9)],
        2: [("D", 7), ("D", 8), ("D", 9), ("F", 7), ("F", 8), ("F", 9), (0, 0), (0, 1), (0, 2)],
        3: [(1, 2)],
    },
    "tile_mid": {
        0: [("X", 9), ("C", 8)],
        2: [(1, 0), (1, 1)],
        3: [(2, 1), (2, 0)],
    },
    "ff_done": [(0, 3), (0, 4), (0, 5)],
    "second_back": [("F", 3), (2, 2), (3, 1), (3, 0), (1, 4)],
    "context_back": [(0, 6), (1, 3), (1, 5)],
    "backward": {
        0: [(1, 6), (2, 4), (3, 2), (4, 1), (4, 0)],
        1: [(2, 3)],
        2: [(2, 5), (3, 4), (5, 0), (5, 1)],
        3: [(0, 7), (4, 2), (2, 6)],
        4: [(3, 3), (1, 7), (3, 5), (4, 4), (6, 0)],
        5: [(3, 6), (4, 3), (5, 2)],
        6: [(2, 7), (4, 5), (5, 4), (4, 6)],
        7: [(0, 8), (5, 3), (5, 6), (6, 2)],
        8: [(1, 8), (3, 7), (5, 5), (6, 4)],
        9: [(2, 8), (4, 7), (6, 6)],
        10: [(3, 8), (5, 7)],
        11: [(0, 9), (4, 8)],
    },
    "attention_back": [(1, 9), (5, 8)],
    "tail_one": [(2, 9), (6, 8)],
    "tail_two": [(3, 9)],
    "tail_three": [(4, 9), (5, 9)],
}


BF16 = jnp.bfloat16
F32 = jnp.float32
MESH = pl.DeviceIdType.MESH
PAIR = 2


def dot(left, right, on_left, on_right):
    return lax.dot_general(
        left, right, (((on_left,), (on_right,)), ((), ())), preferred_element_type=F32
    )


def aligned(index, step):
    return pl.multiple_of(index, step)


class Place:
    def __init__(self, reps, group):
        self.reps, self.group, self.deep = reps, group, group // PAIR
        self.rep = lax.axis_index("rep")
        self.pos = lax.axis_index("fsdp")
        self.x, self.core = self.rep // PAIR, self.rep % PAIR
        self.z, self.y = self.pos // PAIR, self.pos % PAIR

    def sibling(self):
        return (self.x * PAIR + 1 - self.core, self.pos)

    def across(self):
        return ((1 - self.x) * PAIR + self.core, self.pos)

    def beside(self):
        return (self.rep, self.z * PAIR + 1 - self.y)

    def deeper(self, step):
        return lax.rem(self.z + step, self.deep)

    def along(self, step):
        return (self.rep, self.deeper(step) * PAIR + self.y)

    def member(self, step):
        return (lax.rem(self.rep + step, self.reps), self.pos)

    def peer(self, step):
        return (self.rep, lax.rem(self.pos + step, self.group))


def send(source, target, send_sem, recv_sem, device):
    return pltpu.make_async_remote_copy(
        src_ref=source,
        dst_ref=target,
        send_sem=send_sem,
        recv_sem=recv_sem,
        device_id=device,
        device_id_type=MESH,
    )


class Gather:
    def __init__(self, place, ref, half, skip, along_sems, hop_sems):
        self.p, self.ref, self.half, self.skip = place, ref, half, skip
        self.along_sems, self.hop_sems = along_sems, hop_sems

    def carried(self):
        p = self.p
        return pl.ds(
            aligned(p.core * self.half + p.x * self.skip, 128), self.half - self.skip
        )

    def own(self):
        return self.ref.at[self.p.z, self.p.y, :, self.carried()]

    def copies_z(self):
        p, out = self.p, []
        for step in range(1, p.deep):
            out.append(
                send(
                    self.own(),
                    self.own(),
                    self.along_sems.at[0, step - 1],
                    self.along_sems.at[1, step - 1],
                    p.along(step),
                )
            )
        return out

    def hop(self, index, part, device):
        return send(
            part, part, self.hop_sems.at[0, index], self.hop_sems.at[1, index], device
        )

    def copy_y(self):
        part = self.ref.at[:, self.p.y, :, self.carried()]
        return self.hop(0, part, self.p.beside())

    def copy_x(self):
        p = self.p
        start = p.core * self.half + p.x * (self.half - self.skip)
        part = self.ref.at[:, :, :, pl.ds(aligned(start, 128), self.skip)]
        return self.hop(1, part, p.across())

    def copy_core(self):
        p = self.p
        part = self.ref.at[:, :, :, pl.ds(aligned(p.core * self.half, 128), self.half)]
        return self.hop(2, part, p.sibling())

    def start_z(self):
        for copy in self.copies_z():
            copy.start()

    def start_y(self):
        for copy in self.copies_z():
            copy.wait_recv()
        self.copy_y().start()

    def start_x(self):
        self.copy_y().wait_recv()
        self.copy_x().start()

    def start_core(self):
        self.copy_x().wait_recv()
        self.copy_core().start()

    def arrive(self):
        self.copy_core().wait_recv()

    def finish(self):
        for copy in self.copies_z():
            copy.wait_send()
        self.copy_y().wait_send()
        self.copy_x().wait_send()
        self.copy_core().wait_send()


class Reduce:
    def __init__(self, place, ref, recv, first, second, third, res, sems, x_first):
        self.p, self.ref, self.recv, self.first = place, ref, recv, first
        self.second, self.third, self.res, self.sems = second, third, res, sems
        self.x_first = x_first
        self.rows, self.half = recv.shape[2], recv.shape[3]
        self.steps = 6 if x_first else 5

    def columns(self, core):
        return pl.ds(aligned(core * self.half, 128), self.half)

    def one(self, index, source, target, device):
        return send(source, target, self.sems.at[0, index], self.sems.at[1, index], device)

    def split(self, x):
        return pl.ds(aligned(x * (self.rows // 2), 16), self.rows // 2)

    def copies(self, phase):
        p = self.p
        if phase == 0:
            part = self.ref.at[:, :, :, self.columns(1 - p.core)]
            return [self.one(0, part, self.recv, p.sibling())]
        if self.x_first:
            if phase == 1:
                part = self.recv.at[:, :, self.split(1 - p.x), :]
                return [self.one(1, part, self.first, p.across())]
            if phase == 2:
                return [self.one(2, self.first.at[:, 1 - p.y], self.second, p.beside())]
            if phase == 3:
                return [
                    self.one(
                        2 + step,
                        self.second.at[p.deeper(step)],
                        self.third.at[step - 1],
                        p.along(step),
                    )
                    for step in range(1, p.deep)
                ]
            last = 2 + p.deep
            if phase == 4:
                part = self.res.at[self.split(p.x), self.columns(p.core)]
                return [self.one(last, part, part, p.across())]
            part = self.res.at[:, self.columns(p.core)]
            return [self.one(last + 1, part, part, p.sibling())]
        if phase == 1:
            return [self.one(1, self.recv.at[:, 1 - p.y], self.first, p.beside())]
        if phase == 2:
            return [
                self.one(
                    1 + step,
                    self.first.at[p.deeper(step)],
                    self.second.at[step - 1],
                    p.along(step),
                )
                for step in range(1, p.deep)
            ]
        last = 1 + p.deep
        if phase == 3:
            return [self.one(last, self.first.at[p.z], self.third, p.across())]
        part = self.res.at[:, self.columns(p.core)]
        return [self.one(last + 1, part, part, p.sibling())]

    def add(self, phase):
        p = self.p
        if phase == 0:

            def fold(index, _):
                a, b = index // PAIR, index % PAIR
                self.recv[a, b] = self.recv[a, b] + self.ref[a, b, :, self.columns(p.core)]
                return 0

            lax.fori_loop(0, p.deep * PAIR, fold, 0)
        elif self.x_first:
            if phase == 1:

                def fold(index, _):
                    a, b = index // PAIR, index % PAIR
                    self.first[a, b] = self.first[a, b] + self.recv[a, b, self.split(p.x), :]
                    return 0

                lax.fori_loop(0, p.deep * PAIR, fold, 0)
            elif phase == 2:

                def fold(index, _):
                    self.second[index] = self.second[index] + self.first[index, p.y]
                    return 0

                lax.fori_loop(0, p.deep, fold, 0)
            elif phase == 3:
                total = self.second[p.z].astype(F32)
                for step in range(1, p.deep):
                    total = total + self.third[step - 1].astype(F32)
                self.res[self.split(p.x), self.columns(p.core)] = total.astype(BF16)
        elif phase == 1:

            def fold(index, _):
                self.first[index] = self.first[index] + self.recv[index, p.y]
                return 0

            lax.fori_loop(0, p.deep, fold, 0)
        elif phase == 2:
            total = self.first[p.z].astype(F32)
            for step in range(1, p.deep):
                total = total + self.second[step - 1].astype(F32)
            self.first[p.z] = total.astype(BF16)
        elif phase == 3:
            self.res[:, self.columns(p.core)] = self.first[p.z] + self.third[...]

    def step(self, phase):
        if phase > 0:
            for copy in self.copies(phase - 1):
                copy.wait()
            self.add(phase - 1)
        if phase < self.steps:
            for copy in self.copies(phase):
                copy.start()


def layer(config, *refs):
    (reps, group, count, width, heads, hidden, tasks_held) = config
    (
        lengths_ref, tasks_ref, small_ref, patches_ref, cot_ref,
        wq_ref, wk_ref, wv_ref, wo_ref, wg_ref, wu_ref, wd_ref,
        out_ref, grad_ref, done_in, done_gate, done_up, done_down, done_small, spare,
        w_in, w_out, w_gate, w_up, w_down,
        normed, qkv, context, extra, mixed, tokens, second, hid, gate_g, up_g,
        acc_out, acc_in, key_extra, vectors, small_buf, small_grads, member_buf, peer_out, peer_buf,
        *rest,
    ) = refs
    p = Place(reps, group)
    deep = p.deep
    head_dim = width // heads
    scale = head_dim ** -0.5
    groups = width // 256
    quad = heads // groups
    rows = wo_ref.shape[0]
    down_rows = wd_ref.shape[0] // 2
    (
        local_sems, along_sems, hop_sems, small_sems, member_sems, peer_sems, red_sems, out_sems,
        *red_bufs,
    ) = rest

    specs = [(w_in.at[g], 384, 128) for g in range(groups)] + [(w_out.at[0], 384, 128)]
    for j in range(2):
        specs += [(w_gate.at[j], 512, 128), (w_up.at[j], 512, 256), (w_down.at[j], 384, 128)]
    chunks = [
        Gather(p, ref, half, skip, along_sems.at[i], hop_sems.at[i])
        for i, (ref, half, skip) in enumerate(specs)
    ]

    sem = 0
    fills = [[] for _ in chunks]
    for g in range(groups):
        for i in range(2):
            start = pl.ds(aligned(g * 256 + p.core * 128, 128), 128)
            target = w_in.at[g, p.z, p.y, :, pl.ds(aligned(p.core * 384 + (p.x + i) * 128, 128), 128)]
            pair = (wq_ref, wk_ref) if i == 0 else (wk_ref, wv_ref)
            fills[g].append(
                tuple(
                    pltpu.make_async_copy(w.at[:, start], target, local_sems.at[sem]) for w in pair
                )
            )
            sem += 1
    columns = pl.ds(aligned(p.core * 384 + p.x * 128, 128), 256)
    fills[groups].append(
        pltpu.make_async_copy(
            wo_ref.at[:, columns], w_out.at[0, p.z, p.y, :, columns], local_sems.at[sem]
        )
    )
    sem += 1
    for j in range(2):
        for i in range(3):
            seg = 4 * p.core + p.x + i
            fills[groups + 1 + 3 * j].append(
                pltpu.make_async_copy(
                    wg_ref.at[:, pl.ds(aligned(seg * 256 + j * 128, 128), 128)],
                    w_gate.at[j, p.z, p.y, :, pl.ds(aligned(seg * 128, 128), 128)],
                    local_sems.at[sem],
                )
            )
            sem += 1
        for i in range(2):
            seg = 4 * p.core + 2 * p.x + i
            fills[groups + 2 + 3 * j].append(
                pltpu.make_async_copy(
                    wu_ref.at[:, pl.ds(aligned(seg * 256 + j * 128, 128), 128)],
                    w_up.at[j, p.z, p.y, :, pl.ds(aligned(seg * 128, 128), 128)],
                    local_sems.at[sem],
                )
            )
            sem += 1
        fills[groups + 3 + 3 * j].append(
            pltpu.make_async_copy(
                wd_ref.at[pl.ds(j * down_rows, down_rows), columns],
                w_down.at[j, p.z, p.y, :, columns],
                local_sems.at[sem],
            )
        )
        sem += 1

    def fill_start(i):
        for copy in fills[i]:
            if isinstance(copy, tuple):
                for x in range(2):

                    @pl.when(p.x == x)
                    def _(copy=copy, x=x):
                        copy[x].start()
            else:
                copy.start()

    def fill_wait(i):
        for copy in fills[i]:
            (copy[0] if isinstance(copy, tuple) else copy).wait()

    reds = []
    grads = []
    for j in range(2):
        grads += [
            (w_gate.at[j], done_gate.at[j], j == 0),
            (w_up.at[j], done_up.at[j], j == 1),
            (w_down.at[j], done_down.at[j], j == 0),
        ]
    grads += [(w_out.at[0], done_in.at[groups], True)]
    grads += [(w_in.at[g], done_in.at[g], g % 2 == 1) for g in range(groups)]
    for i, (ref, _, x_first) in enumerate(grads):
        recv, first, sec, third, res = red_bufs[5 * i : 5 * i + 5]
        reds.append(Reduce(p, ref, recv, first, sec, third, res, red_sems.at[i], x_first))

    tokens_in = pltpu.make_async_copy(patches_ref, tokens, out_sems.at[0])
    tokens_in.start()
    for i in range(len(chunks)):
        fill_start(i)
    small_buf[p.pos] = small_ref[...]
    barrier = pltpu.get_barrier_semaphore()
    for step in range(1, reps):
        pl.semaphore_signal(barrier, inc=1, device_id=p.member(step), device_id_type=MESH)
    for step in range(1, group):
        pl.semaphore_signal(barrier, inc=1, device_id=p.peer(step), device_id_type=MESH)
    pl.semaphore_wait(barrier, reps + group - 2)
    small_copies = [
        send(
            small_buf.at[p.pos], small_buf.at[p.pos],
            small_sems.at[0, step - 1], small_sems.at[1, step - 1], p.peer(step),
        )
        for step in range(1, group)
    ]
    for copy in small_copies:
        copy.start()

    def go(*events):
        for kind, i in events:
            if kind == "Z":
                fill_wait(i)
                chunks[i].start_z()
            elif kind == "Y":
                chunks[i].start_y()
            elif kind == "X":
                chunks[i].start_x()
            elif kind == "C":
                chunks[i].start_core()
            elif kind == "D":
                chunks[i].arrive()
            elif kind == "F":
                chunks[i].finish()
            else:
                reds[i].step(kind)

    go(("Z", 0), ("Z", 1))

    for copy in small_copies:
        copy.wait_recv()
    shard = width // group
    wide_row = lax.broadcasted_iota(jnp.int32, (128, width), 0)
    wide_col = lax.broadcasted_iota(jnp.int32, (128, width), 1)
    total = None
    for f in range(group):
        place_f = jnp.logical_and(wide_col == wide_row + f * shard, wide_row < shard)
        part = dot(small_buf[f], place_f.astype(F32).astype(BF16), 1, 0)
        total = part if total is None else total + part
    vectors[...] = total
    task = tasks_ref[0]
    chosen = [(task == k).astype(F32) for k in range(tasks_held)]

    def task_row():
        row = vectors[2:3, :] * chosen[0]
        for k in range(1, tasks_held):
            row = row + vectors[2 + k : 3 + k, :] * chosen[k]
        return row

    position = lax.broadcasted_iota(jnp.int32, (16, count), 1)
    kind = lax.broadcasted_iota(jnp.int32, (16, count), 0)
    mask = jnp.where(position < lengths_ref[0], 0.0, FAR)
    key_extra[...] = jnp.where(
        kind < 3, 1.0, jnp.where(kind == 3, mask, 0.0)
    ).astype(BF16)

    tokens_in.wait()
    block = 256
    blocks = count // block

    def rows_of(i, size=block):
        return pl.ds(aligned(i * size, size), size)

    def norm_one(i, _):
        r = rows_of(i)
        resid = tokens[r, :].astype(F32) + task_row()
        inv = lax.rsqrt(jnp.mean(resid * resid, axis=-1, keepdims=True) + EPS)
        normed[r, :] = (resid * inv * vectors[0:1, :]).astype(BF16)
        return 0

    lax.fori_loop(0, blocks, norm_one, 0)

    go(*EVENTS["pre"])

    def project(g):
        for core in range(2):
            base = core * 384
            weight = w_in[g, :, :, :, base : base + 384].reshape(width, 384)
            got = dot(weight, normed[...], 0, 1)
            qkv[g, base : base + 128] = (got[:128] * scale).astype(BF16)
            qkv[g, base + 128 : base + 384] = got[128:].astype(BF16)

    tile = 256
    tiles = count // tile
    wide = count // 2
    sixteen = lax.broadcasted_iota(jnp.int32, (16, count), 0)

    def offsets(h):
        g, left = h // quad, h % quad
        return g, (left // 2) * 384 + (left % 2) * head_dim

    def forward_head(h):
        g, off = offsets(h)
        ask = jnp.concatenate(
            [
                qkv[g, pl.ds(aligned(off, 64), head_dim), :],
                (sixteen == 3).astype(F32).astype(BF16),
            ],
            0,
        )
        scores, top = [], None
        for j in range(tiles):
            cut = slice(j * tile, (j + 1) * tile)
            keys = jnp.concatenate(
                [qkv[g, pl.ds(aligned(off + 128, 64), head_dim), cut], key_extra[:, cut]], 0
            )
            s = dot(keys, ask, 0, 0)
            scores.append(s)
            here = jnp.max(s, axis=0, keepdims=True)
            top = here if top is None else jnp.maximum(top, here)
        acc = None
        for j in range(tiles):
            cut = slice(j * tile, (j + 1) * tile)
            expd = jnp.exp(scores[j] - top).astype(BF16)
            vals = jnp.concatenate(
                [
                    qkv[g, pl.ds(aligned(off + 256, 64), head_dim), cut],
                    jnp.ones((16, tile), BF16),
                ],
                0,
            )
            part = dot(vals, expd, 1, 0)
            acc = part if acc is None else acc + part
        total = acc[head_dim : head_dim + 1]
        exact = acc[:head_dim] * (1.0 / total)
        low = exact.astype(BF16)
        missing = (exact - low.astype(F32)).astype(BF16)
        r = pl.ds(aligned(h * head_dim, 64), head_dim)
        context[r, :] = low
        hid[r, :] = missing[:, :wide]
        gate_g[r, :] = missing[:, wide:]
        extra[h, 0:16] = splits(-(top + jnp.log(total)), 1.0)

    def splits(row, fourth):
        high = row.astype(BF16).astype(F32)
        mid = (row - high).astype(BF16).astype(F32)
        low = row - high - mid
        return jnp.where(
            sixteen == 0,
            high,
            jnp.where(
                sixteen == 1,
                mid,
                jnp.where(sixteen == 2, low, jnp.where(sixteen == 3, fourth, 0.0)),
            ),
        ).astype(BF16)

    def each_head(h, _):
        for at, events in EVENTS["forward"].items():

            @pl.when(h == at)
            def _(events=events):
                go(*events)

        @pl.when(h % quad == 0)
        def _():
            project(h // quad)

        forward_head(h)
        return 0

    lax.fori_loop(0, heads, each_head, 0)
    kept = [hid.at[pl.ds(0, width), :], gate_g.at[pl.ds(0, width), :]]
    first_out = 6 + len(grads)
    keep = [
        pltpu.make_async_copy(kept[i], spare.at[i], out_sems.at[first_out + i]) for i in range(2)
    ]
    fetch = [
        pltpu.make_async_copy(spare.at[i], kept[i], out_sems.at[first_out + 2 + i])
        for i in range(2)
    ]
    for copy in keep:
        copy.start()
    go(*EVENTS["attended"])

    big = 256

    def out_project(i, _):
        r = rows_of(i, big)
        m = tokens[r, :].astype(F32) + task_row()
        m = m + dot(context[:, r], w_out[0].reshape(width, width), 0, 0)
        mixed[r, :] = m
        inv = lax.rsqrt(jnp.mean(m * m, axis=-1, keepdims=True) + EPS)
        second[r, :] = (m * inv * vectors[1:2, :]).astype(BF16)
        return 0

    lax.fori_loop(0, count // big, out_project, 0)
    cot_in = pltpu.make_async_copy(cot_ref, tokens, out_sems.at[1])
    cot_in.start()
    go(*EVENTS["normed"])
    cot_in.wait()

    curve = 0.7978845608028654
    cube = 0.044715
    part = 512
    for copy in keep:
        copy.wait()

    def ff_tile(t, _):
        j, u = t // 2, t % 2
        cols = pl.ds(aligned(u * part, part), part)
        for at, events in EVENTS["tile"].items():

            @pl.when(t == at)
            def _(events=events):
                go(*events)

        half = pl.ds(u * (deep // 2), deep // 2)

        def block_of(i, _):
            r = rows_of(i, big)
            gate_w = w_gate[j, :, :, :, cols].reshape(width, part)
            up_w = w_up[j, :, :, :, cols].reshape(width, part)
            down_w = w_down[j, half].reshape(part, width)
            two = second[r, :]
            gate = dot(two, gate_w, 1, 0)
            up = dot(two, up_w, 1, 0)
            back = dot(tokens[r, :], down_w, 1, 1)
            square = gate * gate
            bend = jnp.tanh(curve * gate * (1.0 + cube * square))
            flat = 0.5 * (1.0 + bend)
            gelu = gate * flat
            slope = flat + 0.5 * gate * (1.0 - bend * bend) * (
                curve * (1.0 + 3.0 * cube * square)
            )
            h = (gelu * up).astype(BF16)
            g_grad = (back * up * slope).astype(BF16)
            u_grad = (back * gelu).astype(BF16)
            hid[r, :] = h
            gate_g[r, :] = g_grad
            up_g[r, :] = u_grad
            o = dot(h, down_w, 1, 0)
            n = dot(g_grad, gate_w, 1, 1) + dot(u_grad, up_w, 1, 1)

            @pl.when(t == 0)
            def _():
                acc_out[r, :] = o
                acc_in[r, :] = n

            @pl.when(t > 0)
            def _():
                acc_out[r, :] = acc_out[r, :] + o
                acc_in[r, :] = acc_in[r, :] + n

            return 0

        lax.fori_loop(0, count // big, block_of, 0)
        for at, events in EVENTS["tile_mid"].items():

            @pl.when(t == at)
            def _(events=events):
                go(*events)

        w_down[j, half] = (
            dot(hid[...], tokens[...], 0, 0).astype(BF16).reshape(deep // 2, 2, down_rows, width)
        )
        w_gate[j, :, :, :, cols] = (
            dot(second[...], gate_g[...], 0, 0).astype(BF16).reshape(deep, 2, rows, part)
        )
        w_up[j, :, :, :, cols] = (
            dot(second[...], up_g[...], 0, 0).astype(BF16).reshape(deep, 2, rows, part)
        )
        return 0

    lax.fori_loop(0, 4, ff_tile, 0)
    for copy in fetch:
        copy.start()
    go(*EVENTS["ff_done"])

    small_grads[...] = jnp.zeros_like(small_grads)

    def second_back(i, _):
        r = rows_of(i)
        m = mixed[r, :]
        second[r, :] = (m + acc_out[r, :]).astype(BF16)
        inv = lax.rsqrt(jnp.mean(m * m, axis=-1, keepdims=True) + EPS)
        unit = m * inv
        got = acc_in[r, :]
        scaled = got * vectors[1:2, :]
        grad = tokens[r, :].astype(F32) + inv * (
            scaled - unit * jnp.mean(scaled * unit, axis=-1, keepdims=True)
        )
        small_grads[1:2, :] = small_grads[1:2, :] + jnp.sum(got * unit, axis=0, keepdims=True)
        mixed[r, :] = grad
        tokens[r, :] = grad.astype(BF16)
        return 0

    lax.fori_loop(0, blocks, second_back, 0)
    result = pltpu.make_async_copy(second, out_ref, out_sems.at[2])
    result.start()
    go(*EVENTS["second_back"])

    out_w = w_out[0].reshape(width, width)
    acc_out[0:width, :] = dot(context[...], tokens[...], 1, 0)
    lowered = dot(out_w, tokens[...], 1, 1).astype(BF16)
    for copy in fetch:
        copy.wait()
    for h in range(heads):
        r = slice(h * head_dim, (h + 1) * head_dim)
        low = lowered[r]
        exact = context[r, :].astype(F32) + jnp.concatenate(
            [hid[r, :], gate_g[r, :]], 1
        ).astype(F32)
        delta = jnp.sum(low.astype(F32) * exact, axis=0, keepdims=True)
        extra[h, 16:32] = splits(-delta, 0.0)
        context[r, :] = low
    w_out[0] = acc_out[0:width, :].astype(BF16).reshape(deep, 2, rows, width)
    go(*EVENTS["context_back"])

    def backward_head(h):
        g, off = offsets(h)
        q_rows = pl.ds(aligned(off, 64), head_dim)
        k_rows = pl.ds(aligned(off + 128, 64), head_dim)
        v_rows = pl.ds(aligned(off + 256, 64), head_dim)
        query = qkv[g, q_rows, :]
        back = context[pl.ds(aligned(h * head_dim, 64), head_dim), :]
        ask = jnp.concatenate([query, extra[h, 0:16]], 0)
        back_ask = jnp.concatenate([back, extra[h, 16:32]], 0)
        query_grad = None
        for j in range(tiles):
            cut = slice(j * tile, (j + 1) * tile)
            keys = qkv[g, k_rows, cut]
            lift = key_extra[:, cut]
            probs = jnp.exp(dot(jnp.concatenate([keys, lift], 0), ask, 0, 0))
            gap = dot(jnp.concatenate([qkv[g, v_rows, cut], lift], 0), back_ask, 0, 0)
            score_grad = (probs * gap).astype(BF16)
            part = dot(keys, score_grad, 1, 0)
            query_grad = part if query_grad is None else query_grad + part
            qkv[g, k_rows, cut] = dot(query, score_grad, 1, 1).astype(BF16)
            qkv[g, v_rows, cut] = dot(back, probs.astype(BF16), 1, 1).astype(BF16)
        qkv[g, q_rows, :] = (query_grad * scale).astype(BF16)

    def first_back(g):
        def part_of(i, _):
            r = rows_of(i, big)
            weight = w_in[g].reshape(width, width)
            got = dot(qkv[g, :, r], weight, 0, 1)

            @pl.when(g == 0)
            def _():
                acc_in[r, :] = got

            @pl.when(g > 0)
            def _():
                acc_in[r, :] = acc_in[r, :] + got

            return 0

        lax.fori_loop(0, count // big, part_of, 0)

    def in_grad(g):
        w_in[g] = dot(normed[...], qkv[g], 0, 1).astype(BF16).reshape(deep, 2, rows, width)

    def each_back(h, _):
        backward_head(h)

        @pl.when(h % quad == quad - 1)
        def _():
            g = h // quad
            first_back(g)
            in_grad(g)

        for at, events in EVENTS["backward"].items():

            @pl.when(h == at)
            def _(events=events):
                go(*events)

        return 0

    lax.fori_loop(0, heads, each_back, 0)
    result.wait()
    again = pltpu.make_async_copy(patches_ref, second, out_sems.at[3])
    again.start()
    go(*EVENTS["attention_back"])
    again.wait()

    def first_norm_back(i, _):
        r = rows_of(i)
        resid = second[r, :].astype(F32) + task_row()
        inv = lax.rsqrt(jnp.mean(resid * resid, axis=-1, keepdims=True) + EPS)
        unit = resid * inv
        got = acc_in[r, :]
        scaled = got * vectors[0:1, :]
        grad = mixed[r, :] + inv * (
            scaled - unit * jnp.mean(scaled * unit, axis=-1, keepdims=True)
        )
        small_grads[0:1, :] = small_grads[0:1, :] + jnp.sum(got * unit, axis=0, keepdims=True)
        small_grads[7:8, :] = small_grads[7:8, :] + jnp.sum(grad, axis=0, keepdims=True)
        acc_out[r, :] = grad
        return 0

    lax.fori_loop(0, blocks, first_norm_back, 0)
    grad_out = pltpu.make_async_copy(acc_out, grad_ref, out_sems.at[4])
    grad_out.start()
    for k in range(tasks_held):
        small_grads[2 + k : 3 + k, :] = small_grads[7:8, :] * chosen[k]

    member_buf[p.rep] = small_grads[...]
    member_copies = [
        send(
            member_buf.at[p.rep], member_buf.at[p.rep],
            member_sems.at[0, step - 1], member_sems.at[1, step - 1], p.member(step),
        )
        for step in range(1, reps)
    ]
    for copy in member_copies:
        copy.start()
    go(*EVENTS["tail_one"])
    for copy in member_copies:
        copy.wait_recv()
    summed = member_buf[0]
    for i in range(1, reps):
        summed = summed + member_buf[i]
    peer_out[...] = jnp.zeros_like(peer_out)
    for f in range(group):
        peer_out[f, :, 0:shard] = summed[:, f * shard : (f + 1) * shard]
    peer_copies = []
    for step in range(1, group):
        target = lax.rem(p.pos + step, group)
        peer_copies.append(
            send(
                peer_out.at[target], peer_buf.at[p.pos],
                peer_sems.at[0, step - 1], peer_sems.at[1, step - 1], p.peer(step),
            )
        )
    for copy in peer_copies:
        copy.start()
    peer_buf[p.pos] = peer_out[p.pos]
    go(*EVENTS["tail_two"])
    for copy in peer_copies:
        copy.wait_recv()
    summed = peer_buf[0]
    for i in range(1, group):
        summed = summed + peer_buf[i]
    small_grads[:, 0:128] = summed
    ends = [
        pltpu.make_async_copy(small_grads.at[:, pl.ds(0, 128)], done_small, out_sems.at[5])
    ]
    ends[0].start()
    go(*EVENTS["tail_three"])
    for i, (_, done, _) in enumerate(grads):
        copy = pltpu.make_async_copy(reds[i].res, done, out_sems.at[6 + i])
        copy.start()
        ends.append(copy)
    for copy in small_copies + member_copies + peer_copies:
        copy.wait_send()
    for copy in ends:
        copy.wait()
    grad_out.wait()


def fits(reps, group, args):
    patches, w_query, w_gate, w_down = args[0], args[3], args[7], args[9]
    return (
        reps == 4
        and group == 8
        and patches.shape == (1, 1024, 768)
        and w_query.shape == (96, 768)
        and w_gate.shape == (96, 2048)
        and w_down.shape == (256, 768)
    )


def ending(config, *refs):
    groups, group, rows, held = config
    output, grad, done_in, done_gate, done_up, done_down, done_small = refs[:7]
    out, out_grad, query, key, value, proj, gate, up, down, one, two, table = refs[7:19]
    sems = refs[19]
    copies = [
        pltpu.make_async_copy(output, out.at[0], sems.at[0]),
        pltpu.make_async_copy(grad, out_grad.at[0], sems.at[1]),
    ]
    for copy in copies:
        copy.start()
    for g in range(groups):
        for core in range(2):
            for i, ref in enumerate((query, key, value)):
                start = core * 384 + i * 128
                to = g * 256 + core * 128
                ref[:, to : to + 128] = done_in[g, :, start : start + 128].astype(F32)
    proj[...] = done_in[groups].astype(F32)
    for done, ref in ((done_gate, gate), (done_up, up)):
        for j in range(2):
            for f in range(group):
                to = f * 256 + j * 128
                ref[:, to : to + 128] = done[j, :, f * 128 : (f + 1) * 128].astype(F32)
    half = done_down.shape[1]
    for j in range(2):
        down[j * half : (j + 1) * half, :] = done_down[j].astype(F32)
    one[...] = done_small[0, :rows]
    two[...] = done_small[1, :rows]
    table[...] = done_small[...].T[:rows, 2 : 2 + held]
    for copy in copies:
        copy.wait()


def fused(
    reps, group, patches, lengths, tasks, w_query, w_key, w_value, w_out, w_gate, w_up, w_down,
    gain_attn, gain_mlp, task_table, cotangent,
):
    count, width = patches.shape[1:]
    rows, hidden = w_gate.shape
    held = task_table.shape[1]
    deep = group // PAIR
    groups = width // 256
    down_rows = w_down.shape[0] // 2
    small = jnp.concatenate([gain_attn[None], gain_mlp[None], task_table.T], axis=0)
    small = jnp.pad(small, ((0, 16 - small.shape[0]), (0, 128 - rows)))

    def of(rows, columns, x_first):
        half = columns // 2
        if x_first:
            shapes = [
                (deep, 2, rows, half),
                (deep, 2, rows // 2, half),
                (deep, rows // 2, half),
                (deep - 1, rows // 2, half),
                (rows, columns),
            ]
        else:
            shapes = [
                (deep, 2, rows, half),
                (deep, rows, half),
                (deep - 1, rows, half),
                (rows, half),
                (rows, columns),
            ]
        return [pltpu.VMEM(shape, BF16) for shape in shapes]

    red_bufs = []
    for j in range(2):
        red_bufs += of(rows, hidden // 2, j == 0)
        red_bufs += of(rows, hidden // 2, j == 1)
        red_bufs += of(down_rows, width, j == 0)
    red_bufs += of(rows, width, True)
    for g in range(groups):
        red_bufs += of(rows, width, g % 2 == 1)
    chunks = groups + 1 + 6
    scratch = [
        pltpu.VMEM((groups, deep, 2, rows, width), BF16),
        pltpu.VMEM((1, deep, 2, rows, width), BF16),
        pltpu.VMEM((2, deep, 2, rows, hidden // 2), BF16),
        pltpu.VMEM((2, deep, 2, rows, hidden // 2), BF16),
        pltpu.VMEM((2, deep, 2, down_rows, width), BF16),
        pltpu.VMEM((count, width), BF16),
        pltpu.VMEM((groups, width, count), BF16),
        pltpu.VMEM((width, count), BF16),
        pltpu.VMEM((HEADS, 32, count), BF16),
        pltpu.VMEM((count, width), F32),
        pltpu.VMEM((count, width), BF16),
        pltpu.VMEM((count, width), BF16),
        pltpu.VMEM((count, 512), BF16),
        pltpu.VMEM((count, 512), BF16),
        pltpu.VMEM((count, 512), BF16),
        pltpu.VMEM((count, width), F32),
        pltpu.VMEM((count, width), F32),
        pltpu.VMEM((16, count), BF16),
        pltpu.VMEM((16, width), F32),
        pltpu.VMEM((group, 16, 128), BF16),
        pltpu.VMEM((8, width), F32),
        pltpu.VMEM((reps, 8, width), F32),
        pltpu.VMEM((group, 8, 128), F32),
        pltpu.VMEM((group, 8, 128), F32),
        pltpu.SemaphoreType.DMA((groups * 2 + 1 + 12,)),
        pltpu.SemaphoreType.DMA((chunks, 2, deep - 1)),
        pltpu.SemaphoreType.DMA((chunks, 2, 3)),
        pltpu.SemaphoreType.DMA((2, group - 1)),
        pltpu.SemaphoreType.DMA((2, reps - 1)),
        pltpu.SemaphoreType.DMA((2, group - 1)),
        pltpu.SemaphoreType.DMA((chunks, 2, deep + 4)),
        pltpu.SemaphoreType.DMA((10 + chunks,)),
        *red_bufs,
    ]
    shape = jax.ShapeDtypeStruct
    smem = pl.BlockSpec(memory_space=pltpu.SMEM)
    anywhere = pl.BlockSpec(memory_space=pl.ANY)
    config = (reps, group, count, width, HEADS, hidden, held)
    output, grad, done_in, done_gate, done_up, done_down, done_small, _ = pl.pallas_call(
        functools.partial(layer, config),
        out_shape=[
            shape((count, width), BF16),
            shape((count, width), F32),
            shape((groups + 1, rows, width), BF16),
            shape((2, rows, hidden // 2), BF16),
            shape((2, rows, hidden // 2), BF16),
            shape((2, down_rows, width), BF16),
            shape((8, 128), F32),
            shape((2, width, count // 2), BF16),
        ],
        in_specs=[smem, smem, pl.BlockSpec(memory_space=pltpu.VMEM)] + [anywhere] * 9,
        out_specs=[anywhere] * 8,
        scratch_shapes=scratch,
        compiler_params=pltpu.CompilerParams(
            collective_id=0, has_side_effects=True, vmem_limit_bytes=62 * 1024 * 1024
        ),
        name="layer",
    )(
        lengths, tasks, small, patches[0], cotangent[0],
        w_query, w_key, w_value, w_out, w_gate, w_up, w_down,
    )
    lane = pl.BlockSpec(memory_space=pltpu.VMEM)
    return pl.pallas_call(
        functools.partial(ending, (groups, group, rows, held)),
        out_shape=[
            shape((1, count, width), BF16),
            shape((1, count, width), F32),
            *[shape((rows, width), F32)] * 4,
            *[shape((rows, hidden), F32)] * 2,
            shape((2 * down_rows, width), F32),
            shape((rows,), F32),
            shape((rows,), F32),
            shape((rows, held), F32),
        ],
        in_specs=[anywhere] * 2 + [lane] * 5,
        out_specs=[anywhere] * 2 + [lane] * 10,
        scratch_shapes=[pltpu.SemaphoreType.DMA((2,))],
        compiler_params=pltpu.CompilerParams(vmem_limit_bytes=62 * 1024 * 1024),
        name="ending",
    )(output, grad, done_in, done_gate, done_up, done_down, done_small)


def solution(mesh):
    in_specs = (
        P(("rep", "fsdp"), None, None),
        P(("rep", "fsdp")),
        P(("rep", "fsdp")),
        P("fsdp", None),
        P("fsdp", None),
        P("fsdp", None),
        P("fsdp", None),
        P("fsdp", None),
        P("fsdp", None),
        P("fsdp", None),
        P("fsdp"),
        P("fsdp"),
        P("fsdp", None),
        P(("rep", "fsdp"), None, None),
    )
    out_specs = (
        P(("rep", "fsdp"), None, None),
        P(("rep", "fsdp"), None, None),
        P("fsdp", None),
        P("fsdp", None),
        P("fsdp", None),
        P("fsdp", None),
        P("fsdp", None),
        P("fsdp", None),
        P("fsdp", None),
        P("fsdp"),
        P("fsdp"),
        P("fsdp", None),
    )
    reps, group = mesh.shape["rep"], mesh.shape["fsdp"]

    def per_device(*args):
        if fits(reps, group, args):
            return fused(reps, group, *args)
        return plain(*args)

    return jax.shard_map(
        per_device, mesh=mesh, in_specs=in_specs, out_specs=out_specs, check_vma=False
    )
```

```python
import functools

import jax
import jax.numpy as jnp
from jax import lax
from jax.experimental import pallas as pl
from jax.experimental.pallas import tpu as pltpu
from jax.sharding import PartitionSpec as P

HEADS = 12
HEAD_DIM = 64


EPS = 1e-06
FAR = -1e30


def normalize(resid, gain):
    return resid * lax.rsqrt(jnp.mean(resid * resid, axis=-1, keepdims=True) + EPS) * gain


def gated(gate, up):
    return jax.nn.gelu(gate, approximate=True) * up


def matmul(left, right):
    return jnp.dot(left, right, preferred_element_type=jnp.float32)


def matmul_back(left, right):
    return lax.dot_general(
        left, right, (((1,), (1,)), ((), ())), preferred_element_type=jnp.float32
    )


def outer_sum(left, right):
    return lax.dot_general(
        left, right, (((0,), (0,)), ((), ())), preferred_element_type=jnp.float32
    )


def plain(
    patches,
    lengths,
    tasks,
    w_query,
    w_key,
    w_value,
    w_out,
    w_gate,
    w_up,
    w_down,
    gain_attn,
    gain_mlp,
    task_table,
    cotangent,
):
    gathered = (
        lax.all_gather(w_query, "fsdp", axis=0, tiled=True),
        lax.all_gather(w_key, "fsdp", axis=0, tiled=True),
        lax.all_gather(w_value, "fsdp", axis=0, tiled=True),
        lax.all_gather(w_out, "fsdp", axis=0, tiled=True),
        lax.all_gather(w_gate, "fsdp", axis=0, tiled=True),
        lax.all_gather(w_up, "fsdp", axis=0, tiled=True),
        lax.all_gather(w_down, "fsdp", axis=0, tiled=True),
        lax.all_gather(gain_attn, "fsdp", axis=0, tiled=True),
        lax.all_gather(gain_mlp, "fsdp", axis=0, tiled=True),
        lax.all_gather(task_table, "fsdp", axis=0, tiled=True),
    )
    query_w, key_w, value_w, out_w, gate_w, up_w, down_w, gain_one, gain_two, table = gathered
    source = patches[0].astype(jnp.float32)
    count, width = source.shape
    scale = HEAD_DIM ** (-0.5)
    span = min(512, count)
    blocks = count // span
    gain_one = gain_one.astype(jnp.float32)
    gain_two = gain_two.astype(jnp.float32)
    picked = (jnp.arange(table.shape[1]) == tasks[0]).astype(jnp.float32)
    resid = source + jnp.sum(table.astype(jnp.float32) * picked[None, :], axis=1)[None, :]
    normed = normalize(resid, gain_one).astype(jnp.bfloat16)
    query = matmul(normed, query_w).astype(jnp.bfloat16).reshape(count, HEADS, HEAD_DIM)
    keys = matmul(normed, key_w).astype(jnp.bfloat16).reshape(count, HEADS, HEAD_DIM)
    values = matmul(normed, value_w).astype(jnp.bfloat16).reshape(count, HEADS, HEAD_DIM)
    valid = (jnp.arange(count) < lengths[0])[None, None, :]

    def scores_of(rows):
        raw = jnp.einsum("qhd,khd->hqk", rows, keys, preferred_element_type=jnp.float32) * scale
        return jnp.where(valid, raw, FAR)

    contexts = []
    logsums = []
    for index in range(blocks):
        rows = query[index * span : (index + 1) * span]
        scores = scores_of(rows)
        top = jnp.max(scores, axis=-1, keepdims=True)
        expd = jnp.exp(scores - top)
        total = jnp.sum(expd, axis=-1, keepdims=True)
        probs = (expd / total).astype(jnp.bfloat16)
        block_out = jnp.einsum("hqk,khd->qhd", probs, values, preferred_element_type=jnp.float32)
        contexts.append(block_out.reshape(span, width).astype(jnp.bfloat16))
        logsums.append(top + jnp.log(total))
    context = jnp.concatenate(contexts, axis=0)
    mixed = resid + matmul(context, out_w)
    normed_two = normalize(mixed, gain_two).astype(jnp.bfloat16)
    gate = matmul(normed_two, gate_w)
    up = matmul(normed_two, up_w)
    hidden = gated(gate, up).astype(jnp.bfloat16)
    output = (mixed + matmul(hidden, down_w)).astype(jnp.bfloat16)[None]
    fetched = (
        lax.all_gather(w_query, "fsdp", axis=0, tiled=True),
        lax.all_gather(w_key, "fsdp", axis=0, tiled=True),
        lax.all_gather(w_value, "fsdp", axis=0, tiled=True),
        lax.all_gather(w_out, "fsdp", axis=0, tiled=True),
        lax.all_gather(w_gate, "fsdp", axis=0, tiled=True),
        lax.all_gather(w_up, "fsdp", axis=0, tiled=True),
        lax.all_gather(w_down, "fsdp", axis=0, tiled=True),
        lax.all_gather(gain_attn, "fsdp", axis=0, tiled=True),
        lax.all_gather(gain_mlp, "fsdp", axis=0, tiled=True),
        lax.all_gather(task_table, "fsdp", axis=0, tiled=True),
    )
    query_w, key_w, value_w, out_w, gate_w, up_w, down_w, gain_one, gain_two, table = fetched
    gain_one = gain_one.astype(jnp.float32)
    gain_two = gain_two.astype(jnp.float32)
    upstream = cotangent[0].astype(jnp.float32)
    branch_grad = upstream.astype(jnp.bfloat16)
    grad_down = outer_sum(hidden, branch_grad)
    hidden_grad = matmul_back(branch_grad, down_w)
    _, pull_gated = jax.vjp(gated, gate, up)
    gate_grad, up_grad = pull_gated(hidden_grad)
    gate_grad = gate_grad.astype(jnp.bfloat16)
    up_grad = up_grad.astype(jnp.bfloat16)
    grad_gate = outer_sum(normed_two, gate_grad)
    grad_up = outer_sum(normed_two, up_grad)
    second_grad = matmul_back(gate_grad, gate_w) + matmul_back(up_grad, up_w)
    _, pull_second = jax.vjp(normalize, mixed, gain_two)
    mixed_grad, grad_gain_two = pull_second(second_grad)
    mixed_grad = mixed_grad + upstream
    attn_grad = mixed_grad.astype(jnp.bfloat16)
    grad_out = outer_sum(context, attn_grad)
    context_grad = (
        matmul_back(attn_grad, out_w).astype(jnp.bfloat16).reshape(count, HEADS, HEAD_DIM)
    )
    key_grad = jnp.zeros((count, HEADS, HEAD_DIM), jnp.float32)
    value_grad = jnp.zeros((count, HEADS, HEAD_DIM), jnp.float32)
    query_parts = []
    for index in range(blocks):
        rows = query[index * span : (index + 1) * span]
        back_rows = context_grad[index * span : (index + 1) * span]
        probs = jnp.exp(scores_of(rows) - logsums[index])
        probs_low = probs.astype(jnp.bfloat16)
        prob_grad = jnp.einsum(
            "qhd,khd->hqk", back_rows, values, preferred_element_type=jnp.float32
        )
        weighted = jnp.sum(probs * prob_grad, axis=-1, keepdims=True)
        score_grad = (probs * (prob_grad - weighted)).astype(jnp.bfloat16)
        query_parts.append(
            jnp.einsum("hqk,khd->qhd", score_grad, keys, preferred_element_type=jnp.float32) * scale
        )
        key_grad = (
            key_grad
            + jnp.einsum("hqk,qhd->khd", score_grad, rows, preferred_element_type=jnp.float32)
            * scale
        )
        value_grad = value_grad + jnp.einsum(
            "hqk,qhd->khd", probs_low, back_rows, preferred_element_type=jnp.float32
        )
    query_grad = jnp.concatenate(query_parts, axis=0).reshape(count, width).astype(jnp.bfloat16)
    key_grad = key_grad.reshape(count, width).astype(jnp.bfloat16)
    value_grad = value_grad.reshape(count, width).astype(jnp.bfloat16)
    grad_query = outer_sum(normed, query_grad)
    grad_key = outer_sum(normed, key_grad)
    grad_value = outer_sum(normed, value_grad)
    first_grad = (
        matmul_back(query_grad, query_w)
        + matmul_back(key_grad, key_w)
        + matmul_back(value_grad, value_w)
    )
    _, pull_first = jax.vjp(normalize, resid, gain_one)
    resid_grad, grad_gain_one = pull_first(first_grad)
    resid_grad = resid_grad + mixed_grad
    grad_table = jnp.sum(resid_grad, axis=0)[:, None] * picked[None, :]
    shares = (
        lax.psum_scatter(grad_query, "fsdp", scatter_dimension=0, tiled=True),
        lax.psum_scatter(grad_key, "fsdp", scatter_dimension=0, tiled=True),
        lax.psum_scatter(grad_value, "fsdp", scatter_dimension=0, tiled=True),
        lax.psum_scatter(grad_out, "fsdp", scatter_dimension=0, tiled=True),
        lax.psum_scatter(grad_gate, "fsdp", scatter_dimension=0, tiled=True),
        lax.psum_scatter(grad_up, "fsdp", scatter_dimension=0, tiled=True),
        lax.psum_scatter(grad_down, "fsdp", scatter_dimension=0, tiled=True),
        lax.psum_scatter(grad_gain_one, "fsdp", scatter_dimension=0, tiled=True),
        lax.psum_scatter(grad_gain_two, "fsdp", scatter_dimension=0, tiled=True),
        lax.psum_scatter(grad_table, "fsdp", scatter_dimension=0, tiled=True),
    )
    (
        share_query,
        share_key,
        share_value,
        share_out,
        share_gate,
        share_up,
        share_down,
        share_one,
        share_two,
        share_table,
    ) = shares
    summed = (
        lax.psum(share_query.astype(jnp.bfloat16), "rep").astype(jnp.float32),
        lax.psum(share_key.astype(jnp.bfloat16), "rep").astype(jnp.float32),
        lax.psum(share_value.astype(jnp.bfloat16), "rep").astype(jnp.float32),
        lax.psum(share_out.astype(jnp.bfloat16), "rep").astype(jnp.float32),
        lax.psum(share_gate.astype(jnp.bfloat16), "rep").astype(jnp.float32),
        lax.psum(share_up.astype(jnp.bfloat16), "rep").astype(jnp.float32),
        lax.psum(share_down.astype(jnp.bfloat16), "rep").astype(jnp.float32),
        lax.psum(share_one.astype(jnp.bfloat16), "rep").astype(jnp.float32),
        lax.psum(share_two.astype(jnp.bfloat16), "rep").astype(jnp.float32),
        lax.psum(share_table.astype(jnp.bfloat16), "rep").astype(jnp.float32),
    )
    return (
        output,
        resid_grad[None],
        summed[0],
        summed[1],
        summed[2],
        summed[3],
        summed[4],
        summed[5],
        summed[6],
        summed[7],
        summed[8],
        summed[9],
    )


PARTS = [2, 1, 1, 1, 2, 2, 2, 2, 2, 2]

EVENTS = {
    "start": [("Z", 0), ("Z", 1), ("Z", 2)],
    "pre": [
        ("Y", 0), ("Y", 1), ("Z", 3), ("X", 0), ("X", 1), ("Z", 4), ("Y", 2), ("C", 0), ("D", 0),
        ("C", 1), ("Y", 3), ("Z", 5), ("D", 1),
    ],
    "forward": {
        1: [("X", 2), ("Z", 6)],
        2: [("Y", 4), ("Z", 7)],
        3: [("X", 3)],
        4: [("Z", 8), ("Y", 5), ("C", 2), ("Z", 9), ("Y", 6), ("X", 4), ("D", 2), ("Z", 10)],
        5: [("C", 3), ("X", 5), ("Y", 7), ("Z", 11), ("Y", 8)],
        7: [("C", 4), ("X", 6), ("Y", 9), ("Z", 12)],
        8: [("D", 3), ("X", 7)],
        9: [("C", 5), ("C", 6), ("X", 8), ("Y", 10), ("Z", 13)],
        10: [("X", 9), ("Y", 11), ("Z", 14)],
    },
    "attended": [
        ("D", 4), ("C", 7), ("Y", 12), ("Z", 15), ("X", 10), ("F", 0), ("F", 1), ("F", 2),
        ("F", 3),
    ],
    "normed": [("Y", 13), ("Z", 16)],
    "block": {
        0: [
            ("D", 5), ("D", 6), ("D", 7), ("C", 8), ("X", 11), ("C", 9), ("Y", 14), ("D", 8),
            ("X", 12), ("D", 9), ("C", 10), ("Y", 15), ("X", 13), ("C", 11), ("D", 10),
        ],
        1: [("Y", 16)],
        3: [("C", 12), ("X", 14)],
        4: [("X", 16)],
        6: [("C", 15)],
        8: [
            ("D", 11), ("D", 12), ("D", 13), ("D", 14), ("D", 15), ("D", 16), (0, 0), (0, 1),
            (0, 2),
        ],
        12: [(1, 2)],
    },
    "outer": {
        0: [("F", 5), ("F", 6), ("F", 7), ("F", 8), ("F", 9), ("F", 10), ("C", 13)],
        1: [("X", 15)],
        2: [("C", 14)],
        3: [("C", 16)],
        6: [("F", 11), ("F", 12), ("F", 13), ("F", 14), ("F", 15), ("F", 16), (1, 0)],
        8: [(1, 1)],
        10: [(2, 0)],
    },
    "ff_done": [(2, 1), (0, 3), (0, 4), (0, 5)],
    "second_back": [("F", 4)],
    "context_back": [(3, 0), (1, 3), (0, 6)],
    "backward": {
        0: [(2, 2), (1, 4)],
        1: [(3, 1), (1, 5), (1, 6), (0, 7)],
        2: [(4, 0), (3, 2), (2, 3), (1, 7)],
        3: [(4, 1), (0, 8)],
        4: [(5, 1), (4, 2), (2, 4), (1, 8)],
        5: [(3, 3), (2, 5), (0, 9)],
        6: [(2, 7), (1, 9)],
        7: [(5, 0), (5, 2), (3, 4), (2, 6), (2, 8), (0, 10)],
        8: [(6, 0), (6, 2), (4, 3), (3, 5), (1, 10)],
        9: [(5, 3), (4, 4), (3, 6), (3, 7), (2, 9), (0, 11)],
        10: [(6, 3), (5, 4), (4, 7), (3, 8), (2, 10), (1, 11)],
        11: [(4, 5), (4, 6), (5, 7), (4, 8), (0, 12)],
    },
    "attention_back": [],
    "last": {
        1: [(5, 8), (2, 11)],
        2: [(5, 5), (5, 6), (3, 9), (1, 12)],
        3: [(6, 5), (3, 10), (6, 6)],
    },
    "tail_one": [(4, 9), (3, 11)],
    "tail_two": [(5, 9), (4, 10), (2, 12)],
    "tail_three": [(4, 11), (5, 10), (5, 11), (3, 12), (4, 12), (5, 12)],
}


BF16 = jnp.bfloat16
F32 = jnp.float32
MESH = pl.DeviceIdType.MESH
PAIR = 2


def dot(left, right, on_left, on_right):
    return lax.dot_general(
        left, right, (((on_left,), (on_right,)), ((), ())), preferred_element_type=F32
    )


def aligned(index, step):
    return pl.multiple_of(index, step)


class Place:
    def __init__(self, reps, group):
        self.reps, self.group, self.deep = reps, group, group // PAIR
        self.rep = lax.axis_index("rep")
        self.pos = lax.axis_index("fsdp")
        self.x, self.core = self.rep // PAIR, self.rep % PAIR
        self.z, self.y = self.pos // PAIR, self.pos % PAIR

    def sibling(self):
        return (self.x * PAIR + 1 - self.core, self.pos)

    def across(self):
        return ((1 - self.x) * PAIR + self.core, self.pos)

    def beside(self):
        return (self.rep, self.z * PAIR + 1 - self.y)

    def deeper(self, step):
        return lax.rem(self.z + step, self.deep)

    def along(self, step):
        return (self.rep, self.deeper(step) * PAIR + self.y)

    def member(self, step):
        return (lax.rem(self.rep + step, self.reps), self.pos)

    def peer(self, step):
        return (self.rep, lax.rem(self.pos + step, self.group))


def send(source, target, send_sem, recv_sem, device):
    return pltpu.make_async_remote_copy(
        src_ref=source,
        dst_ref=target,
        send_sem=send_sem,
        recv_sem=recv_sem,
        device_id=device,
        device_id_type=MESH,
    )


class Gather:
    def __init__(self, place, ref, rows, half, skip, along_sems, hop_sems):
        self.p, self.ref, self.half, self.skip = place, ref, half, skip
        self.rows, self.along_sems, self.hop_sems = pl.ds(*rows), along_sems, hop_sems

    def carried(self):
        p = self.p
        return pl.ds(
            aligned(p.core * self.half + p.x * self.skip, 128), self.half - self.skip
        )

    def own(self):
        return self.ref.at[self.p.z, self.p.y, self.rows, self.carried()]

    def copies_z(self):
        p, out = self.p, []
        for step in range(1, p.deep):
            out.append(
                send(
                    self.own(),
                    self.own(),
                    self.along_sems.at[0, step - 1],
                    self.along_sems.at[1, step - 1],
                    p.along(step),
                )
            )
        return out

    def hop(self, index, part, device):
        return send(
            part, part, self.hop_sems.at[0, index], self.hop_sems.at[1, index], device
        )

    def copy_y(self):
        part = self.ref.at[:, self.p.y, self.rows, self.carried()]
        return self.hop(0, part, self.p.beside())

    def copy_x(self):
        p = self.p
        start = p.core * self.half + p.x * (self.half - self.skip)
        part = self.ref.at[:, :, self.rows, pl.ds(aligned(start, 128), self.skip)]
        return self.hop(1, part, p.across())

    def copy_core(self):
        p = self.p
        part = self.ref.at[:, :, self.rows, pl.ds(aligned(p.core * self.half, 128), self.half)]
        return self.hop(2, part, p.sibling())

    def start_z(self):
        for copy in self.copies_z():
            copy.start()

    def start_y(self):
        for copy in self.copies_z():
            copy.wait_recv()
        self.copy_y().start()

    def start_x(self):
        self.copy_y().wait_recv()
        self.copy_x().start()

    def start_core(self):
        self.copy_x().wait_recv()
        self.copy_core().start()

    def arrive(self):
        self.copy_core().wait_recv()

    def finish(self):
        for copy in self.copies_z():
            copy.wait_send()
        self.copy_y().wait_send()
        self.copy_x().wait_send()
        self.copy_core().wait_send()


class Reduce:
    def __init__(self, place, ref, recv, first, second, third, res, sems, x_first):
        self.p, self.ref, self.recv, self.first = place, ref, recv, first
        self.second, self.third, self.res, self.sems = second, third, res, sems
        self.x_first = x_first
        self.rows, self.half = recv.shape[2], recv.shape[3]
        self.by_rows = ref.shape[2] > self.rows
        self.steps = 6 if x_first else 5

    def share(self, core):
        if self.by_rows:
            return pl.ds(aligned(core * self.rows, 16), self.rows), slice(None)
        return slice(None), pl.ds(aligned(core * self.half, 128), self.half)

    def columns(self, core):
        return self.share(core)[1]

    def one(self, index, source, target, device):
        return send(source, target, self.sems.at[0, index], self.sems.at[1, index], device)

    def split(self, x):
        return pl.ds(aligned(x * (self.rows // 2), 16), self.rows // 2)

    def copies(self, phase):
        p = self.p
        if phase == 0:
            part = self.ref.at[(slice(None), slice(None), *self.share(1 - p.core))]
            return [self.one(0, part, self.recv, p.sibling())]
        if self.x_first:
            if phase == 1:
                part = self.recv.at[:, :, self.split(1 - p.x), :]
                return [self.one(1, part, self.first, p.across())]
            if phase == 2:
                return [self.one(2, self.first.at[:, 1 - p.y], self.second, p.beside())]
            if phase == 3:
                return [
                    self.one(
                        2 + step,
                        self.second.at[p.deeper(step)],
                        self.third.at[step - 1],
                        p.along(step),
                    )
                    for step in range(1, p.deep)
                ]
            last = 2 + p.deep
            if phase == 4:
                part = self.res.at[self.split(p.x), self.columns(p.core)]
                return [self.one(last, part, part, p.across())]
            part = self.res.at[self.share(p.core)]
            return [self.one(last + 1, part, part, p.sibling())]
        if phase == 1:
            return [self.one(1, self.recv.at[:, 1 - p.y], self.first, p.beside())]
        if phase == 2:
            return [
                self.one(
                    1 + step,
                    self.first.at[p.deeper(step)],
                    self.second.at[step - 1],
                    p.along(step),
                )
                for step in range(1, p.deep)
            ]
        last = 1 + p.deep
        if phase == 3:
            return [self.one(last, self.first.at[p.z], self.third, p.across())]
        part = self.res.at[self.share(p.core)]
        return [self.one(last + 1, part, part, p.sibling())]

    def add(self, phase):
        p = self.p
        if phase == 0:

            def fold(index, _):
                a, b = index // PAIR, index % PAIR
                self.recv[a, b] = self.recv[a, b] + self.ref[(a, b, *self.share(p.core))]
                return 0

            lax.fori_loop(0, p.deep * PAIR, fold, 0)
        elif self.x_first:
            if phase == 1:

                def fold(index, _):
                    a, b = index // PAIR, index % PAIR
                    self.first[a, b] = self.first[a, b] + self.recv[a, b, self.split(p.x), :]
                    return 0

                lax.fori_loop(0, p.deep * PAIR, fold, 0)
            elif phase == 2:

                def fold(index, _):
                    self.second[index] = self.second[index] + self.first[index, p.y]
                    return 0

                lax.fori_loop(0, p.deep, fold, 0)
            elif phase == 3:
                total = self.second[p.z].astype(F32)
                for step in range(1, p.deep):
                    total = total + self.third[step - 1].astype(F32)
                self.res[self.split(p.x), self.columns(p.core)] = total.astype(BF16)
        elif phase == 1:

            def fold(index, _):
                self.first[index] = self.first[index] + self.recv[index, p.y]
                return 0

            lax.fori_loop(0, p.deep, fold, 0)
        elif phase == 2:
            total = self.first[p.z].astype(F32)
            for step in range(1, p.deep):
                total = total + self.second[step - 1].astype(F32)
            self.first[p.z] = total.astype(BF16)
        elif phase == 3:
            self.res[self.share(p.core)] = self.first[p.z] + self.third[...]

    def step(self, phase):
        if phase > 0:
            for copy in self.copies(phase - 1):
                copy.wait()
            self.add(phase - 1)
        if phase < self.steps:
            for copy in self.copies(phase):
                copy.start()


def layer(config, *refs):
    (reps, group, count, width, heads, hidden, tasks_held) = config
    (
        lengths_ref, tasks_ref, small_ref, patches_ref, cot_ref,
        wq_ref, wk_ref, wv_ref, wo_ref, wg_ref, wu_ref, wd_ref,
        out_ref, grad_ref, done_in, done_gate, done_up, done_down, done_small, spare,
        w_in, w_out, w_ff, w_down,
        normed, qkv, context, extra, mixed, tokens, second, hid, gate_g, up_g,
        acc_out, acc_in, key_extra, vectors, small_buf, small_grads, member_buf, peer_out, peer_buf,
        *rest,
    ) = refs
    p = Place(reps, group)
    deep = p.deep
    head_dim = width // heads
    scale = head_dim ** -0.5
    groups = width // 256
    quad = heads // groups
    rows = wo_ref.shape[0]
    down_rows = wd_ref.shape[0] // 2
    (
        local_sems, along_sems, hop_sems, small_sems, member_sems, peer_sems, red_sems, out_sems,
        *red_bufs,
    ) = rest

    specs = []
    cuts = [0]

    def spec(ref, half, skip, parts):
        held_rows = ref.shape[2] // parts
        for i in range(parts):
            specs.append((ref, (i * held_rows, held_rows), half, skip))
        cuts.append(len(specs))

    for g in range(groups):
        spec(w_in.at[g], 384, 128, PARTS[g])
    spec(w_out.at[0], 384, 128, PARTS[groups])
    for j in range(2):
        spec(w_ff.at[j], 512, 128, PARTS[groups + 1 + 3 * j])
        spec(w_ff.at[2 + j], 512, 256 - 128 * j, PARTS[groups + 2 + 3 * j])
        spec(w_down.at[j], 384, 128, PARTS[groups + 3 + 3 * j])
    chunks = [
        Gather(p, ref, held_rows, half, skip, along_sems.at[i], hop_sems.at[i])
        for i, (ref, held_rows, half, skip) in enumerate(specs)
    ]

    sem = 0
    fills = [[] for _ in PARTS]
    for g in range(groups):
        for i in range(2):
            start = pl.ds(aligned(g * 256 + p.core * 128, 128), 128)
            target = w_in.at[g, p.z, p.y, :, pl.ds(aligned(p.core * 384 + (p.x + i) * 128, 128), 128)]
            pair = (wq_ref, wk_ref) if i == 0 else (wk_ref, wv_ref)
            fills[g].append(
                tuple(
                    pltpu.make_async_copy(w.at[:, start], target, local_sems.at[sem]) for w in pair
                )
            )
            sem += 1
    columns = pl.ds(aligned(p.core * 384 + p.x * 128, 128), 256)
    fills[groups].append(
        pltpu.make_async_copy(
            wo_ref.at[:, columns], w_out.at[0, p.z, p.y, :, columns], local_sems.at[sem]
        )
    )
    sem += 1
    for j in range(2):
        for i in range(3):
            seg = 4 * p.core + p.x + i
            fills[groups + 1 + 3 * j].append(
                pltpu.make_async_copy(
                    wg_ref.at[:, pl.ds(aligned(seg * 256 + j * 128, 128), 128)],
                    w_ff.at[j, p.z, p.y, :, pl.ds(aligned(seg * 128, 128), 128)],
                    local_sems.at[sem],
                )
            )
            sem += 1
        for i in range(2 + j):
            seg = 4 * p.core + (2 - j) * p.x + i
            fills[groups + 2 + 3 * j].append(
                pltpu.make_async_copy(
                    wu_ref.at[:, pl.ds(aligned(seg * 256 + j * 128, 128), 128)],
                    w_ff.at[2 + j, p.z, p.y, :, pl.ds(aligned(seg * 128, 128), 128)],
                    local_sems.at[sem],
                )
            )
            sem += 1
        fills[groups + 3 + 3 * j].append(
            pltpu.make_async_copy(
                wd_ref.at[pl.ds(j * down_rows, down_rows), columns],
                w_down.at[j, p.z, p.y, :, columns],
                local_sems.at[sem],
            )
        )
        sem += 1

    def fill_start(i):
        for copy in fills[i]:
            if isinstance(copy, tuple):
                for x in range(2):

                    @pl.when(p.x == x)
                    def _(copy=copy, x=x):
                        copy[x].start()
            else:
                copy.start()

    def fill_wait(i):
        for copy in fills[i]:
            (copy[0] if isinstance(copy, tuple) else copy).wait()

    reds = []
    grads = []
    for j in range(2):
        grads += [
            (w_ff.at[j], done_gate.at[j], True),
            (w_ff.at[2 + j], done_up.at[j], False),
            (w_down.at[j], done_down.at[j], True),
        ]
    grads += [(w_out.at[0], done_in.at[groups], True)]
    for pair in range(2 * groups):
        columns = pl.ds((pair % 2) * 384, 384)
        grads.append(
            (
                w_ff.at[pair // 2, :, :, :, columns],
                done_in.at[pair // 2, :, columns],
                False,
            )
        )
    for i, (ref, _, x_first) in enumerate(grads):
        recv, first, sec, third, res = red_bufs[5 * i : 5 * i + 5]
        reds.append(Reduce(p, ref, recv, first, sec, third, res, red_sems.at[i], x_first))

    tokens_in = pltpu.make_async_copy(patches_ref, tokens, out_sems.at[0])
    tokens_in.start()
    for i in range(len(fills)):
        fill_start(i)
    small_buf[p.pos] = small_ref[...]
    barrier = pltpu.get_barrier_semaphore()
    for step in range(1, reps):
        pl.semaphore_signal(barrier, inc=1, device_id=p.member(step), device_id_type=MESH)
    for step in range(1, group):
        pl.semaphore_signal(barrier, inc=1, device_id=p.peer(step), device_id_type=MESH)
    pl.semaphore_wait(barrier, reps + group - 2)
    small_copies = [
        send(
            small_buf.at[p.pos], small_buf.at[p.pos],
            small_sems.at[0, step - 1], small_sems.at[1, step - 1], p.peer(step),
        )
        for step in range(1, group)
    ]
    for copy in small_copies:
        copy.start()

    def go(*events):
        for kind, i in events:
            if kind == "Z":
                if i in cuts:
                    fill_wait(cuts.index(i))
                chunks[i].start_z()
            elif kind == "Y":
                chunks[i].start_y()
            elif kind == "X":
                chunks[i].start_x()
            elif kind == "C":
                chunks[i].start_core()
            elif kind == "D":
                chunks[i].arrive()
            elif kind == "F":
                chunks[i].finish()
            else:
                reds[i].step(kind)

    go(*EVENTS["start"])

    for copy in small_copies:
        copy.wait_recv()
    shard = width // group
    wide_row = lax.broadcasted_iota(jnp.int32, (128, width), 0)
    wide_col = lax.broadcasted_iota(jnp.int32, (128, width), 1)
    total = None
    for f in range(group):
        place_f = jnp.logical_and(wide_col == wide_row + f * shard, wide_row < shard)
        part = dot(small_buf[f], place_f.astype(F32).astype(BF16), 1, 0)
        total = part if total is None else total + part
    vectors[...] = total
    task = tasks_ref[0]
    chosen = [(task == k).astype(F32) for k in range(tasks_held)]

    def task_row():
        row = vectors[2:3, :] * chosen[0]
        for k in range(1, tasks_held):
            row = row + vectors[2 + k : 3 + k, :] * chosen[k]
        return row

    position = lax.broadcasted_iota(jnp.int32, (16, count), 1)
    kind = lax.broadcasted_iota(jnp.int32, (16, count), 0)
    mask = jnp.where(position < lengths_ref[0], 0.0, FAR)
    key_extra[...] = jnp.where(
        kind < 3, 1.0, jnp.where(kind == 3, mask, 0.0)
    ).astype(BF16)

    tokens_in.wait()
    block = 256
    blocks = count // block

    def rows_of(i, size=block):
        return pl.ds(aligned(i * size, size), size)

    def norm_one(i, _):
        r = rows_of(i)
        resid = tokens[r, :].astype(F32) + task_row()
        inv = lax.rsqrt(jnp.mean(resid * resid, axis=-1, keepdims=True) + EPS)
        normed[r, :] = (resid * inv * vectors[0:1, :]).astype(BF16)
        return 0

    lax.fori_loop(0, blocks, norm_one, 0)

    go(*EVENTS["pre"])

    def project(g):
        for core in range(2):
            base = core * 384
            weight = w_in[g, :, :, :, base : base + 384].reshape(width, 384)
            got = dot(weight, normed[...], 0, 1)
            qkv[g, base : base + 128] = (got[:128] * scale).astype(BF16)
            qkv[g, base + 128 : base + 384] = got[128:].astype(BF16)

    tile = 256
    tiles = count // tile
    wide = count // 2
    sixteen = lax.broadcasted_iota(jnp.int32, (16, count), 0)

    def offsets(h):
        g, left = h // quad, h % quad
        return g, (left // 2) * 384 + (left % 2) * head_dim

    def forward_head(h):
        g, off = offsets(h)
        ask = jnp.concatenate(
            [
                qkv[g, pl.ds(aligned(off, 64), head_dim), :],
                (sixteen == 3).astype(F32).astype(BF16),
            ],
            0,
        )
        scores, top = [], None
        for j in range(tiles):
            cut = slice(j * tile, (j + 1) * tile)
            keys = jnp.concatenate(
                [qkv[g, pl.ds(aligned(off + 128, 64), head_dim), cut], key_extra[:, cut]], 0
            )
            s = dot(keys, ask, 0, 0)
            scores.append(s)
            here = jnp.max(s, axis=0, keepdims=True)
            top = here if top is None else jnp.maximum(top, here)
        acc = None
        for j in range(tiles):
            cut = slice(j * tile, (j + 1) * tile)
            expd = jnp.exp(scores[j] - top).astype(BF16)
            vals = jnp.concatenate(
                [
                    qkv[g, pl.ds(aligned(off + 256, 64), head_dim), cut],
                    jnp.ones((16, tile), BF16),
                ],
                0,
            )
            part = dot(vals, expd, 1, 0)
            acc = part if acc is None else acc + part
        total = acc[head_dim : head_dim + 1]
        exact = acc[:head_dim] * (1.0 / total)
        low = exact.astype(BF16)
        missing = (exact - low.astype(F32)).astype(BF16)
        r = pl.ds(aligned(h * head_dim, 64), head_dim)
        context[r, :] = low
        hid[r, :] = missing[:, :wide]
        gate_g[r, :] = missing[:, wide:]
        extra[h, 0:16] = splits(-(top + jnp.log(total)), 1.0)

    def splits(row, fourth):
        high = row.astype(BF16).astype(F32)
        mid = (row - high).astype(BF16).astype(F32)
        low = row - high - mid
        return jnp.where(
            sixteen == 0,
            high,
            jnp.where(
                sixteen == 1,
                mid,
                jnp.where(sixteen == 2, low, jnp.where(sixteen == 3, fourth, 0.0)),
            ),
        ).astype(BF16)

    def each_head(h, _):
        for at, events in EVENTS["forward"].items():

            @pl.when(h == at)
            def _(events=events):
                go(*events)

        @pl.when(h % quad == 0)
        def _():
            project(h // quad)

        forward_head(h)
        return 0

    lax.fori_loop(0, heads, each_head, 0)
    kept = [hid.at[pl.ds(0, width), :], gate_g.at[pl.ds(0, width), :]]
    first_out = 6 + len(grads)
    keep = [
        pltpu.make_async_copy(kept[i], spare.at[i], out_sems.at[first_out + i]) for i in range(2)
    ]
    fetch = [
        pltpu.make_async_copy(spare.at[i], kept[i], out_sems.at[first_out + 2 + i])
        for i in range(2)
    ]
    for copy in keep:
        copy.start()
    go(*EVENTS["attended"])

    big = 256

    def out_project(i, _):
        r = rows_of(i, big)
        m = tokens[r, :].astype(F32) + task_row()
        m = m + dot(context[:, r], w_out[0].reshape(width, width), 0, 0)
        mixed[r, :] = m
        inv = lax.rsqrt(jnp.mean(m * m, axis=-1, keepdims=True) + EPS)
        second[r, :] = (m * inv * vectors[1:2, :]).astype(BF16)
        return 0

    lax.fori_loop(0, count // big, out_project, 0)
    cot_in = pltpu.make_async_copy(cot_ref, tokens, out_sems.at[1])
    cot_in.start()
    go(*EVENTS["normed"])
    cot_in.wait()

    curve = 0.7978845608028654
    cube = 0.044715
    part = 512
    for copy in keep:
        copy.wait()

    def ff_tile(t, _):
        j, u = t // 2, t % 2
        cols = pl.ds(aligned(u * part, part), part)
        half = pl.ds(u * (deep // 2), deep // 2)

        def block_of(i, _):
            for at, events in EVENTS["block"].items():

                @pl.when(t * (count // big) + i == at)
                def _(events=events):
                    go(*events)

            r = rows_of(i, big)
            gate_w = w_ff[j, :, :, :, cols].reshape(width, part)
            up_w = w_ff[2 + j, :, :, :, cols].reshape(width, part)
            down_w = w_down[j, half].reshape(part, width)
            two = second[r, :]
            gate = dot(two, gate_w, 1, 0)
            up = dot(two, up_w, 1, 0)
            back = dot(tokens[r, :], down_w, 1, 1)
            square = gate * gate
            bend = jnp.tanh(curve * gate * (1.0 + cube * square))
            flat = 0.5 * (1.0 + bend)
            gelu = gate * flat
            slope = flat + 0.5 * gate * (1.0 - bend * bend) * (
                curve * (1.0 + 3.0 * cube * square)
            )
            h = (gelu * up).astype(BF16)
            g_grad = (back * up * slope).astype(BF16)
            u_grad = (back * gelu).astype(BF16)
            hid[r, :] = h
            gate_g[r, :] = g_grad
            up_g[r, :] = u_grad
            o = dot(h, down_w, 1, 0)
            n = dot(g_grad, gate_w, 1, 1) + dot(u_grad, up_w, 1, 1)

            @pl.when(t == 0)
            def _():
                acc_out[r, :] = o
                acc_in[r, :] = n

            @pl.when(t > 0)
            def _():
                acc_out[r, :] = acc_out[r, :] + o
                acc_in[r, :] = acc_in[r, :] + n

            return 0

        lax.fori_loop(0, count // big, block_of, 0)
        def pause(k):
            for at, events in EVENTS["outer"].items():

                @pl.when(t * 3 + k == at)
                def _(events=events):
                    go(*events)

        pause(0)
        w_down[j, half] = (
            dot(hid[...], tokens[...], 0, 0).astype(BF16).reshape(deep // 2, 2, down_rows, width)
        )
        pause(1)
        w_ff[j, :, :, :, cols] = (
            dot(second[...], gate_g[...], 0, 0).astype(BF16).reshape(deep, 2, rows, part)
        )
        pause(2)
        w_ff[2 + j, :, :, :, cols] = (
            dot(second[...], up_g[...], 0, 0).astype(BF16).reshape(deep, 2, rows, part)
        )
        return 0

    lax.fori_loop(0, 4, ff_tile, 0)
    for copy in fetch:
        copy.start()
    go(*EVENTS["ff_done"])

    small_grads[...] = jnp.zeros_like(small_grads)

    def second_back(i, _):
        r = rows_of(i)
        m = mixed[r, :]
        second[r, :] = (m + acc_out[r, :]).astype(BF16)
        inv = lax.rsqrt(jnp.mean(m * m, axis=-1, keepdims=True) + EPS)
        unit = m * inv
        got = acc_in[r, :]
        scaled = got * vectors[1:2, :]
        grad = tokens[r, :].astype(F32) + inv * (
            scaled - unit * jnp.mean(scaled * unit, axis=-1, keepdims=True)
        )
        small_grads[1:2, :] = small_grads[1:2, :] + jnp.sum(got * unit, axis=0, keepdims=True)
        mixed[r, :] = grad
        tokens[r, :] = grad.astype(BF16)
        return 0

    lax.fori_loop(0, blocks, second_back, 0)
    result = pltpu.make_async_copy(second, out_ref, out_sems.at[2])
    result.start()
    go(*EVENTS["second_back"])

    out_w = w_out[0].reshape(width, width)
    acc_out[0:width, :] = dot(context[...], tokens[...], 1, 0)
    lowered = dot(out_w, tokens[...], 1, 1).astype(BF16)
    for copy in fetch:
        copy.wait()
    for h in range(heads):
        r = slice(h * head_dim, (h + 1) * head_dim)
        low = lowered[r]
        exact = context[r, :].astype(F32) + jnp.concatenate(
            [hid[r, :], gate_g[r, :]], 1
        ).astype(F32)
        delta = jnp.sum(low.astype(F32) * exact, axis=0, keepdims=True)
        extra[h, 16:32] = splits(-delta, 0.0)
        context[r, :] = low
    w_out[0] = acc_out[0:width, :].astype(BF16).reshape(deep, 2, rows, width)
    go(*EVENTS["context_back"])

    def backward_head(h):
        g, off = offsets(h)
        q_rows = pl.ds(aligned(off, 64), head_dim)
        k_rows = pl.ds(aligned(off + 128, 64), head_dim)
        v_rows = pl.ds(aligned(off + 256, 64), head_dim)
        query = qkv[g, q_rows, :]
        back = context[pl.ds(aligned(h * head_dim, 64), head_dim), :]
        ask = jnp.concatenate([query, extra[h, 0:16]], 0)
        back_ask = jnp.concatenate([back, extra[h, 16:32]], 0)
        query_grad = None
        for j in range(tiles):
            cut = slice(j * tile, (j + 1) * tile)
            keys = qkv[g, k_rows, cut]
            lift = key_extra[:, cut]
            probs = jnp.exp(dot(jnp.concatenate([keys, lift], 0), ask, 0, 0))
            gap = dot(jnp.concatenate([qkv[g, v_rows, cut], lift], 0), back_ask, 0, 0)
            score_grad = (probs * gap).astype(BF16)
            part = dot(keys, score_grad, 1, 0)
            query_grad = part if query_grad is None else query_grad + part
            qkv[g, k_rows, cut] = dot(query, score_grad, 1, 1).astype(BF16)
            qkv[g, v_rows, cut] = dot(back, probs.astype(BF16), 1, 1).astype(BF16)
        qkv[g, q_rows, :] = (query_grad * scale).astype(BF16)

    def in_grad(pair):
        weight = dot(
            normed[...], qkv[pair // 2, pl.ds(aligned((pair % 2) * 384, 128), 384), :], 0, 1
        )
        w_ff[pair // 2, :, :, :, pl.ds(aligned((pair % 2) * 384, 128), 384)] = weight.astype(
            BF16
        ).reshape(deep, 2, rows, 384)

    def each_back(h, _):
        backward_head(h)

        @pl.when(h % 2 == 1)
        def _():
            in_grad(h // 2)

        for at, events in EVENTS["backward"].items():

            @pl.when(h == at)
            def _(events=events):
                go(*events)

        return 0

    lax.fori_loop(0, heads, each_back, 0)
    result.wait()
    again = pltpu.make_async_copy(patches_ref, second, out_sems.at[3])
    again.start()
    go(*EVENTS["attention_back"])
    again.wait()

    def first_norm_back(i, _):
        for at, events in EVENTS["last"].items():

            @pl.when(i == at)
            def _(events=events):
                go(*events)

        r = rows_of(i)
        got = dot(qkv[0, :, r], w_in[0].reshape(width, width), 0, 1)
        for g in range(1, groups):
            got = got + dot(qkv[g, :, r], w_in[g].reshape(width, width), 0, 1)
        resid = second[r, :].astype(F32) + task_row()
        inv = lax.rsqrt(jnp.mean(resid * resid, axis=-1, keepdims=True) + EPS)
        unit = resid * inv
        scaled = got * vectors[0:1, :]
        grad = mixed[r, :] + inv * (
            scaled - unit * jnp.mean(scaled * unit, axis=-1, keepdims=True)
        )
        small_grads[0:1, :] = small_grads[0:1, :] + jnp.sum(got * unit, axis=0, keepdims=True)
        small_grads[7:8, :] = small_grads[7:8, :] + jnp.sum(grad, axis=0, keepdims=True)
        acc_out[r, :] = grad
        return 0

    lax.fori_loop(0, blocks, first_norm_back, 0)
    grad_out = pltpu.make_async_copy(acc_out, grad_ref, out_sems.at[4])
    grad_out.start()
    for k in range(tasks_held):
        small_grads[2 + k : 3 + k, :] = small_grads[7:8, :] * chosen[k]

    member_buf[p.rep] = small_grads[...]
    member_copies = [
        send(
            member_buf.at[p.rep], member_buf.at[p.rep],
            member_sems.at[0, step - 1], member_sems.at[1, step - 1], p.member(step),
        )
        for step in range(1, reps)
    ]
    for copy in member_copies:
        copy.start()
    go(*EVENTS["tail_one"])
    for copy in member_copies:
        copy.wait_recv()
    summed = member_buf[0]
    for i in range(1, reps):
        summed = summed + member_buf[i]
    peer_out[...] = jnp.zeros_like(peer_out)
    for f in range(group):
        peer_out[f, :, 0:shard] = summed[:, f * shard : (f + 1) * shard]
    peer_copies = []
    for step in range(1, group):
        target = lax.rem(p.pos + step, group)
        peer_copies.append(
            send(
                peer_out.at[target], peer_buf.at[p.pos],
                peer_sems.at[0, step - 1], peer_sems.at[1, step - 1], p.peer(step),
            )
        )
    for copy in peer_copies:
        copy.start()
    peer_buf[p.pos] = peer_out[p.pos]
    go(*EVENTS["tail_two"])
    for copy in peer_copies:
        copy.wait_recv()
    summed = peer_buf[0]
    for i in range(1, group):
        summed = summed + peer_buf[i]
    small_grads[:, 0:128] = summed
    ends = [
        pltpu.make_async_copy(small_grads.at[:, pl.ds(0, 128)], done_small, out_sems.at[5])
    ]
    ends[0].start()
    go(*EVENTS["tail_three"])
    for i, (_, done, _) in enumerate(grads):
        copy = pltpu.make_async_copy(reds[i].res, done, out_sems.at[6 + i])
        copy.start()
        ends.append(copy)
    for copy in small_copies + member_copies + peer_copies:
        copy.wait_send()
    for copy in ends:
        copy.wait()
    grad_out.wait()


def fits(reps, group, args):
    patches, w_query, w_gate, w_down = args[0], args[3], args[7], args[9]
    return (
        reps == 4
        and group == 8
        and patches.shape == (1, 1024, 768)
        and w_query.shape == (96, 768)
        and w_gate.shape == (96, 2048)
        and w_down.shape == (256, 768)
    )


def ending(config, *refs):
    groups, group, rows, held = config
    output, grad, done_in, done_gate, done_up, done_down, done_small = refs[:7]
    out, out_grad, query, key, value, proj, gate, up, down, one, two, table = refs[7:19]
    sems = refs[19]
    held_out, held_grad = refs[20:22]
    parts = 4
    span = output.shape[0] // parts
    brought, copies = [], []
    for i in range(parts):
        r = pl.ds(i * span, span)
        for k, (source, middle, target) in enumerate(
            ((output, held_out, out.at[0]), (grad, held_grad, out_grad.at[0]))
        ):
            brought.append(
                pltpu.make_async_copy(source.at[r], middle.at[r], sems.at[0, k, i])
            )
            copies.append(
                pltpu.make_async_copy(middle.at[r], target.at[r], sems.at[1, k, i])
            )
    for copy in brought:
        copy.start()
    for first, then in zip(brought, copies):
        first.wait()
        then.start()
    for g in range(groups):
        for core in range(2):
            for i, ref in enumerate((query, key, value)):
                start = core * 384 + i * 128
                to = g * 256 + core * 128
                ref[:, to : to + 128] = done_in[g, :, start : start + 128].astype(F32)
    proj[...] = done_in[groups].astype(F32)
    for done, ref in ((done_gate, gate), (done_up, up)):
        for j in range(2):
            for f in range(group):
                to = f * 256 + j * 128
                ref[:, to : to + 128] = done[j, :, f * 128 : (f + 1) * 128].astype(F32)
    half = done_down.shape[1]
    for j in range(2):
        down[j * half : (j + 1) * half, :] = done_down[j].astype(F32)
    one[...] = done_small[0, :rows]
    two[...] = done_small[1, :rows]
    table[...] = done_small[...].T[:rows, 2 : 2 + held]
    for copy in copies:
        copy.wait()


def fused(
    reps, group, patches, lengths, tasks, w_query, w_key, w_value, w_out, w_gate, w_up, w_down,
    gain_attn, gain_mlp, task_table, cotangent,
):
    count, width = patches.shape[1:]
    rows, hidden = w_gate.shape
    held = task_table.shape[1]
    deep = group // PAIR
    groups = width // 256
    down_rows = w_down.shape[0] // 2
    small = jnp.concatenate([gain_attn[None], gain_mlp[None], task_table.T], axis=0)
    small = jnp.pad(small, ((0, 16 - small.shape[0]), (0, 128 - rows)))

    def of(rows, columns, x_first, by_rows=False):
        whole = (rows, columns)
        half = columns // 2
        if by_rows:
            rows, half = rows // 2, columns
        if x_first:
            shapes = [
                (deep, 2, rows, half),
                (deep, 2, rows // 2, half),
                (deep, rows // 2, half),
                (deep - 1, rows // 2, half),
                whole,
            ]
        else:
            shapes = [
                (deep, 2, rows, half),
                (deep, rows, half),
                (deep - 1, rows, half),
                (rows, half),
                whole,
            ]
        return [pltpu.VMEM(shape, BF16) for shape in shapes]

    red_bufs = []
    for j in range(2):
        red_bufs += of(rows, hidden // 2, True)
        red_bufs += of(rows, hidden // 2, False)
        red_bufs += of(down_rows, width, True)
    red_bufs += of(rows, width, True)
    for _ in range(2 * groups):
        red_bufs += of(rows, width // 2, False, True)
    sums = 7 + 2 * groups
    chunks = sum(PARTS)
    scratch = [
        pltpu.VMEM((groups, deep, 2, rows, width), BF16),
        pltpu.VMEM((1, deep, 2, rows, width), BF16),
        pltpu.VMEM((4, deep, 2, rows, hidden // 2), BF16),
        pltpu.VMEM((2, deep, 2, down_rows, width), BF16),
        pltpu.VMEM((count, width), BF16),
        pltpu.VMEM((groups, width, count), BF16),
        pltpu.VMEM((width, count), BF16),
        pltpu.VMEM((HEADS, 32, count), BF16),
        pltpu.VMEM((count, width), F32),
        pltpu.VMEM((count, width), BF16),
        pltpu.VMEM((count, width), BF16),
        pltpu.VMEM((count, 512), BF16),
        pltpu.VMEM((count, 512), BF16),
        pltpu.VMEM((count, 512), BF16),
        pltpu.VMEM((count, width), F32),
        pltpu.VMEM((count, width), F32),
        pltpu.VMEM((16, count), BF16),
        pltpu.VMEM((16, width), F32),
        pltpu.VMEM((group, 16, 128), BF16),
        pltpu.VMEM((8, width), F32),
        pltpu.VMEM((reps, 8, width), F32),
        pltpu.VMEM((group, 8, 128), F32),
        pltpu.VMEM((group, 8, 128), F32),
        pltpu.SemaphoreType.DMA((groups * 2 + 1 + 13,)),
        pltpu.SemaphoreType.DMA((chunks, 2, deep - 1)),
        pltpu.SemaphoreType.DMA((chunks, 2, 3)),
        pltpu.SemaphoreType.DMA((2, group - 1)),
        pltpu.SemaphoreType.DMA((2, reps - 1)),
        pltpu.SemaphoreType.DMA((2, group - 1)),
        pltpu.SemaphoreType.DMA((sums, 2, deep + 4)),
        pltpu.SemaphoreType.DMA((10 + sums,)),
        *red_bufs,
    ]
    shape = jax.ShapeDtypeStruct
    smem = pl.BlockSpec(memory_space=pltpu.SMEM)
    anywhere = pl.BlockSpec(memory_space=pl.ANY)
    config = (reps, group, count, width, HEADS, hidden, held)
    output, grad, done_in, done_gate, done_up, done_down, done_small, _ = pl.pallas_call(
        functools.partial(layer, config),
        out_shape=[
            shape((count, width), BF16),
            shape((count, width), F32),
            shape((groups + 1, rows, width), BF16),
            shape((2, rows, hidden // 2), BF16),
            shape((2, rows, hidden // 2), BF16),
            shape((2, down_rows, width), BF16),
            shape((8, 128), F32),
            shape((2, width, count // 2), BF16),
        ],
        in_specs=[smem, smem, pl.BlockSpec(memory_space=pltpu.VMEM)] + [anywhere] * 9,
        out_specs=[anywhere] * 8,
        scratch_shapes=scratch,
        compiler_params=pltpu.CompilerParams(
            collective_id=0, has_side_effects=True, vmem_limit_bytes=62 * 1024 * 1024
        ),
        name="layer",
    )(
        lengths, tasks, small, patches[0], cotangent[0],
        w_query, w_key, w_value, w_out, w_gate, w_up, w_down,
    )
    lane = pl.BlockSpec(memory_space=pltpu.VMEM)
    return pl.pallas_call(
        functools.partial(ending, (groups, group, rows, held)),
        out_shape=[
            shape((1, count, width), BF16),
            shape((1, count, width), F32),
            *[shape((rows, width), F32)] * 4,
            *[shape((rows, hidden), F32)] * 2,
            shape((2 * down_rows, width), F32),
            shape((rows,), F32),
            shape((rows,), F32),
            shape((rows, held), F32),
        ],
        in_specs=[anywhere] * 2 + [lane] * 5,
        out_specs=[anywhere] * 2 + [lane] * 10,
        scratch_shapes=[
            pltpu.SemaphoreType.DMA((2, 2, 4)),
            pltpu.VMEM((count, width), BF16),
            pltpu.VMEM((count, width), F32),
        ],
        compiler_params=pltpu.CompilerParams(vmem_limit_bytes=62 * 1024 * 1024),
        name="ending",
    )(output, grad, done_in, done_gate, done_up, done_down, done_small)


def solution(mesh):
    in_specs = (
        P(("rep", "fsdp"), None, None),
        P(("rep", "fsdp")),
        P(("rep", "fsdp")),
        P("fsdp", None),
        P("fsdp", None),
        P("fsdp", None),
        P("fsdp", None),
        P("fsdp", None),
        P("fsdp", None),
        P("fsdp", None),
        P("fsdp"),
        P("fsdp"),
        P("fsdp", None),
        P(("rep", "fsdp"), None, None),
    )
    out_specs = (
        P(("rep", "fsdp"), None, None),
        P(("rep", "fsdp"), None, None),
        P("fsdp", None),
        P("fsdp", None),
        P("fsdp", None),
        P("fsdp", None),
        P("fsdp", None),
        P("fsdp", None),
        P("fsdp", None),
        P("fsdp"),
        P("fsdp"),
        P("fsdp", None),
    )
    reps, group = mesh.shape["rep"], mesh.shape["fsdp"]

    def per_device(*args):
        if fits(reps, group, args):
            return fused(reps, group, *args)
        return plain(*args)

    return jax.shard_map(
        per_device, mesh=mesh, in_specs=in_specs, out_specs=out_specs, check_vma=False
    )
```

```python
import functools

import jax
import jax.numpy as jnp
from jax import lax
from jax.experimental import pallas as pl
from jax.experimental.pallas import tpu as pltpu
from jax.sharding import PartitionSpec as P

HEADS = 12
HEAD_DIM = 64


EPS = 1e-06
FAR = -1e30


def normalize(resid, gain):
    return resid * lax.rsqrt(jnp.mean(resid * resid, axis=-1, keepdims=True) + EPS) * gain


def gated(gate, up):
    return jax.nn.gelu(gate, approximate=True) * up


def matmul(left, right):
    return jnp.dot(left, right, preferred_element_type=jnp.float32)


def matmul_back(left, right):
    return lax.dot_general(
        left, right, (((1,), (1,)), ((), ())), preferred_element_type=jnp.float32
    )


def outer_sum(left, right):
    return lax.dot_general(
        left, right, (((0,), (0,)), ((), ())), preferred_element_type=jnp.float32
    )


def plain(
    patches,
    lengths,
    tasks,
    w_query,
    w_key,
    w_value,
    w_out,
    w_gate,
    w_up,
    w_down,
    gain_attn,
    gain_mlp,
    task_table,
    cotangent,
):
    gathered = (
        lax.all_gather(w_query, "fsdp", axis=0, tiled=True),
        lax.all_gather(w_key, "fsdp", axis=0, tiled=True),
        lax.all_gather(w_value, "fsdp", axis=0, tiled=True),
        lax.all_gather(w_out, "fsdp", axis=0, tiled=True),
        lax.all_gather(w_gate, "fsdp", axis=0, tiled=True),
        lax.all_gather(w_up, "fsdp", axis=0, tiled=True),
        lax.all_gather(w_down, "fsdp", axis=0, tiled=True),
        lax.all_gather(gain_attn, "fsdp", axis=0, tiled=True),
        lax.all_gather(gain_mlp, "fsdp", axis=0, tiled=True),
        lax.all_gather(task_table, "fsdp", axis=0, tiled=True),
    )
    query_w, key_w, value_w, out_w, gate_w, up_w, down_w, gain_one, gain_two, table = gathered
    source = patches[0].astype(jnp.float32)
    count, width = source.shape
    scale = HEAD_DIM ** (-0.5)
    span = min(512, count)
    blocks = count // span
    gain_one = gain_one.astype(jnp.float32)
    gain_two = gain_two.astype(jnp.float32)
    picked = (jnp.arange(table.shape[1]) == tasks[0]).astype(jnp.float32)
    resid = source + jnp.sum(table.astype(jnp.float32) * picked[None, :], axis=1)[None, :]
    normed = normalize(resid, gain_one).astype(jnp.bfloat16)
    query = matmul(normed, query_w).astype(jnp.bfloat16).reshape(count, HEADS, HEAD_DIM)
    keys = matmul(normed, key_w).astype(jnp.bfloat16).reshape(count, HEADS, HEAD_DIM)
    values = matmul(normed, value_w).astype(jnp.bfloat16).reshape(count, HEADS, HEAD_DIM)
    valid = (jnp.arange(count) < lengths[0])[None, None, :]

    def scores_of(rows):
        raw = jnp.einsum("qhd,khd->hqk", rows, keys, preferred_element_type=jnp.float32) * scale
        return jnp.where(valid, raw, FAR)

    contexts = []
    logsums = []
    for index in range(blocks):
        rows = query[index * span : (index + 1) * span]
        scores = scores_of(rows)
        top = jnp.max(scores, axis=-1, keepdims=True)
        expd = jnp.exp(scores - top)
        total = jnp.sum(expd, axis=-1, keepdims=True)
        probs = (expd / total).astype(jnp.bfloat16)
        block_out = jnp.einsum("hqk,khd->qhd", probs, values, preferred_element_type=jnp.float32)
        contexts.append(block_out.reshape(span, width).astype(jnp.bfloat16))
        logsums.append(top + jnp.log(total))
    context = jnp.concatenate(contexts, axis=0)
    mixed = resid + matmul(context, out_w)
    normed_two = normalize(mixed, gain_two).astype(jnp.bfloat16)
    gate = matmul(normed_two, gate_w)
    up = matmul(normed_two, up_w)
    hidden = gated(gate, up).astype(jnp.bfloat16)
    output = (mixed + matmul(hidden, down_w)).astype(jnp.bfloat16)[None]
    fetched = (
        lax.all_gather(w_query, "fsdp", axis=0, tiled=True),
        lax.all_gather(w_key, "fsdp", axis=0, tiled=True),
        lax.all_gather(w_value, "fsdp", axis=0, tiled=True),
        lax.all_gather(w_out, "fsdp", axis=0, tiled=True),
        lax.all_gather(w_gate, "fsdp", axis=0, tiled=True),
        lax.all_gather(w_up, "fsdp", axis=0, tiled=True),
        lax.all_gather(w_down, "fsdp", axis=0, tiled=True),
        lax.all_gather(gain_attn, "fsdp", axis=0, tiled=True),
        lax.all_gather(gain_mlp, "fsdp", axis=0, tiled=True),
        lax.all_gather(task_table, "fsdp", axis=0, tiled=True),
    )
    query_w, key_w, value_w, out_w, gate_w, up_w, down_w, gain_one, gain_two, table = fetched
    gain_one = gain_one.astype(jnp.float32)
    gain_two = gain_two.astype(jnp.float32)
    upstream = cotangent[0].astype(jnp.float32)
    branch_grad = upstream.astype(jnp.bfloat16)
    grad_down = outer_sum(hidden, branch_grad)
    hidden_grad = matmul_back(branch_grad, down_w)
    _, pull_gated = jax.vjp(gated, gate, up)
    gate_grad, up_grad = pull_gated(hidden_grad)
    gate_grad = gate_grad.astype(jnp.bfloat16)
    up_grad = up_grad.astype(jnp.bfloat16)
    grad_gate = outer_sum(normed_two, gate_grad)
    grad_up = outer_sum(normed_two, up_grad)
    second_grad = matmul_back(gate_grad, gate_w) + matmul_back(up_grad, up_w)
    _, pull_second = jax.vjp(normalize, mixed, gain_two)
    mixed_grad, grad_gain_two = pull_second(second_grad)
    mixed_grad = mixed_grad + upstream
    attn_grad = mixed_grad.astype(jnp.bfloat16)
    grad_out = outer_sum(context, attn_grad)
    context_grad = (
        matmul_back(attn_grad, out_w).astype(jnp.bfloat16).reshape(count, HEADS, HEAD_DIM)
    )
    key_grad = jnp.zeros((count, HEADS, HEAD_DIM), jnp.float32)
    value_grad = jnp.zeros((count, HEADS, HEAD_DIM), jnp.float32)
    query_parts = []
    for index in range(blocks):
        rows = query[index * span : (index + 1) * span]
        back_rows = context_grad[index * span : (index + 1) * span]
        probs = jnp.exp(scores_of(rows) - logsums[index])
        probs_low = probs.astype(jnp.bfloat16)
        prob_grad = jnp.einsum(
            "qhd,khd->hqk", back_rows, values, preferred_element_type=jnp.float32
        )
        weighted = jnp.sum(probs * prob_grad, axis=-1, keepdims=True)
        score_grad = (probs * (prob_grad - weighted)).astype(jnp.bfloat16)
        query_parts.append(
            jnp.einsum("hqk,khd->qhd", score_grad, keys, preferred_element_type=jnp.float32) * scale
        )
        key_grad = (
            key_grad
            + jnp.einsum("hqk,qhd->khd", score_grad, rows, preferred_element_type=jnp.float32)
            * scale
        )
        value_grad = value_grad + jnp.einsum(
            "hqk,qhd->khd", probs_low, back_rows, preferred_element_type=jnp.float32
        )
    query_grad = jnp.concatenate(query_parts, axis=0).reshape(count, width).astype(jnp.bfloat16)
    key_grad = key_grad.reshape(count, width).astype(jnp.bfloat16)
    value_grad = value_grad.reshape(count, width).astype(jnp.bfloat16)
    grad_query = outer_sum(normed, query_grad)
    grad_key = outer_sum(normed, key_grad)
    grad_value = outer_sum(normed, value_grad)
    first_grad = (
        matmul_back(query_grad, query_w)
        + matmul_back(key_grad, key_w)
        + matmul_back(value_grad, value_w)
    )
    _, pull_first = jax.vjp(normalize, resid, gain_one)
    resid_grad, grad_gain_one = pull_first(first_grad)
    resid_grad = resid_grad + mixed_grad
    grad_table = jnp.sum(resid_grad, axis=0)[:, None] * picked[None, :]
    shares = (
        lax.psum_scatter(grad_query, "fsdp", scatter_dimension=0, tiled=True),
        lax.psum_scatter(grad_key, "fsdp", scatter_dimension=0, tiled=True),
        lax.psum_scatter(grad_value, "fsdp", scatter_dimension=0, tiled=True),
        lax.psum_scatter(grad_out, "fsdp", scatter_dimension=0, tiled=True),
        lax.psum_scatter(grad_gate, "fsdp", scatter_dimension=0, tiled=True),
        lax.psum_scatter(grad_up, "fsdp", scatter_dimension=0, tiled=True),
        lax.psum_scatter(grad_down, "fsdp", scatter_dimension=0, tiled=True),
        lax.psum_scatter(grad_gain_one, "fsdp", scatter_dimension=0, tiled=True),
        lax.psum_scatter(grad_gain_two, "fsdp", scatter_dimension=0, tiled=True),
        lax.psum_scatter(grad_table, "fsdp", scatter_dimension=0, tiled=True),
    )
    (
        share_query,
        share_key,
        share_value,
        share_out,
        share_gate,
        share_up,
        share_down,
        share_one,
        share_two,
        share_table,
    ) = shares
    summed = (
        lax.psum(share_query.astype(jnp.bfloat16), "rep").astype(jnp.float32),
        lax.psum(share_key.astype(jnp.bfloat16), "rep").astype(jnp.float32),
        lax.psum(share_value.astype(jnp.bfloat16), "rep").astype(jnp.float32),
        lax.psum(share_out.astype(jnp.bfloat16), "rep").astype(jnp.float32),
        lax.psum(share_gate.astype(jnp.bfloat16), "rep").astype(jnp.float32),
        lax.psum(share_up.astype(jnp.bfloat16), "rep").astype(jnp.float32),
        lax.psum(share_down.astype(jnp.bfloat16), "rep").astype(jnp.float32),
        lax.psum(share_one.astype(jnp.bfloat16), "rep").astype(jnp.float32),
        lax.psum(share_two.astype(jnp.bfloat16), "rep").astype(jnp.float32),
        lax.psum(share_table.astype(jnp.bfloat16), "rep").astype(jnp.float32),
    )
    return (
        output,
        resid_grad[None],
        summed[0],
        summed[1],
        summed[2],
        summed[3],
        summed[4],
        summed[5],
        summed[6],
        summed[7],
        summed[8],
        summed[9],
    )


PARTS = [1, 1, 1, 1, 1, 1, 1, 2, 2, 2, 2, 2, 2, 2, 2, 2, 2]

UP_SKIP = (0, 128, 0, 128)

EVENTS = {
    "start": [("Z", 0), ("Z", 1), ("Z", 2)],
    "ready": [],
    "pre": [
        ("Y", 0), ("Z", 3), ("Z", 4), ("Y", 1), ("X", 0), ("Z", 5), ("Y", 2), ("X", 1), ("Z", 6),
        ("Y", 3), ("C", 0), ("X", 2), ("Y", 4), ("D", 0), ("Z", 7),
    ],
    "forward": {
        1: [("X", 3), ("Y", 5), ("Z", 9)],
        2: [("D", 1), ("C", 2), ("X", 4), ("Z", 10)],
        3: [("C", 3), ("X", 5), ("Y", 6), ("Z", 11)],
        4: [("D", 2), ("Y", 7), ("Y", 8)],
        5: [("C", 5), ("Y", 9)],
        6: [("D", 3), ("Z", 13)],
        7: [("X", 7), ("X", 8), ("Z", 15), ("Z", 16)],
        8: [("D", 4), ("Y", 11), ("Z", 17)],
        9: [("C", 9), ("Y", 12), ("Y", 13), ("Z", 19), ("X", 10)],
        10: [("D", 5), ("C", 6), ("C", 10), ("Y", 14), ("Z", 20)],
        11: [("Y", 16), ("Y", 17), ("Z", 21)],
    },
    "projected": {
        0: [("C", 1), ("Z", 8)],
        4: [("C", 4), ("Z", 12)],
        6: [("X", 6), ("Y", 10), ("Z", 14)],
        8: [("X", 9), ("Z", 18)],
        10: [("C", 7), ("Y", 15), ("X", 11)],
    },
    "attended": [
        ("D", 6), ("C", 8), ("X", 12), ("Y", 18), ("Z", 22), ("F", 0), ("F", 1), ("F", 2),
        ("F", 3), ("F", 4), ("F", 5),
    ],
    "normed": [("C", 11), ("X", 13), ("X", 14), ("X", 15), ("Y", 19), ("Z", 23)],
    "block": {
        0: [
            ("D", 7), ("D", 8), ("D", 9), ("D", 10), ("Y", 20), ("X", 16), ("C", 12), ("Z", 24),
            ("X", 17), ("D", 11), ("Z", 25), ("X", 18), ("Y", 21), ("C", 13), ("Z", 26), ("D", 12),
        ],
        2: [("C", 14), ("X", 19)],
        3: [("C", 19), ("X", 20), ("Y", 22), ("Y", 23)],
        4: [
            ("D", 13), ("D", 14), ("D", 15), ("C", 16), ("Y", 26), ("C", 17), ("X", 22), ("X", 23),
            ("C", 18), ("D", 16),
        ],
        5: [("X", 24)],
        6: [("X", 25)],
        7: [("C", 21), ("X", 26)],
        8: [
            ("D", 17), ("D", 18), ("D", 19), ("D", 20), ("D", 21), ("C", 23), ("D", 22), (0, 0),
            (0, 1), (0, 2),
        ],
        9: [("C", 24)],
        11: [("C", 25)],
        12: [("D", 23), ("D", 24), ("D", 25), ("D", 26), (1, 1), (1, 2)],
    },
    "outer": {
        0: [
            ("F", 7), ("F", 8), ("F", 9), ("F", 10), ("F", 11), ("F", 12), ("C", 15), ("C", 20),
            ("Y", 24),
        ],
        1: [("X", 21), ("Y", 25)],
        2: [("F", 13), ("F", 14), ("F", 15), ("F", 16)],
        3: [("C", 22)],
        4: [("F", 17), ("F", 18), ("F", 19), ("F", 20), ("F", 21), ("F", 22), (1, 0)],
        5: [("C", 26)],
        6: [("F", 23), ("F", 24), ("F", 25), ("F", 26)],
        7: [(2, 0)],
    },
    "ff_done": [(0, 3), (0, 4), (0, 5)],
    "second_back": [("F", 6), (2, 1)],
    "context_back": [(1, 3), (0, 6)],
    "backward": {
        0: [(3, 0), (2, 2), (1, 4)],
        1: [(1, 5), (1, 6), (0, 7), (3, 1)],
        2: [(3, 2), (2, 3), (1, 7)],
        3: [(4, 0), (0, 8)],
        4: [(4, 2), (2, 4), (1, 8)],
        5: [(3, 3), (2, 5), (0, 9)],
        6: [(2, 6), (2, 7), (1, 9)],
        7: [(5, 0), (4, 1), (5, 2), (3, 4), (2, 8), (0, 10)],
        8: [(6, 0), (5, 1), (6, 2), (4, 3), (3, 5), (1, 10)],
        9: [(5, 3), (4, 4), (3, 6), (3, 7), (0, 11)],
        10: [(6, 3), (5, 4), (4, 7), (3, 8), (2, 9), (1, 11)],
        11: [(4, 5), (5, 7), (4, 8), (2, 10), (0, 12)],
    },
    "attention_back": [],
    "last": {
        0: [(1, 12), (4, 6), (5, 8), (2, 11)],
        1: [(5, 5), (3, 9)],
        2: [(2, 12), (6, 5), (5, 6)],
        3: [(4, 9), (3, 10)],
    },
    "tail_one": [(6, 6), (5, 9), (3, 11)],
    "tail_two": [(4, 10), (3, 12)],
    "tail_three": [(4, 11), (5, 10), (4, 12), (5, 11), (5, 12)],
}


BF16 = jnp.bfloat16
F32 = jnp.float32
MESH = pl.DeviceIdType.MESH
PAIR = 2


def dot(left, right, on_left, on_right):
    return lax.dot_general(
        left, right, (((on_left,), (on_right,)), ((), ())), preferred_element_type=F32
    )


def aligned(index, step):
    return pl.multiple_of(index, step)


class Place:
    def __init__(self, reps, group):
        self.reps, self.group, self.deep = reps, group, group // PAIR
        self.rep = lax.axis_index("rep")
        self.pos = lax.axis_index("fsdp")
        self.x, self.core = self.rep // PAIR, self.rep % PAIR
        self.z, self.y = self.pos // PAIR, self.pos % PAIR

    def sibling(self):
        return (self.x * PAIR + 1 - self.core, self.pos)

    def across(self):
        return ((1 - self.x) * PAIR + self.core, self.pos)

    def beside(self):
        return (self.rep, self.z * PAIR + 1 - self.y)

    def deeper(self, step):
        return lax.rem(self.z + step, self.deep)

    def along(self, step):
        return (self.rep, self.deeper(step) * PAIR + self.y)

    def member(self, step):
        return (lax.rem(self.rep + step, self.reps), self.pos)

    def peer(self, step):
        return (self.rep, lax.rem(self.pos + step, self.group))


def send(source, target, send_sem, recv_sem, device):
    return pltpu.make_async_remote_copy(
        src_ref=source,
        dst_ref=target,
        send_sem=send_sem,
        recv_sem=recv_sem,
        device_id=device,
        device_id_type=MESH,
    )


class Gather:
    def __init__(self, place, ref, rows, base, half, skip, by_rows, along_sems, hop_sems):
        self.p, self.ref, self.half, self.skip = place, ref, half, skip
        self.along_sems, self.hop_sems = along_sems, hop_sems
        first, held = rows
        if by_rows:
            self.rows = pl.ds(aligned(first + place.core * held, 16), held)
            self.base = base
        else:
            self.rows = pl.ds(first, held)
            self.base = base + place.core * half

    def carried(self):
        p = self.p
        return pl.ds(
            aligned(self.base + p.x * self.skip, 128),
            self.half - self.skip,
        )

    def own(self):
        return self.ref.at[self.p.z, self.p.y, self.rows, self.carried()]

    def copies_z(self):
        p, out = self.p, []
        for step in range(1, p.deep):
            out.append(
                send(
                    self.own(),
                    self.own(),
                    self.along_sems.at[0, step - 1],
                    self.along_sems.at[1, step - 1],
                    p.along(step),
                )
            )
        return out

    def hop(self, index, part, device):
        return send(
            part, part, self.hop_sems.at[0, index], self.hop_sems.at[1, index], device
        )

    def copy_y(self):
        part = self.ref.at[:, self.p.y, self.rows, self.carried()]
        return self.hop(0, part, self.p.beside())

    def copy_x(self):
        p = self.p
        start = self.base + p.x * (self.half - self.skip)
        part = self.ref.at[:, :, self.rows, pl.ds(aligned(start, 128), self.skip)]
        return self.hop(1, part, p.across())

    def copy_core(self):
        p = self.p
        part = self.ref.at[:, :, self.rows, pl.ds(aligned(self.base, 128), self.half)]
        return self.hop(2, part, p.sibling())

    def start_z(self):
        for copy in self.copies_z():
            copy.start()

    def start_y(self):
        for copy in self.copies_z():
            copy.wait_recv()
        self.copy_y().start()

    def start_x(self):
        self.copy_y().wait_recv()
        if self.skip:
            self.copy_x().start()

    def start_core(self):
        if self.skip:
            self.copy_x().wait_recv()
        self.copy_core().start()

    def arrive(self):
        self.copy_core().wait_recv()

    def finish(self):
        for copy in self.copies_z():
            copy.wait_send()
        self.copy_y().wait_send()
        if self.skip:
            self.copy_x().wait_send()
        self.copy_core().wait_send()


class Reduce:
    def __init__(self, place, ref, recv, first, second, third, res, sems, x_first):
        self.p, self.ref, self.recv, self.first = place, ref, recv, first
        self.second, self.third, self.res, self.sems = second, third, res, sems
        self.x_first = x_first
        self.rows, self.half = recv.shape[2], recv.shape[3]
        self.by_rows = ref.shape[2] > self.rows
        self.steps = 6 if x_first else 5

    def share(self, core):
        if self.by_rows:
            return pl.ds(aligned(core * self.rows, 16), self.rows), slice(None)
        return slice(None), pl.ds(aligned(core * self.half, 128), self.half)

    def columns(self, core):
        return self.share(core)[1]

    def one(self, index, source, target, device):
        return send(source, target, self.sems.at[0, index], self.sems.at[1, index], device)

    def split(self, x):
        return pl.ds(aligned(x * (self.rows // 2), 16), self.rows // 2)

    def copies(self, phase):
        p = self.p
        if phase == 0:
            part = self.ref.at[(slice(None), slice(None), *self.share(1 - p.core))]
            return [self.one(0, part, self.recv, p.sibling())]
        if self.x_first:
            if phase == 1:
                part = self.recv.at[:, :, self.split(1 - p.x), :]
                return [self.one(1, part, self.first, p.across())]
            if phase == 2:
                return [self.one(2, self.first.at[:, 1 - p.y], self.second, p.beside())]
            if phase == 3:
                return [
                    self.one(
                        2 + step,
                        self.second.at[p.deeper(step)],
                        self.third.at[step - 1],
                        p.along(step),
                    )
                    for step in range(1, p.deep)
                ]
            last = 2 + p.deep
            if phase == 4:
                part = self.res.at[self.split(p.x), self.columns(p.core)]
                return [self.one(last, part, part, p.across())]
            part = self.res.at[self.share(p.core)]
            return [self.one(last + 1, part, part, p.sibling())]
        if phase == 1:
            return [self.one(1, self.recv.at[:, 1 - p.y], self.first, p.beside())]
        if phase == 2:
            return [
                self.one(
                    1 + step,
                    self.first.at[p.deeper(step)],
                    self.second.at[step - 1],
                    p.along(step),
                )
                for step in range(1, p.deep)
            ]
        last = 1 + p.deep
        if phase == 3:
            return [self.one(last, self.first.at[p.z], self.third, p.across())]
        part = self.res.at[self.share(p.core)]
        return [self.one(last + 1, part, part, p.sibling())]

    def add(self, phase):
        p = self.p
        if phase == 0:

            def fold(index, _):
                a, b = index // PAIR, index % PAIR
                self.recv[a, b] = self.recv[a, b] + self.ref[(a, b, *self.share(p.core))]
                return 0

            lax.fori_loop(0, p.deep * PAIR, fold, 0)
        elif self.x_first:
            if phase == 1:

                def fold(index, _):
                    a, b = index // PAIR, index % PAIR
                    self.first[a, b] = self.first[a, b] + self.recv[a, b, self.split(p.x), :]
                    return 0

                lax.fori_loop(0, p.deep * PAIR, fold, 0)
            elif phase == 2:

                def fold(index, _):
                    self.second[index] = self.second[index] + self.first[index, p.y]
                    return 0

                lax.fori_loop(0, p.deep, fold, 0)
            elif phase == 3:
                total = self.second[p.z].astype(F32)
                for step in range(1, p.deep):
                    total = total + self.third[step - 1].astype(F32)
                self.res[self.split(p.x), self.columns(p.core)] = total.astype(BF16)
        elif phase == 1:

            def fold(index, _):
                self.first[index] = self.first[index] + self.recv[index, p.y]
                return 0

            lax.fori_loop(0, p.deep, fold, 0)
        elif phase == 2:
            total = self.first[p.z].astype(F32)
            for step in range(1, p.deep):
                total = total + self.second[step - 1].astype(F32)
            self.first[p.z] = total.astype(BF16)
        elif phase == 3:
            self.res[self.share(p.core)] = self.first[p.z] + self.third[...]

    def step(self, phase):
        if phase > 0:
            for copy in self.copies(phase - 1):
                copy.wait()
            self.add(phase - 1)
        if phase < self.steps:
            for copy in self.copies(phase):
                copy.start()


def layer(config, *refs):
    (reps, group, count, width, heads, hidden, tasks_held) = config
    (
        lengths_ref, tasks_ref, gain_one_ref, gain_two_ref, table_ref, patches_ref, cot_ref,
        wq_ref, wk_ref, wv_ref, wo_ref, wg_ref, wu_ref, wd_ref,
        out_ref, grad_ref, done_in, done_gate, done_up, done_down, done_small, spare,
        w_in, w_out, w_ff, w_down,
        normed, qkv, context, extra, mixed, tokens, second, hid, both_g,
        acc_out, acc_in, key_extra, vectors, small_buf, small_grads, member_buf, peer_out, peer_buf,
        *rest,
    ) = refs
    p = Place(reps, group)
    deep = p.deep
    head_dim = width // heads
    scale = head_dim ** -0.5
    groups = width // 256
    quad = heads // groups
    rows = wo_ref.shape[0]
    down_rows = wd_ref.shape[0] // 2
    (
        local_sems, along_sems, hop_sems, small_sems, member_sems, peer_sems, red_sems, out_sems,
        *red_bufs,
    ) = rest

    specs = []
    cuts = [0]

    def spec(ref, base, half, skip):
        parts = PARTS[len(cuts) - 1]
        held_rows = ref.shape[2] // parts
        for i in range(parts):
            specs.append((ref, (i * held_rows, held_rows), base, half, skip, False))
        cuts.append(len(specs))

    pairs = 2 * groups
    for pair in range(pairs):
        specs.append((w_in.at[pair // 2], (0, rows // 2), (pair % 2) * 384, 384, 128, True))
        cuts.append(len(specs))
    spec(w_out.at[0], 0, 384, 128)
    for j in range(2):
        for u in range(2):
            spec(w_ff.at[j], u * 512, 256, 128)
            spec(w_ff.at[2 + j], u * 512, 256, UP_SKIP[2 * j + u])
            if u == 0:
                spec(w_down.at[j], 0, 384, 128)
    chunks = [Gather(p, *one, along_sems.at[i], hop_sems.at[i]) for i, one in enumerate(specs)]

    sem = 0
    fills = [[] for _ in PARTS]
    own_rows = pl.ds(aligned(p.core * (rows // 2), 16), rows // 2)
    for pair in range(pairs):
        for i in range(2):
            source = pl.ds(pair * 128, 128)
            start = (pair % 2) * 384 + (p.x + i) * 128
            target = w_in.at[pair // 2, p.z, p.y, own_rows, pl.ds(aligned(start, 128), 128)]
            choice = (wq_ref, wk_ref) if i == 0 else (wk_ref, wv_ref)
            fills[pair].append(
                tuple(
                    pltpu.make_async_copy(w.at[own_rows, source], target, local_sems.at[sem])
                    for w in choice
                )
            )
            sem += 1
    columns = pl.ds(aligned(p.core * 384 + p.x * 128, 128), 256)
    fills[pairs].append(
        pltpu.make_async_copy(
            wo_ref.at[:, columns], w_out.at[0, p.z, p.y, :, columns], local_sems.at[sem]
        )
    )
    sem += 1
    at = pairs + 1

    def fill(source, target):
        nonlocal sem
        fills[at].append(pltpu.make_async_copy(source, target, local_sems.at[sem]))
        sem += 1

    def segment(ref, held, j, seg):
        fill(
            ref.at[:, pl.ds(aligned(seg * 256 + j * 128, 128), 128)],
            held.at[p.z, p.y, :, pl.ds(aligned(seg * 128, 128), 128)],
        )

    for j in range(2):
        for u in range(2):
            segment(wg_ref, w_ff.at[j], j, 4 * u + 2 * p.core + p.x)
            at += 1
            if UP_SKIP[2 * j + u]:
                segment(wu_ref, w_ff.at[2 + j], j, 4 * u + 2 * p.core + p.x)
            else:
                for i in range(2):
                    segment(wu_ref, w_ff.at[2 + j], j, 4 * u + 2 * p.core + i)
            at += 1
            if u == 0:
                fill(
                    wd_ref.at[pl.ds(j * down_rows, down_rows), columns],
                    w_down.at[j, p.z, p.y, :, columns],
                )
                at += 1

    def fill_start(i):
        for copy in fills[i]:
            if isinstance(copy, tuple):
                for x in range(2):

                    @pl.when(p.x == x)
                    def _(copy=copy, x=x):
                        copy[x].start()
            else:
                copy.start()

    def fill_wait(i):
        for copy in fills[i]:
            (copy[0] if isinstance(copy, tuple) else copy).wait()

    reds = []
    grads = []
    for j in range(2):
        grads += [
            (w_ff.at[j], done_gate.at[j], True),
            (w_ff.at[2 + j], done_up.at[j], False),
            (w_down.at[j], done_down.at[j], True),
        ]
    grads += [(w_out.at[0], done_in.at[groups], True)]
    for pair in range(pairs):
        columns = pl.ds((pair % 2) * 384, 384)
        grads.append(
            (
                w_ff.at[pair // 2, :, :, :, columns],
                done_in.at[pair // 2, :, columns],
                False,
            )
        )
    for i, (ref, _, x_first) in enumerate(grads):
        recv, first, sec, third, res = red_bufs[5 * i : 5 * i + 5]
        reds.append(Reduce(p, ref, recv, first, sec, third, res, red_sems.at[i], x_first))

    tokens_in = pltpu.make_async_copy(patches_ref, tokens, out_sems.at[0])
    tokens_in.start()
    for i in range(len(fills)):
        fill_start(i)
    shard = width // group
    own_small = jnp.concatenate(
        [ref[...].astype(F32) for ref in (gain_one_ref, gain_two_ref, table_ref)]
        + [jnp.zeros((14 - tasks_held, shard), F32)],
        0,
    )
    small_buf[p.pos] = jnp.concatenate(
        [own_small, jnp.zeros((16, 128 - shard), F32)], 1
    ).astype(BF16)
    barrier = pltpu.get_barrier_semaphore()
    for step in range(1, reps):
        pl.semaphore_signal(barrier, inc=1, device_id=p.member(step), device_id_type=MESH)
    for step in range(1, group):
        pl.semaphore_signal(barrier, inc=1, device_id=p.peer(step), device_id_type=MESH)
    pl.semaphore_wait(barrier, reps + group - 2)
    small_copies = [
        send(
            small_buf.at[p.pos], small_buf.at[p.pos],
            small_sems.at[0, step - 1], small_sems.at[1, step - 1], p.peer(step),
        )
        for step in range(1, group)
    ]
    for copy in small_copies:
        copy.start()

    def go(*events):
        for kind, i in events:
            if kind == "Z":
                if i in cuts:
                    fill_wait(cuts.index(i))
                chunks[i].start_z()
            elif kind == "Y":
                chunks[i].start_y()
            elif kind == "X":
                chunks[i].start_x()
            elif kind == "C":
                chunks[i].start_core()
            elif kind == "D":
                chunks[i].arrive()
            elif kind == "F":
                chunks[i].finish()
            else:
                reds[i].step(kind)

    go(*EVENTS["start"])

    for copy in small_copies:
        copy.wait_recv()
    wide_row = lax.broadcasted_iota(jnp.int32, (128, width), 0)
    wide_col = lax.broadcasted_iota(jnp.int32, (128, width), 1)
    total = None
    for f in range(group):
        place_f = jnp.logical_and(wide_col == wide_row + f * shard, wide_row < shard)
        part = dot(small_buf[f], place_f.astype(F32).astype(BF16), 1, 0)
        total = part if total is None else total + part
    vectors[...] = total
    task = tasks_ref[0]
    chosen = [(task == k).astype(F32) for k in range(tasks_held)]

    def task_row():
        row = vectors[2:3, :] * chosen[0]
        for k in range(1, tasks_held):
            row = row + vectors[2 + k : 3 + k, :] * chosen[k]
        return row

    position = lax.broadcasted_iota(jnp.int32, (16, count), 1)
    kind = lax.broadcasted_iota(jnp.int32, (16, count), 0)
    mask = jnp.where(position < lengths_ref[0], 0.0, FAR)
    key_extra[...] = jnp.where(
        kind < 3, 1.0, jnp.where(kind == 3, mask, 0.0)
    ).astype(BF16)

    tokens_in.wait()
    block = 256
    blocks = count // block

    def rows_of(i, size=block):
        return pl.ds(aligned(i * size, size), size)

    def norm_one(i, _):
        r = rows_of(i)
        resid = tokens[r, :].astype(F32) + task_row()
        inv = lax.rsqrt(jnp.mean(resid * resid, axis=-1, keepdims=True) + EPS)
        normed[r, :] = (resid * inv * vectors[0:1, :]).astype(BF16)
        return 0

    go(*EVENTS["ready"])
    lax.fori_loop(0, blocks, norm_one, 0)

    go(*EVENTS["pre"])

    def project(pair):
        g = pair // 2
        base = aligned((pair % 2) * 384, 128)
        weight = w_in[g, :, :, :, pl.ds(base, 384)].reshape(width, 384)
        got = dot(weight, normed[...], 0, 1)
        qkv[g, pl.ds(base, 128)] = (got[:128] * scale).astype(BF16)
        qkv[g, pl.ds(base + 128, 256)] = got[128:].astype(BF16)

    tile = 256
    tiles = count // tile
    sixteen = lax.broadcasted_iota(jnp.int32, (16, count), 0)

    def offsets(h):
        g, left = h // quad, h % quad
        return g, (left // 2) * 384 + (left % 2) * head_dim

    def forward_head(h):
        g, off = offsets(h)
        ask = jnp.concatenate(
            [
                qkv[g, pl.ds(aligned(off, 64), head_dim), :],
                (sixteen == 3).astype(F32).astype(BF16),
            ],
            0,
        )
        scores, top = [], None
        for j in range(tiles):
            cut = slice(j * tile, (j + 1) * tile)
            keys = jnp.concatenate(
                [qkv[g, pl.ds(aligned(off + 128, 64), head_dim), cut], key_extra[:, cut]], 0
            )
            s = dot(keys, ask, 0, 0)
            scores.append(s)
            here = jnp.max(s, axis=0, keepdims=True)
            top = here if top is None else jnp.maximum(top, here)
        acc = None
        for j in range(tiles):
            cut = slice(j * tile, (j + 1) * tile)
            expd = jnp.exp(scores[j] - top).astype(BF16)
            vals = jnp.concatenate(
                [
                    qkv[g, pl.ds(aligned(off + 256, 64), head_dim), cut],
                    jnp.ones((16, tile), BF16),
                ],
                0,
            )
            part = dot(vals, expd, 1, 0)
            acc = part if acc is None else acc + part
        total = acc[head_dim : head_dim + 1]
        exact = acc[:head_dim] * (1.0 / total)
        low = exact.astype(BF16)
        missing = (exact - low.astype(F32)).astype(BF16)
        r = pl.ds(aligned(h * head_dim, 64), head_dim)
        context[r, :] = low
        both_g[r, :] = missing
        extra[0, pl.ds(h, 1), :] = -(top + jnp.log(total))

    def splits(row, fourth):
        high = row.astype(BF16).astype(F32)
        mid = (row - high).astype(BF16).astype(F32)
        low = row - high - mid
        return jnp.where(
            sixteen == 0,
            high,
            jnp.where(
                sixteen == 1,
                mid,
                jnp.where(sixteen == 2, low, jnp.where(sixteen == 3, fourth, 0.0)),
            ),
        ).astype(BF16)

    def each_head(h, _):
        for at, events in EVENTS["forward"].items():

            @pl.when(h == at)
            def _(events=events):
                go(*events)

        @pl.when(h % 2 == 0)
        def _():
            project(h // 2)

        for at, events in EVENTS["projected"].items():

            @pl.when(h == at)
            def _(events=events):
                go(*events)

        forward_head(h)
        return 0

    lax.fori_loop(0, heads, each_head, 0)
    kept = both_g.at[pl.ds(0, width), :]
    first_out = 6 + len(grads)
    keep = pltpu.make_async_copy(kept, spare, out_sems.at[first_out])
    fetch = pltpu.make_async_copy(spare, kept, out_sems.at[first_out + 1])
    keep.start()
    go(*EVENTS["attended"])

    big = 256

    def out_project(i, _):
        r = rows_of(i, big)
        m = tokens[r, :].astype(F32) + task_row()
        m = m + dot(context[:, r], w_out[0].reshape(width, width), 0, 0)
        mixed[r, :] = m
        acc_out[r, :] = m
        acc_in[r, :] = jnp.zeros_like(m)
        inv = lax.rsqrt(jnp.mean(m * m, axis=-1, keepdims=True) + EPS)
        second[r, :] = (m * inv * vectors[1:2, :]).astype(BF16)
        return 0

    lax.fori_loop(0, count // big, out_project, 0)
    cot_in = pltpu.make_async_copy(cot_ref, tokens, out_sems.at[1])
    cot_in.start()
    go(*EVENTS["normed"])
    cot_in.wait()

    curve = 0.7978845608028654
    cube = 0.044715
    part = 512
    keep.wait()

    def ff_tile(t, _):
        j, u = t // 2, t % 2
        cols = pl.ds(aligned(u * part, part), part)
        half = pl.ds(u * (deep // 2), deep // 2)

        def block_of(i, _):
            for at, events in EVENTS["block"].items():

                @pl.when(t * (count // big) + i == at)
                def _(events=events):
                    go(*events)

            r = rows_of(i, big)
            gate_w = w_ff[j, :, :, :, cols].reshape(width, part)
            up_w = w_ff[2 + j, :, :, :, cols].reshape(width, part)
            down_w = w_down[j, half].reshape(part, width)
            two = second[r, :]
            gate = dot(two, gate_w, 1, 0)
            up = dot(two, up_w, 1, 0)
            back = dot(tokens[r, :], down_w, 1, 1)
            square = gate * gate
            bend = jnp.tanh(curve * gate * (1.0 + cube * square))
            flat = 0.5 * (1.0 + bend)
            gelu = gate * flat
            slope = flat + 0.5 * gate * (1.0 - bend * bend) * (
                curve * (1.0 + 3.0 * cube * square)
            )
            h = (gelu * up).astype(BF16)
            g_grad = (back * up * slope).astype(BF16)
            u_grad = (back * gelu).astype(BF16)
            hid[r, :] = h
            both_g[r, 0:part] = g_grad
            both_g[r, part : 2 * part] = u_grad
            o = dot(h, down_w, 1, 0)
            n = dot(g_grad, gate_w, 1, 1) + dot(u_grad, up_w, 1, 1)
            acc_out[r, :] = acc_out[r, :] + o
            acc_in[r, :] = acc_in[r, :] + n
            return 0

        lax.fori_loop(0, count // big, block_of, 0)
        def pause(k):
            for at, events in EVENTS["outer"].items():

                @pl.when(t * 2 + k == at)
                def _(events=events):
                    go(*events)

        pause(0)
        w_down[j, half] = (
            dot(hid[...], tokens[...], 0, 0).astype(BF16).reshape(deep // 2, 2, down_rows, width)
        )
        pause(1)
        for v in range(2):
            some = slice(v * width // 2, (v + 1) * width // 2)
            to = slice(v * deep // 2, (v + 1) * deep // 2)
            both = dot(second[:, some], both_g[...], 0, 0).astype(BF16)
            both = both.reshape(deep // 2, 2, rows, 2 * part)
            w_ff[j, to, :, :, cols] = both[..., :part]
            w_ff[2 + j, to, :, :, cols] = both[..., part:]
        return 0

    lax.fori_loop(0, 4, ff_tile, 0)
    fetch.start()
    go(*EVENTS["ff_done"])

    small_grads[...] = jnp.zeros_like(small_grads)

    def second_back(i, _):
        r = rows_of(i)
        m = mixed[r, :]
        second[r, :] = acc_out[r, :].astype(BF16)
        inv = lax.rsqrt(jnp.mean(m * m, axis=-1, keepdims=True) + EPS)
        unit = m * inv
        got = acc_in[r, :]
        scaled = got * vectors[1:2, :]
        grad = tokens[r, :].astype(F32) + inv * (
            scaled - unit * jnp.mean(scaled * unit, axis=-1, keepdims=True)
        )
        small_grads[1:2, :] = small_grads[1:2, :] + jnp.sum(got * unit, axis=0, keepdims=True)
        mixed[r, :] = grad
        tokens[r, :] = grad.astype(BF16)
        return 0

    lax.fori_loop(0, blocks, second_back, 0)
    result = pltpu.make_async_copy(second, out_ref, out_sems.at[2])
    result.start()
    go(*EVENTS["second_back"])

    out_w = w_out[0].reshape(width, width)
    acc_out[0:width, :] = dot(context[...], tokens[...], 1, 0)
    lowered = dot(out_w, tokens[...], 1, 1).astype(BF16)
    fetch.wait()
    for h in range(heads):
        r = slice(h * head_dim, (h + 1) * head_dim)
        low = lowered[r]
        exact = context[r, :].astype(F32) + both_g[r, :].astype(F32)
        delta = jnp.sum(low.astype(F32) * exact, axis=0, keepdims=True)
        extra[1, h : h + 1, :] = -delta
        context[r, :] = low
    w_out[0] = acc_out[0:width, :].astype(BF16).reshape(deep, 2, rows, width)
    go(*EVENTS["context_back"])

    def backward_head(h):
        g, off = offsets(h)
        q_rows = pl.ds(aligned(off, 64), head_dim)
        k_rows = pl.ds(aligned(off + 128, 64), head_dim)
        v_rows = pl.ds(aligned(off + 256, 64), head_dim)
        query = qkv[g, q_rows, :]
        all_keys = qkv[g, k_rows, :]
        all_vals = qkv[g, v_rows, :]
        back = context[pl.ds(aligned(h * head_dim, 64), head_dim), :]
        ask = jnp.concatenate([query, splits(extra[0, pl.ds(h, 1), :], 1.0)], 0)
        back_ask = jnp.concatenate([back, splits(extra[1, pl.ds(h, 1), :], 0.0)], 0)
        query_grad = None
        for j in range(tiles):
            cut = slice(j * tile, (j + 1) * tile)
            keys = all_keys[:, cut]
            lift = key_extra[:, cut]
            probs = jnp.exp(dot(jnp.concatenate([keys, lift], 0), ask, 0, 0))
            gap = dot(jnp.concatenate([all_vals[:, cut], lift], 0), back_ask, 0, 0)
            score_grad = (probs * gap).astype(BF16)
            part = dot(keys, score_grad, 1, 0)
            query_grad = part if query_grad is None else query_grad + part
            qkv[g, k_rows, cut] = dot(query, score_grad, 1, 1).astype(BF16)
            qkv[g, v_rows, cut] = dot(back, probs.astype(BF16), 1, 1).astype(BF16)
        qkv[g, q_rows, :] = (query_grad * scale).astype(BF16)

    def in_grad(pair):
        weight = dot(
            normed[...], qkv[pair // 2, pl.ds(aligned((pair % 2) * 384, 128), 384), :], 0, 1
        )
        w_ff[pair // 2, :, :, :, pl.ds(aligned((pair % 2) * 384, 128), 384)] = weight.astype(
            BF16
        ).reshape(deep, 2, rows, 384)

    def each_back(h, _):
        backward_head(h)

        @pl.when(h % 2 == 1)
        def _():
            in_grad(h // 2)

        for at, events in EVENTS["backward"].items():

            @pl.when(h == at)
            def _(events=events):
                go(*events)

        return 0

    lax.fori_loop(0, heads, each_back, 0)
    result.wait()
    again = pltpu.make_async_copy(patches_ref, second, out_sems.at[3])
    again.start()
    go(*EVENTS["attention_back"])
    again.wait()

    def first_norm_back(i, _):
        for at, events in EVENTS["last"].items():

            @pl.when(i == at)
            def _(events=events):
                go(*events)

        r = rows_of(i)
        got = dot(qkv[0, :, r], w_in[0].reshape(width, width), 0, 1)
        for g in range(1, groups):
            got = got + dot(qkv[g, :, r], w_in[g].reshape(width, width), 0, 1)
        resid = second[r, :].astype(F32) + task_row()
        inv = lax.rsqrt(jnp.mean(resid * resid, axis=-1, keepdims=True) + EPS)
        unit = resid * inv
        scaled = got * vectors[0:1, :]
        grad = mixed[r, :] + inv * (
            scaled - unit * jnp.mean(scaled * unit, axis=-1, keepdims=True)
        )
        small_grads[0:1, :] = small_grads[0:1, :] + jnp.sum(got * unit, axis=0, keepdims=True)
        small_grads[7:8, :] = small_grads[7:8, :] + jnp.sum(grad, axis=0, keepdims=True)
        acc_out[r, :] = grad
        return 0

    lax.fori_loop(0, blocks, first_norm_back, 0)
    grad_out = pltpu.make_async_copy(acc_out, grad_ref, out_sems.at[4])
    grad_out.start()
    for k in range(tasks_held):
        small_grads[2 + k : 3 + k, :] = small_grads[7:8, :] * chosen[k]

    member_buf[p.rep] = small_grads[...]
    member_copies = [
        send(
            member_buf.at[p.rep], member_buf.at[p.rep],
            member_sems.at[0, step - 1], member_sems.at[1, step - 1], p.member(step),
        )
        for step in range(1, reps)
    ]
    for copy in member_copies:
        copy.start()
    go(*EVENTS["tail_one"])
    for copy in member_copies:
        copy.wait_recv()
    summed = member_buf[0]
    for i in range(1, reps):
        summed = summed + member_buf[i]
    peer_out[...] = jnp.zeros_like(peer_out)
    for f in range(group):
        peer_out[f, :, 0:shard] = summed[:, f * shard : (f + 1) * shard]
    peer_copies = []
    for step in range(1, group):
        target = lax.rem(p.pos + step, group)
        peer_copies.append(
            send(
                peer_out.at[target], peer_buf.at[p.pos],
                peer_sems.at[0, step - 1], peer_sems.at[1, step - 1], p.peer(step),
            )
        )
    for copy in peer_copies:
        copy.start()
    peer_buf[p.pos] = peer_out[p.pos]
    go(*EVENTS["tail_two"])
    for copy in peer_copies:
        copy.wait_recv()
    summed = peer_buf[0]
    for i in range(1, group):
        summed = summed + peer_buf[i]
    small_grads[:, 0:128] = summed
    ends = [
        pltpu.make_async_copy(small_grads.at[:, pl.ds(0, 128)], done_small, out_sems.at[5])
    ]
    ends[0].start()
    go(*EVENTS["tail_three"])
    for i, (_, done, _) in enumerate(grads):
        copy = pltpu.make_async_copy(reds[i].res, done, out_sems.at[6 + i])
        copy.start()
        ends.append(copy)
    for copy in small_copies + member_copies + peer_copies:
        copy.wait_send()
    for copy in ends:
        copy.wait()
    grad_out.wait()


def fits(reps, group, args):
    patches, w_query, w_gate, w_down = args[0], args[3], args[7], args[9]
    return (
        reps == 4
        and group == 8
        and patches.shape == (1, 1024, 768)
        and w_query.shape == (96, 768)
        and w_gate.shape == (96, 2048)
        and w_down.shape == (256, 768)
    )


def ending(config, *refs):
    groups, group, rows, held = config
    sources, small = refs[:6], refs[6]
    targets, (one, two, table) = refs[7:16], refs[16:19]
    in_sems, out_sems = refs[19:21]
    held_out, held_grad, from_in, from_gate, from_up, from_down = refs[21:27]
    made = refs[27:34]
    parts = 4
    span = held_out.shape[0] // parts
    brought, copies = [], []
    middles = (from_in, from_gate, from_up, from_down)
    for i, (source, middle) in enumerate(zip(sources[2:], middles)):
        brought.append(pltpu.make_async_copy(source, middle, in_sems.at[i]))
        brought[-1].start()
    whole = []
    for i in range(parts):
        r = pl.ds(i * span, span)
        for k, middle in enumerate((held_out, held_grad)):
            at = 4 + 2 * i + k
            whole.append(
                (
                    pltpu.make_async_copy(sources[k].at[r], middle.at[r], in_sems.at[at]),
                    pltpu.make_async_copy(middle.at[r], targets[k].at[0, r], out_sems.at[at]),
                )
            )
            whole[-1][0].start()

    def finish(i):
        copies.append(pltpu.make_async_copy(made[i], targets[2 + i], out_sems.at[12 + i]))
        copies[-1].start()

    def pass_on(count):
        for _ in range(count):
            first, then = whole.pop(0)
            first.wait()
            then.start()
            copies.append(then)

    brought[0].wait()
    for i in range(3):
        for g in range(groups):
            for core in range(2):
                start = core * 384 + i * 128
                to = g * 256 + core * 128
                made[i][:, to : to + 128] = from_in[g, :, start : start + 128].astype(F32)
        finish(i)
    made[3][...] = from_in[groups].astype(F32)
    finish(3)
    for k, source in enumerate((from_gate, from_up)):
        brought[1 + k].wait()
        for j in range(2):
            for f in range(group):
                to = f * 256 + j * 128
                made[4 + k][:, to : to + 128] = source[j, :, f * 128 : (f + 1) * 128].astype(F32)
        finish(4 + k)
        pass_on(2)
    brought[3].wait()
    half = from_down.shape[1]
    for j in range(2):
        made[6][j * half : (j + 1) * half, :] = from_down[j].astype(F32)
    finish(6)
    pass_on(4)
    one[...] = small[0, :rows]
    two[...] = small[1, :rows]
    table[...] = small[2 : 2 + held, :rows]
    for copy in copies:
        copy.wait()


def fused(
    reps, group, patches, lengths, tasks, w_query, w_key, w_value, w_out, w_gate, w_up, w_down,
    gain_attn, gain_mlp, task_table, cotangent,
):
    count, width = patches.shape[1:]
    rows, hidden = w_gate.shape
    held = task_table.shape[1]
    deep = group // PAIR
    groups = width // 256
    down_rows = w_down.shape[0] // 2

    def of(rows, columns, x_first, by_rows=False):
        whole = (rows, columns)
        half = columns // 2
        if by_rows:
            rows, half = rows // 2, columns
        if x_first:
            shapes = [
                (deep, 2, rows, half),
                (deep, 2, rows // 2, half),
                (deep, rows // 2, half),
                (deep - 1, rows // 2, half),
                whole,
            ]
        else:
            shapes = [
                (deep, 2, rows, half),
                (deep, rows, half),
                (deep - 1, rows, half),
                (rows, half),
                whole,
            ]
        return [pltpu.VMEM(shape, BF16) for shape in shapes]

    red_bufs = []
    for j in range(2):
        red_bufs += of(rows, hidden // 2, True)
        red_bufs += of(rows, hidden // 2, False)
        red_bufs += of(down_rows, width, True)
    red_bufs += of(rows, width, True)
    for _ in range(2 * groups):
        red_bufs += of(rows, width // 2, False, True)
    sums = 7 + 2 * groups
    chunks = sum(PARTS)
    scratch = [
        pltpu.VMEM((groups, deep, 2, rows, width), BF16),
        pltpu.VMEM((1, deep, 2, rows, width), BF16),
        pltpu.VMEM((4, deep, 2, rows, hidden // 2), BF16),
        pltpu.VMEM((2, deep, 2, down_rows, width), BF16),
        pltpu.VMEM((count, width), BF16),
        pltpu.VMEM((groups, width, count), BF16),
        pltpu.VMEM((width, count), BF16),
        pltpu.VMEM((2, 16, count), F32),
        pltpu.VMEM((count, width), F32),
        pltpu.VMEM((count, width), BF16),
        pltpu.VMEM((count, width), BF16),
        pltpu.VMEM((count, 512), BF16),
        pltpu.VMEM((count, 1024), BF16),
        pltpu.VMEM((count, width), F32),
        pltpu.VMEM((count, width), F32),
        pltpu.VMEM((16, count), BF16),
        pltpu.VMEM((16, width), F32),
        pltpu.VMEM((group, 16, 128), BF16),
        pltpu.VMEM((8, width), F32),
        pltpu.VMEM((reps, 8, width), F32),
        pltpu.VMEM((group, 8, 128), F32),
        pltpu.VMEM((group, 8, 128), F32),
        pltpu.SemaphoreType.DMA((groups * 4 + 1 + 14,)),
        pltpu.SemaphoreType.DMA((chunks, 2, deep - 1)),
        pltpu.SemaphoreType.DMA((chunks, 2, 3)),
        pltpu.SemaphoreType.DMA((2, group - 1)),
        pltpu.SemaphoreType.DMA((2, reps - 1)),
        pltpu.SemaphoreType.DMA((2, group - 1)),
        pltpu.SemaphoreType.DMA((sums, 2, deep + 4)),
        pltpu.SemaphoreType.DMA((10 + sums,)),
        *red_bufs,
    ]
    shape = jax.ShapeDtypeStruct
    smem = pl.BlockSpec(memory_space=pltpu.SMEM)
    anywhere = pl.BlockSpec(memory_space=pl.ANY)
    config = (reps, group, count, width, HEADS, hidden, held)
    output, grad, done_in, done_gate, done_up, done_down, done_small, _ = pl.pallas_call(
        functools.partial(layer, config),
        out_shape=[
            shape((count, width), BF16),
            shape((count, width), F32),
            shape((groups + 1, rows, width), BF16),
            shape((2, rows, hidden // 2), BF16),
            shape((2, rows, hidden // 2), BF16),
            shape((2, down_rows, width), BF16),
            shape((8, 128), F32),
            shape((width, count), BF16),
        ],
        in_specs=[smem, smem] + [pl.BlockSpec(memory_space=pltpu.VMEM)] * 3 + [anywhere] * 9,
        out_specs=[anywhere] * 8,
        scratch_shapes=scratch,
        compiler_params=pltpu.CompilerParams(
            collective_id=0, has_side_effects=True, vmem_limit_bytes=62 * 1024 * 1024
        ),
        name="layer",
    )(
        lengths, tasks, gain_attn[None], gain_mlp[None], task_table.T, patches[0], cotangent[0],
        w_query, w_key, w_value, w_out, w_gate, w_up, w_down,
    )
    lane = pl.BlockSpec(memory_space=pltpu.VMEM)
    sizes = [(rows, width)] * 4 + [(rows, hidden)] * 2 + [(2 * down_rows, width)]
    results = pl.pallas_call(
        functools.partial(ending, (groups, group, rows, held)),
        out_shape=[
            shape((1, count, width), BF16),
            shape((1, count, width), F32),
            *[shape(size, F32) for size in sizes],
            shape((rows,), F32),
            shape((rows,), F32),
            shape((held, rows), F32),
        ],
        in_specs=[anywhere] * 6 + [lane],
        out_specs=[anywhere] * 9 + [lane] * 3,
        scratch_shapes=[
            pltpu.SemaphoreType.DMA((12,)),
            pltpu.SemaphoreType.DMA((19,)),
            pltpu.VMEM((count, width), BF16),
            pltpu.VMEM((count, width), F32),
            pltpu.VMEM((groups + 1, rows, width), BF16),
            pltpu.VMEM((2, rows, hidden // 2), BF16),
            pltpu.VMEM((2, rows, hidden // 2), BF16),
            pltpu.VMEM((2, down_rows, width), BF16),
            *[pltpu.VMEM(size, F32) for size in sizes],
        ],
        compiler_params=pltpu.CompilerParams(vmem_limit_bytes=62 * 1024 * 1024),
        name="ending",
    )(output, grad, done_in, done_gate, done_up, done_down, done_small)
    return (*results[:11], results[11].T)


def solution(mesh):
    in_specs = (
        P(("rep", "fsdp"), None, None),
        P(("rep", "fsdp")),
        P(("rep", "fsdp")),
        P("fsdp", None),
        P("fsdp", None),
        P("fsdp", None),
        P("fsdp", None),
        P("fsdp", None),
        P("fsdp", None),
        P("fsdp", None),
        P("fsdp"),
        P("fsdp"),
        P("fsdp", None),
        P(("rep", "fsdp"), None, None),
    )
    out_specs = (
        P(("rep", "fsdp"), None, None),
        P(("rep", "fsdp"), None, None),
        P("fsdp", None),
        P("fsdp", None),
        P("fsdp", None),
        P("fsdp", None),
        P("fsdp", None),
        P("fsdp", None),
        P("fsdp", None),
        P("fsdp"),
        P("fsdp"),
        P("fsdp", None),
    )
    reps, group = mesh.shape["rep"], mesh.shape["fsdp"]

    def per_device(*args):
        if fits(reps, group, args):
            return fused(reps, group, *args)
        return plain(*args)

    return jax.shard_map(
        per_device, mesh=mesh, in_specs=in_specs, out_specs=out_specs, check_vma=False
    )
```

```python
import functools

import jax
import jax.numpy as jnp
from jax import lax
from jax.experimental import pallas as pl
from jax.experimental.pallas import tpu as pltpu
from jax.sharding import PartitionSpec as P

HEADS = 12
HEAD_DIM = 64


EPS = 1e-06
FAR = -1e30


def normalize(resid, gain):
    return resid * lax.rsqrt(jnp.mean(resid * resid, axis=-1, keepdims=True) + EPS) * gain


def gated(gate, up):
    return jax.nn.gelu(gate, approximate=True) * up


def matmul(left, right):
    return jnp.dot(left, right, preferred_element_type=jnp.float32)


def matmul_back(left, right):
    return lax.dot_general(
        left, right, (((1,), (1,)), ((), ())), preferred_element_type=jnp.float32
    )


def outer_sum(left, right):
    return lax.dot_general(
        left, right, (((0,), (0,)), ((), ())), preferred_element_type=jnp.float32
    )


def plain(
    patches,
    lengths,
    tasks,
    w_query,
    w_key,
    w_value,
    w_out,
    w_gate,
    w_up,
    w_down,
    gain_attn,
    gain_mlp,
    task_table,
    cotangent,
):
    gathered = (
        lax.all_gather(w_query, "fsdp", axis=0, tiled=True),
        lax.all_gather(w_key, "fsdp", axis=0, tiled=True),
        lax.all_gather(w_value, "fsdp", axis=0, tiled=True),
        lax.all_gather(w_out, "fsdp", axis=0, tiled=True),
        lax.all_gather(w_gate, "fsdp", axis=0, tiled=True),
        lax.all_gather(w_up, "fsdp", axis=0, tiled=True),
        lax.all_gather(w_down, "fsdp", axis=0, tiled=True),
        lax.all_gather(gain_attn, "fsdp", axis=0, tiled=True),
        lax.all_gather(gain_mlp, "fsdp", axis=0, tiled=True),
        lax.all_gather(task_table, "fsdp", axis=0, tiled=True),
    )
    query_w, key_w, value_w, out_w, gate_w, up_w, down_w, gain_one, gain_two, table = gathered
    source = patches[0].astype(jnp.float32)
    count, width = source.shape
    scale = HEAD_DIM ** (-0.5)
    span = min(512, count)
    blocks = count // span
    gain_one = gain_one.astype(jnp.float32)
    gain_two = gain_two.astype(jnp.float32)
    picked = (jnp.arange(table.shape[1]) == tasks[0]).astype(jnp.float32)
    resid = source + jnp.sum(table.astype(jnp.float32) * picked[None, :], axis=1)[None, :]
    normed = normalize(resid, gain_one).astype(jnp.bfloat16)
    query = matmul(normed, query_w).astype(jnp.bfloat16).reshape(count, HEADS, HEAD_DIM)
    keys = matmul(normed, key_w).astype(jnp.bfloat16).reshape(count, HEADS, HEAD_DIM)
    values = matmul(normed, value_w).astype(jnp.bfloat16).reshape(count, HEADS, HEAD_DIM)
    valid = (jnp.arange(count) < lengths[0])[None, None, :]

    def scores_of(rows):
        raw = jnp.einsum("qhd,khd->hqk", rows, keys, preferred_element_type=jnp.float32) * scale
        return jnp.where(valid, raw, FAR)

    contexts = []
    logsums = []
    for index in range(blocks):
        rows = query[index * span : (index + 1) * span]
        scores = scores_of(rows)
        top = jnp.max(scores, axis=-1, keepdims=True)
        expd = jnp.exp(scores - top)
        total = jnp.sum(expd, axis=-1, keepdims=True)
        probs = (expd / total).astype(jnp.bfloat16)
        block_out = jnp.einsum("hqk,khd->qhd", probs, values, preferred_element_type=jnp.float32)
        contexts.append(block_out.reshape(span, width).astype(jnp.bfloat16))
        logsums.append(top + jnp.log(total))
    context = jnp.concatenate(contexts, axis=0)
    mixed = resid + matmul(context, out_w)
    normed_two = normalize(mixed, gain_two).astype(jnp.bfloat16)
    gate = matmul(normed_two, gate_w)
    up = matmul(normed_two, up_w)
    hidden = gated(gate, up).astype(jnp.bfloat16)
    output = (mixed + matmul(hidden, down_w)).astype(jnp.bfloat16)[None]
    fetched = (
        lax.all_gather(w_query, "fsdp", axis=0, tiled=True),
        lax.all_gather(w_key, "fsdp", axis=0, tiled=True),
        lax.all_gather(w_value, "fsdp", axis=0, tiled=True),
        lax.all_gather(w_out, "fsdp", axis=0, tiled=True),
        lax.all_gather(w_gate, "fsdp", axis=0, tiled=True),
        lax.all_gather(w_up, "fsdp", axis=0, tiled=True),
        lax.all_gather(w_down, "fsdp", axis=0, tiled=True),
        lax.all_gather(gain_attn, "fsdp", axis=0, tiled=True),
        lax.all_gather(gain_mlp, "fsdp", axis=0, tiled=True),
        lax.all_gather(task_table, "fsdp", axis=0, tiled=True),
    )
    query_w, key_w, value_w, out_w, gate_w, up_w, down_w, gain_one, gain_two, table = fetched
    gain_one = gain_one.astype(jnp.float32)
    gain_two = gain_two.astype(jnp.float32)
    upstream = cotangent[0].astype(jnp.float32)
    branch_grad = upstream.astype(jnp.bfloat16)
    grad_down = outer_sum(hidden, branch_grad)
    hidden_grad = matmul_back(branch_grad, down_w)
    _, pull_gated = jax.vjp(gated, gate, up)
    gate_grad, up_grad = pull_gated(hidden_grad)
    gate_grad = gate_grad.astype(jnp.bfloat16)
    up_grad = up_grad.astype(jnp.bfloat16)
    grad_gate = outer_sum(normed_two, gate_grad)
    grad_up = outer_sum(normed_two, up_grad)
    second_grad = matmul_back(gate_grad, gate_w) + matmul_back(up_grad, up_w)
    _, pull_second = jax.vjp(normalize, mixed, gain_two)
    mixed_grad, grad_gain_two = pull_second(second_grad)
    mixed_grad = mixed_grad + upstream
    attn_grad = mixed_grad.astype(jnp.bfloat16)
    grad_out = outer_sum(context, attn_grad)
    context_grad = (
        matmul_back(attn_grad, out_w).astype(jnp.bfloat16).reshape(count, HEADS, HEAD_DIM)
    )
    key_grad = jnp.zeros((count, HEADS, HEAD_DIM), jnp.float32)
    value_grad = jnp.zeros((count, HEADS, HEAD_DIM), jnp.float32)
    query_parts = []
    for index in range(blocks):
        rows = query[index * span : (index + 1) * span]
        back_rows = context_grad[index * span : (index + 1) * span]
        probs = jnp.exp(scores_of(rows) - logsums[index])
        probs_low = probs.astype(jnp.bfloat16)
        prob_grad = jnp.einsum(
            "qhd,khd->hqk", back_rows, values, preferred_element_type=jnp.float32
        )
        weighted = jnp.sum(probs * prob_grad, axis=-1, keepdims=True)
        score_grad = (probs * (prob_grad - weighted)).astype(jnp.bfloat16)
        query_parts.append(
            jnp.einsum("hqk,khd->qhd", score_grad, keys, preferred_element_type=jnp.float32) * scale
        )
        key_grad = (
            key_grad
            + jnp.einsum("hqk,qhd->khd", score_grad, rows, preferred_element_type=jnp.float32)
            * scale
        )
        value_grad = value_grad + jnp.einsum(
            "hqk,qhd->khd", probs_low, back_rows, preferred_element_type=jnp.float32
        )
    query_grad = jnp.concatenate(query_parts, axis=0).reshape(count, width).astype(jnp.bfloat16)
    key_grad = key_grad.reshape(count, width).astype(jnp.bfloat16)
    value_grad = value_grad.reshape(count, width).astype(jnp.bfloat16)
    grad_query = outer_sum(normed, query_grad)
    grad_key = outer_sum(normed, key_grad)
    grad_value = outer_sum(normed, value_grad)
    first_grad = (
        matmul_back(query_grad, query_w)
        + matmul_back(key_grad, key_w)
        + matmul_back(value_grad, value_w)
    )
    _, pull_first = jax.vjp(normalize, resid, gain_one)
    resid_grad, grad_gain_one = pull_first(first_grad)
    resid_grad = resid_grad + mixed_grad
    grad_table = jnp.sum(resid_grad, axis=0)[:, None] * picked[None, :]
    shares = (
        lax.psum_scatter(grad_query, "fsdp", scatter_dimension=0, tiled=True),
        lax.psum_scatter(grad_key, "fsdp", scatter_dimension=0, tiled=True),
        lax.psum_scatter(grad_value, "fsdp", scatter_dimension=0, tiled=True),
        lax.psum_scatter(grad_out, "fsdp", scatter_dimension=0, tiled=True),
        lax.psum_scatter(grad_gate, "fsdp", scatter_dimension=0, tiled=True),
        lax.psum_scatter(grad_up, "fsdp", scatter_dimension=0, tiled=True),
        lax.psum_scatter(grad_down, "fsdp", scatter_dimension=0, tiled=True),
        lax.psum_scatter(grad_gain_one, "fsdp", scatter_dimension=0, tiled=True),
        lax.psum_scatter(grad_gain_two, "fsdp", scatter_dimension=0, tiled=True),
        lax.psum_scatter(grad_table, "fsdp", scatter_dimension=0, tiled=True),
    )
    (
        share_query,
        share_key,
        share_value,
        share_out,
        share_gate,
        share_up,
        share_down,
        share_one,
        share_two,
        share_table,
    ) = shares
    summed = (
        lax.psum(share_query.astype(jnp.bfloat16), "rep").astype(jnp.float32),
        lax.psum(share_key.astype(jnp.bfloat16), "rep").astype(jnp.float32),
        lax.psum(share_value.astype(jnp.bfloat16), "rep").astype(jnp.float32),
        lax.psum(share_out.astype(jnp.bfloat16), "rep").astype(jnp.float32),
        lax.psum(share_gate.astype(jnp.bfloat16), "rep").astype(jnp.float32),
        lax.psum(share_up.astype(jnp.bfloat16), "rep").astype(jnp.float32),
        lax.psum(share_down.astype(jnp.bfloat16), "rep").astype(jnp.float32),
        lax.psum(share_one.astype(jnp.bfloat16), "rep").astype(jnp.float32),
        lax.psum(share_two.astype(jnp.bfloat16), "rep").astype(jnp.float32),
        lax.psum(share_table.astype(jnp.bfloat16), "rep").astype(jnp.float32),
    )
    return (
        output,
        resid_grad[None],
        summed[0],
        summed[1],
        summed[2],
        summed[3],
        summed[4],
        summed[5],
        summed[6],
        summed[7],
        summed[8],
        summed[9],
    )


PARTS = [1, 1, 1, 1, 1, 1, 1, 2, 1, 2, 1, 1, 1, 1, 2, 1, 1]

UP_SKIP = (0, 0, 0, 128)

LAST_PARTS = 3

EVENTS = {
    "start": [("Z", 0), ("Z", 1)],
    "ready": [("Z", 2)],
    "pre": [
        ("Y", 0), ("Z", 3), ("Y", 1), ("X", 0), ("Z", 4), ("Y", 2), ("X", 1), ("Z", 5), ("Y", 3),
        ("C", 0), ("Z", 6), ("X", 2), ("Y", 4), ("D", 0),
    ],
    "forward": {
        1: [("X", 3), ("Y", 5), ("Z", 7)],
        2: [("D", 1), ("C", 2), ("X", 4), ("Z", 8), ("Z", 9)],
        3: [("C", 3), ("X", 5), ("Y", 6)],
        4: [("D", 2), ("C", 4), ("Y", 7), ("Y", 8), ("Z", 10)],
        5: [("C", 5), ("Z", 11)],
        6: [("D", 3), ("X", 6), ("Y", 9)],
        7: [("X", 8), ("Y", 10), ("Z", 13)],
        8: [("D", 4)],
        9: [("C", 6), ("X", 9), ("Y", 12), ("Z", 14)],
        10: [("D", 5), ("C", 7), ("C", 9), ("X", 10), ("Z", 15)],
        11: [("X", 11), ("Y", 13)],
    },
    "projected": {
        0: [("C", 1)],
        6: [("X", 7), ("Z", 12)],
        8: [("Y", 11)],
        10: [("C", 8)],
    },
    "attended": [
        ("D", 6), ("C", 10), ("X", 12), ("Y", 14), ("Z", 16), ("F", 0), ("F", 1), ("F", 2),
        ("F", 3), ("F", 4), ("F", 5),
    ],
    "project": {
    },
    "normed": [("C", 11), ("Z", 17)],
    "block": {
        0: [("D", 7), ("D", 8), ("D", 9), ("D", 10), ("Y", 15), ("X", 13), ("C", 13), ("D", 11)],
        1: [("X", 14), ("Z", 18)],
        2: [("C", 12), ("Y", 16), ("Z", 19)],
        4: [("D", 12), ("D", 13), ("X", 16), ("Y", 19)],
        5: [("X", 17)],
        7: [("C", 16), ("X", 18)],
        8: [("D", 14), ("D", 15), ("D", 16), ("D", 17), (0, 0), (0, 1), (0, 2)],
        10: [("C", 18)],
        12: [("D", 18), ("D", 19), (1, 2)],
    },
    "outer": {
        0: [("F", 7), ("F", 8), ("F", 9), ("F", 10), ("F", 11), ("X", 15), ("Y", 17)],
        1: [("C", 14), ("C", 15), ("Y", 18)],
        2: [("F", 12), ("F", 13), ("X", 19)],
        3: [("C", 17)],
        4: [("F", 14), ("F", 15), ("F", 16), ("F", 17), (1, 0)],
        5: [("C", 19), (1, 1)],
        6: [("F", 18), ("F", 19)],
        7: [(2, 0)],
    },
    "ff_done": [(2, 1), (0, 3), (0, 4), (0, 5)],
    "second_back": [("F", 6)],
    "context_back": [(3, 0), (2, 2), (1, 3), (0, 6)],
    "backward": {
        0: [(1, 4)],
        1: [(3, 1), (3, 2), (1, 5), (1, 6), (0, 7)],
        2: [(4, 0), (2, 3), (1, 7)],
        3: [(4, 1), (4, 2), (2, 4), (0, 8)],
        4: [(5, 1), (3, 3), (1, 8)],
        5: [(2, 5), (2, 7), (0, 9)],
        6: [(3, 4), (2, 6), (2, 8), (1, 9)],
        7: [(5, 0), (5, 2), (4, 3), (4, 4), (3, 5), (0, 10)],
        8: [(6, 0), (6, 2), (5, 3), (5, 4), (3, 6), (3, 7), (1, 10), (2, 9)],
        9: [(6, 3), (4, 7), (3, 8), (0, 11), (4, 5)],
        10: [(4, 6), (5, 7), (4, 8), (2, 10), (1, 11), (5, 5)],
        11: [(6, 5), (5, 6), (5, 8), (3, 9), (0, 12), (0, 13), (0, 14)],
    },
    "attention_back": [(2, 11)],
    "last": {
        0: [(1, 12), (1, 13), (1, 14), (3, 10)],
        1: [(2, 12), (6, 6), (4, 9)],
        2: [(2, 13), (2, 14), (4, 10), (3, 11)],
        3: [(5, 9), (3, 12)],
    },
    "tail_one": [(3, 13), (3, 14), (5, 10), (4, 11), (4, 12)],
    "tail_two": [(4, 13), (4, 14)],
    "tail_three": [(5, 11), (5, 12), (5, 13), (5, 14)],
}


BF16 = jnp.bfloat16
F32 = jnp.float32
MESH = pl.DeviceIdType.MESH
PAIR = 2


def dot(left, right, on_left, on_right):
    return lax.dot_general(
        left, right, (((on_left,), (on_right,)), ((), ())), preferred_element_type=F32
    )


def aligned(index, step):
    return pl.multiple_of(index, step)


class Place:
    def __init__(self, reps, group):
        self.reps, self.group, self.deep = reps, group, group // PAIR
        self.rep = lax.axis_index("rep")
        self.pos = lax.axis_index("fsdp")
        self.x, self.core = self.rep // PAIR, self.rep % PAIR
        self.z, self.y = self.pos // PAIR, self.pos % PAIR

    def sibling(self):
        return (self.x * PAIR + 1 - self.core, self.pos)

    def across(self):
        return ((1 - self.x) * PAIR + self.core, self.pos)

    def beside(self):
        return (self.rep, self.z * PAIR + 1 - self.y)

    def deeper(self, step):
        return lax.rem(self.z + step, self.deep)

    def along(self, step):
        return (self.rep, self.deeper(step) * PAIR + self.y)

    def member(self, step):
        return (lax.rem(self.rep + step, self.reps), self.pos)

    def peer(self, step):
        return (self.rep, lax.rem(self.pos + step, self.group))


def send(source, target, send_sem, recv_sem, device):
    return pltpu.make_async_remote_copy(
        src_ref=source,
        dst_ref=target,
        send_sem=send_sem,
        recv_sem=recv_sem,
        device_id=device,
        device_id_type=MESH,
    )


class Gather:
    def __init__(self, place, ref, rows, base, half, skip, by_rows, along_sems, hop_sems):
        self.p, self.ref, self.half, self.skip = place, ref, half, skip
        self.along_sems, self.hop_sems = along_sems, hop_sems
        first, held = rows
        if by_rows:
            self.rows = pl.ds(aligned(first + place.core * held, 16), held)
            self.base = base
        else:
            self.rows = pl.ds(first, held)
            self.base = base + place.core * half

    def carried(self):
        p = self.p
        return pl.ds(
            aligned(self.base + p.x * self.skip, 128),
            self.half - self.skip,
        )

    def own(self):
        return self.ref.at[self.p.z, self.p.y, self.rows, self.carried()]

    def copies_z(self):
        p, out = self.p, []
        for step in range(1, p.deep):
            out.append(
                send(
                    self.own(),
                    self.own(),
                    self.along_sems.at[0, step - 1],
                    self.along_sems.at[1, step - 1],
                    p.along(step),
                )
            )
        return out

    def hop(self, index, part, device):
        return send(
            part, part, self.hop_sems.at[0, index], self.hop_sems.at[1, index], device
        )

    def copy_y(self):
        part = self.ref.at[:, self.p.y, self.rows, self.carried()]
        return self.hop(0, part, self.p.beside())

    def copy_x(self):
        p = self.p
        start = self.base + p.x * (self.half - self.skip)
        part = self.ref.at[:, :, self.rows, pl.ds(aligned(start, 128), self.skip)]
        return self.hop(1, part, p.across())

    def copy_core(self):
        p = self.p
        part = self.ref.at[:, :, self.rows, pl.ds(aligned(self.base, 128), self.half)]
        return self.hop(2, part, p.sibling())

    def start_z(self):
        for copy in self.copies_z():
            copy.start()

    def start_y(self):
        for copy in self.copies_z():
            copy.wait_recv()
        self.copy_y().start()

    def start_x(self):
        self.copy_y().wait_recv()
        if self.skip:
            self.copy_x().start()

    def start_core(self):
        if self.skip:
            self.copy_x().wait_recv()
        self.copy_core().start()

    def arrive(self):
        self.copy_core().wait_recv()

    def finish(self):
        for copy in self.copies_z():
            copy.wait_send()
        self.copy_y().wait_send()
        if self.skip:
            self.copy_x().wait_send()
        self.copy_core().wait_send()


class Reduce:
    def __init__(self, place, ref, recv, first, second, third, res, sems, x_first, start=0):
        self.p, self.ref, self.recv, self.first = place, ref, recv, first
        self.second, self.third, self.res, self.sems = second, third, res, sems
        self.x_first = x_first
        self.rows, self.half = recv.shape[2], recv.shape[3]
        self.by_rows, self.start = ref.shape[2] > self.rows, start
        self.steps = 6 if x_first else 5

    def share(self, core):
        if self.by_rows:
            start = core * (self.ref.shape[2] // 2) + self.start
            return pl.ds(aligned(start, 16), self.rows), slice(None)
        return slice(None), pl.ds(aligned(core * self.half, 128), self.half)

    def columns(self, core):
        return self.share(core)[1]

    def one(self, index, source, target, device):
        return send(source, target, self.sems.at[0, index], self.sems.at[1, index], device)

    def split(self, x):
        return pl.ds(aligned(x * (self.rows // 2), 16), self.rows // 2)

    def copies(self, phase):
        p = self.p
        if phase == 0:
            part = self.ref.at[(slice(None), slice(None), *self.share(1 - p.core))]
            return [self.one(0, part, self.recv, p.sibling())]
        if self.x_first:
            if phase == 1:
                part = self.recv.at[:, :, self.split(1 - p.x), :]
                return [self.one(1, part, self.first, p.across())]
            if phase == 2:
                return [self.one(2, self.first.at[:, 1 - p.y], self.second, p.beside())]
            if phase == 3:
                return [
                    self.one(
                        2 + step,
                        self.second.at[p.deeper(step)],
                        self.third.at[step - 1],
                        p.along(step),
                    )
                    for step in range(1, p.deep)
                ]
            last = 2 + p.deep
            if phase == 4:
                part = self.res.at[self.split(p.x), self.columns(p.core)]
                return [self.one(last, part, part, p.across())]
            part = self.res.at[self.share(p.core)]
            return [self.one(last + 1, part, part, p.sibling())]
        if phase == 1:
            return [self.one(1, self.recv.at[:, 1 - p.y], self.first, p.beside())]
        if phase == 2:
            return [
                self.one(
                    1 + step,
                    self.first.at[p.deeper(step)],
                    self.second.at[step - 1],
                    p.along(step),
                )
                for step in range(1, p.deep)
            ]
        last = 1 + p.deep
        if phase == 3:
            return [self.one(last, self.first.at[p.z], self.third, p.across())]
        part = self.res.at[self.share(p.core)]
        return [self.one(last + 1, part, part, p.sibling())]

    def add(self, phase):
        p = self.p
        if phase == 0:

            def fold(index, _):
                a, b = index // PAIR, index % PAIR
                self.recv[a, b] = self.recv[a, b] + self.ref[(a, b, *self.share(p.core))]
                return 0

            lax.fori_loop(0, p.deep * PAIR, fold, 0)
        elif self.x_first:
            if phase == 1:

                def fold(index, _):
                    a, b = index // PAIR, index % PAIR
                    self.first[a, b] = self.first[a, b] + self.recv[a, b, self.split(p.x), :]
                    return 0

                lax.fori_loop(0, p.deep * PAIR, fold, 0)
            elif phase == 2:

                def fold(index, _):
                    self.second[index] = self.second[index] + self.first[index, p.y]
                    return 0

                lax.fori_loop(0, p.deep, fold, 0)
            elif phase == 3:
                total = self.second[p.z].astype(F32)
                for step in range(1, p.deep):
                    total = total + self.third[step - 1].astype(F32)
                self.res[self.split(p.x), self.columns(p.core)] = total.astype(BF16)
        elif phase == 1:

            def fold(index, _):
                self.first[index] = self.first[index] + self.recv[index, p.y]
                return 0

            lax.fori_loop(0, p.deep, fold, 0)
        elif phase == 2:
            total = self.first[p.z].astype(F32)
            for step in range(1, p.deep):
                total = total + self.second[step - 1].astype(F32)
            self.first[p.z] = total.astype(BF16)
        elif phase == 3:
            self.res[self.share(p.core)] = self.first[p.z] + self.third[...]

    def step(self, phase):
        if phase > 0:
            for copy in self.copies(phase - 1):
                copy.wait()
            self.add(phase - 1)
        if phase < self.steps:
            for copy in self.copies(phase):
                copy.start()


def layer(config, *refs):
    (reps, group, count, width, heads, hidden, tasks_held) = config
    (
        lengths_ref, tasks_ref, gain_one_ref, gain_two_ref, table_ref, patches_ref, cot_ref,
        wq_ref, wk_ref, wv_ref, wo_ref, wg_ref, wu_ref, wd_ref,
        out_ref, grad_ref, done_in, done_gate, done_up, done_down, done_small, spare,
        w_in, w_out, w_ff, w_down,
        normed, qkv, context, extra, mixed, tokens, second, hid, both_g,
        acc_out, acc_in, key_extra, vectors, small_buf, small_grads, member_buf, peer_out, peer_buf,
        *rest,
    ) = refs
    p = Place(reps, group)
    deep = p.deep
    head_dim = width // heads
    scale = head_dim ** -0.5
    groups = width // 256
    quad = heads // groups
    rows = wo_ref.shape[0]
    down_rows = wd_ref.shape[0] // 2
    (
        local_sems, along_sems, hop_sems, small_sems, member_sems, peer_sems, red_sems, out_sems,
        *red_bufs,
    ) = rest

    specs = []
    cuts = [0]

    def spec(ref, base, half, skip):
        parts = PARTS[len(cuts) - 1]
        held_rows = ref.shape[2] // parts
        for i in range(parts):
            specs.append((ref, (i * held_rows, held_rows), base, half, skip, False))
        cuts.append(len(specs))

    pairs = 2 * groups
    for pair in range(pairs):
        specs.append((w_in.at[pair // 2], (0, rows // 2), (pair % 2) * 384, 384, 128, True))
        cuts.append(len(specs))
    spec(w_out.at[0], 0, 384, 128)
    for j in range(2):
        for u in range(2):
            spec(w_ff.at[j], u * 512, 256, 128)
            spec(w_ff.at[2 + j], u * 512, 256, UP_SKIP[2 * j + u])
            if u == 0:
                spec(w_down.at[j], 0, 384, 128)
    chunks = [Gather(p, *one, along_sems.at[i], hop_sems.at[i]) for i, one in enumerate(specs)]

    sem = 0
    fills = [[] for _ in PARTS]
    own_rows = pl.ds(aligned(p.core * (rows // 2), 16), rows // 2)
    for pair in range(pairs):
        for i in range(2):
            source = pl.ds(pair * 128, 128)
            start = (pair % 2) * 384 + (p.x + i) * 128
            target = w_in.at[pair // 2, p.z, p.y, own_rows, pl.ds(aligned(start, 128), 128)]
            choice = (wq_ref, wk_ref) if i == 0 else (wk_ref, wv_ref)
            fills[pair].append(
                tuple(
                    pltpu.make_async_copy(w.at[own_rows, source], target, local_sems.at[sem])
                    for w in choice
                )
            )
            sem += 1
    columns = pl.ds(aligned(p.core * 384 + p.x * 128, 128), 256)
    fills[pairs].append(
        pltpu.make_async_copy(
            wo_ref.at[:, columns], w_out.at[0, p.z, p.y, :, columns], local_sems.at[sem]
        )
    )
    sem += 1
    at = pairs + 1

    def fill(source, target):
        nonlocal sem
        fills[at].append(pltpu.make_async_copy(source, target, local_sems.at[sem]))
        sem += 1

    def segment(ref, held, j, seg):
        fill(
            ref.at[:, pl.ds(aligned(seg * 256 + j * 128, 128), 128)],
            held.at[p.z, p.y, :, pl.ds(aligned(seg * 128, 128), 128)],
        )

    for j in range(2):
        for u in range(2):
            segment(wg_ref, w_ff.at[j], j, 4 * u + 2 * p.core + p.x)
            at += 1
            if UP_SKIP[2 * j + u]:
                segment(wu_ref, w_ff.at[2 + j], j, 4 * u + 2 * p.core + p.x)
            else:
                for i in range(2):
                    segment(wu_ref, w_ff.at[2 + j], j, 4 * u + 2 * p.core + i)
            at += 1
            if u == 0:
                fill(
                    wd_ref.at[pl.ds(j * down_rows, down_rows), columns],
                    w_down.at[j, p.z, p.y, :, columns],
                )
                at += 1

    def fill_start(i):
        for copy in fills[i]:
            if isinstance(copy, tuple):
                for x in range(2):

                    @pl.when(p.x == x)
                    def _(copy=copy, x=x):
                        copy[x].start()
            else:
                copy.start()

    def fill_wait(i):
        for copy in fills[i]:
            (copy[0] if isinstance(copy, tuple) else copy).wait()

    reds = []
    grads = []
    for j in range(2):
        grads += [
            (w_ff.at[j], done_gate.at[j], True),
            (w_ff.at[2 + j], done_up.at[j], False),
            (w_down.at[j], done_down.at[j], True),
        ]
    grads += [(w_out.at[0], done_in.at[groups], True)]
    for pair in range(pairs):
        columns = pl.ds((pair % 2) * 384, 384)
        grads.append(
            (
                w_ff.at[pair // 2, :, :, :, columns],
                done_in.at[pair // 2, :, columns],
                False,
            )
        )
    take = iter(red_bufs)
    results = []
    for i, (ref, _, x_first) in enumerate(grads):
        res = next(take)
        results.append(res)
        parts = LAST_PARTS if i == len(grads) - 1 else 1
        for k in range(parts):
            bufs = [next(take) for _ in range(4)]
            start = k * (rows // 2 // parts)
            sems = red_sems.at[len(reds)]
            reds.append(Reduce(p, ref, *bufs, res, sems, x_first, start))

    tokens_in = pltpu.make_async_copy(patches_ref, tokens, out_sems.at[0])
    tokens_in.start()
    for i in range(len(fills)):
        fill_start(i)
    shard = width // group
    own_small = jnp.concatenate(
        [ref[...].astype(F32) for ref in (gain_one_ref, gain_two_ref, table_ref)]
        + [jnp.zeros((14 - tasks_held, shard), F32)],
        0,
    )
    small_buf[p.pos] = jnp.concatenate(
        [own_small, jnp.zeros((16, 128 - shard), F32)], 1
    ).astype(BF16)
    barrier = pltpu.get_barrier_semaphore()
    for step in range(1, reps):
        pl.semaphore_signal(barrier, inc=1, device_id=p.member(step), device_id_type=MESH)
    for step in range(1, group):
        pl.semaphore_signal(barrier, inc=1, device_id=p.peer(step), device_id_type=MESH)
    pl.semaphore_wait(barrier, reps + group - 2)
    small_copies = [
        send(
            small_buf.at[p.pos], small_buf.at[p.pos],
            small_sems.at[0, step - 1], small_sems.at[1, step - 1], p.peer(step),
        )
        for step in range(1, group)
    ]
    for copy in small_copies:
        copy.start()

    def go(*events):
        for kind, i in events:
            if kind == "Z":
                if i in cuts:
                    fill_wait(cuts.index(i))
                chunks[i].start_z()
            elif kind == "Y":
                chunks[i].start_y()
            elif kind == "X":
                chunks[i].start_x()
            elif kind == "C":
                chunks[i].start_core()
            elif kind == "D":
                chunks[i].arrive()
            elif kind == "F":
                chunks[i].finish()
            else:
                reds[i].step(kind)

    go(*EVENTS["start"])

    for copy in small_copies:
        copy.wait_recv()
    wide_row = lax.broadcasted_iota(jnp.int32, (128, width), 0)
    wide_col = lax.broadcasted_iota(jnp.int32, (128, width), 1)
    total = None
    for f in range(group):
        place_f = jnp.logical_and(wide_col == wide_row + f * shard, wide_row < shard)
        part = dot(small_buf[f], place_f.astype(F32).astype(BF16), 1, 0)
        total = part if total is None else total + part
    vectors[...] = total
    task = tasks_ref[0]
    chosen = [(task == k).astype(F32) for k in range(tasks_held)]

    def task_row():
        row = vectors[2:3, :] * chosen[0]
        for k in range(1, tasks_held):
            row = row + vectors[2 + k : 3 + k, :] * chosen[k]
        return row

    position = lax.broadcasted_iota(jnp.int32, (16, count), 1)
    kind = lax.broadcasted_iota(jnp.int32, (16, count), 0)
    mask = jnp.where(position < lengths_ref[0], 0.0, FAR)
    key_extra[...] = jnp.where(
        kind < 3, 1.0, jnp.where(kind == 3, mask, 0.0)
    ).astype(BF16)

    tokens_in.wait()
    block = 256
    blocks = count // block

    def rows_of(i, size=block):
        return pl.ds(aligned(i * size, size), size)

    def norm_one(i, _):
        r = rows_of(i)
        resid = tokens[r, :].astype(F32) + task_row()
        inv = lax.rsqrt(jnp.mean(resid * resid, axis=-1, keepdims=True) + EPS)
        normed[r, :] = (resid * inv * vectors[0:1, :]).astype(BF16)
        return 0

    go(*EVENTS["ready"])
    lax.fori_loop(0, blocks, norm_one, 0)

    go(*EVENTS["pre"])

    def project(pair):
        g = pair // 2
        base = aligned((pair % 2) * 384, 128)
        weight = w_in[g, :, :, :, pl.ds(base, 384)].reshape(width, 384)
        got = dot(weight, normed[...], 0, 1)
        qkv[g, pl.ds(base, 128)] = (got[:128] * scale).astype(BF16)
        qkv[g, pl.ds(base + 128, 256)] = got[128:].astype(BF16)

    tile = 256
    tiles = count // tile
    sixteen = lax.broadcasted_iota(jnp.int32, (16, count), 0)

    def offsets(h):
        g, left = h // quad, h % quad
        return g, (left // 2) * 384 + (left % 2) * head_dim

    def forward_head(h):
        g, off = offsets(h)
        ask = jnp.concatenate(
            [
                qkv[g, pl.ds(aligned(off, 64), head_dim), :],
                (sixteen == 3).astype(F32).astype(BF16),
            ],
            0,
        )
        scores, top = [], None
        for j in range(tiles):
            cut = slice(j * tile, (j + 1) * tile)
            keys = jnp.concatenate(
                [qkv[g, pl.ds(aligned(off + 128, 64), head_dim), cut], key_extra[:, cut]], 0
            )
            s = dot(keys, ask, 0, 0)
            scores.append(s)
            here = jnp.max(s, axis=0, keepdims=True)
            top = here if top is None else jnp.maximum(top, here)
        acc = None
        for j in range(tiles):
            cut = slice(j * tile, (j + 1) * tile)
            expd = jnp.exp(scores[j] - top).astype(BF16)
            vals = jnp.concatenate(
                [
                    qkv[g, pl.ds(aligned(off + 256, 64), head_dim), cut],
                    jnp.ones((16, tile), BF16),
                ],
                0,
            )
            part = dot(vals, expd, 1, 0)
            acc = part if acc is None else acc + part
        total = acc[head_dim : head_dim + 1]
        exact = acc[:head_dim] * (1.0 / total)
        low = exact.astype(BF16)
        missing = (exact - low.astype(F32)).astype(BF16)
        r = pl.ds(aligned(h * head_dim, 64), head_dim)
        context[r, :] = low
        both_g[r, :] = missing
        extra[0, pl.ds(h, 1), :] = -(top + jnp.log(total))

    def splits(row, fourth):
        high = row.astype(BF16).astype(F32)
        mid = (row - high).astype(BF16).astype(F32)
        low = row - high - mid
        return jnp.where(
            sixteen == 0,
            high,
            jnp.where(
                sixteen == 1,
                mid,
                jnp.where(sixteen == 2, low, jnp.where(sixteen == 3, fourth, 0.0)),
            ),
        ).astype(BF16)

    def each_head(h, _):
        for at, events in EVENTS["forward"].items():

            @pl.when(h == at)
            def _(events=events):
                go(*events)

        @pl.when(h % 2 == 0)
        def _():
            project(h // 2)

        for at, events in EVENTS["projected"].items():

            @pl.when(h == at)
            def _(events=events):
                go(*events)

        forward_head(h)
        return 0

    lax.fori_loop(0, heads, each_head, 0)
    kept = both_g.at[pl.ds(0, width), :]
    first_out = 6 + len(grads)
    keep = pltpu.make_async_copy(kept, spare, out_sems.at[first_out])
    fetch = pltpu.make_async_copy(spare, kept, out_sems.at[first_out + 1])
    keep.start()
    go(*EVENTS["attended"])

    big = 256

    def out_project(i, _):
        for at, events in EVENTS["project"].items():

            @pl.when(i == at)
            def _(events=events):
                go(*events)

        r = rows_of(i, big)
        m = tokens[r, :].astype(F32) + task_row()
        m = m + dot(context[:, r], w_out[0].reshape(width, width), 0, 0)
        mixed[r, :] = m
        acc_out[r, :] = m
        acc_in[r, :] = jnp.zeros_like(m)
        inv = lax.rsqrt(jnp.mean(m * m, axis=-1, keepdims=True) + EPS)
        second[r, :] = (m * inv * vectors[1:2, :]).astype(BF16)
        return 0

    lax.fori_loop(0, count // big, out_project, 0)
    cot_in = pltpu.make_async_copy(cot_ref, tokens, out_sems.at[1])
    cot_in.start()
    go(*EVENTS["normed"])
    cot_in.wait()

    curve = 0.7978845608028654
    cube = 0.044715
    part = 512
    keep.wait()

    def ff_tile(t, _):
        j, u = t // 2, t % 2
        cols = pl.ds(aligned(u * part, part), part)
        half = pl.ds(u * (deep // 2), deep // 2)

        def block_of(i, _):
            for at, events in EVENTS["block"].items():

                @pl.when(t * (count // big) + i == at)
                def _(events=events):
                    go(*events)

            r = rows_of(i, big)
            gate_w = w_ff[j, :, :, :, cols].reshape(width, part)
            up_w = w_ff[2 + j, :, :, :, cols].reshape(width, part)
            down_w = w_down[j, half].reshape(part, width)
            two = second[r, :]
            gate = dot(two, gate_w, 1, 0)
            up = dot(two, up_w, 1, 0)
            back = dot(tokens[r, :], down_w, 1, 1)
            square = gate * gate
            bend = jnp.tanh(curve * gate * (1.0 + cube * square))
            flat = 0.5 * (1.0 + bend)
            gelu = gate * flat
            slope = flat + 0.5 * gate * (1.0 - bend * bend) * (
                curve * (1.0 + 3.0 * cube * square)
            )
            h = (gelu * up).astype(BF16)
            g_grad = (back * up * slope).astype(BF16)
            u_grad = (back * gelu).astype(BF16)
            hid[r, :] = h
            both_g[r, 0:part] = g_grad
            both_g[r, part : 2 * part] = u_grad
            o = dot(h, down_w, 1, 0)
            n = dot(g_grad, gate_w, 1, 1) + dot(u_grad, up_w, 1, 1)
            acc_out[r, :] = acc_out[r, :] + o
            acc_in[r, :] = acc_in[r, :] + n
            return 0

        lax.fori_loop(0, count // big, block_of, 0)
        def pause(k):
            for at, events in EVENTS["outer"].items():

                @pl.when(t * 2 + k == at)
                def _(events=events):
                    go(*events)

        pause(0)
        w_down[j, half] = (
            dot(hid[...], tokens[...], 0, 0).astype(BF16).reshape(deep // 2, 2, down_rows, width)
        )
        pause(1)
        for v in range(2):
            some = slice(v * width // 2, (v + 1) * width // 2)
            to = slice(v * deep // 2, (v + 1) * deep // 2)
            both = dot(second[:, some], both_g[...], 0, 0).astype(BF16)
            both = both.reshape(deep // 2, 2, rows, 2 * part)
            w_ff[j, to, :, :, cols] = both[..., :part]
            w_ff[2 + j, to, :, :, cols] = both[..., part:]
        return 0

    lax.fori_loop(0, 4, ff_tile, 0)
    fetch.start()
    go(*EVENTS["ff_done"])

    small_grads[...] = jnp.zeros_like(small_grads)

    def second_back(i, _):
        r = rows_of(i)
        m = mixed[r, :]
        second[r, :] = acc_out[r, :].astype(BF16)
        inv = lax.rsqrt(jnp.mean(m * m, axis=-1, keepdims=True) + EPS)
        unit = m * inv
        got = acc_in[r, :]
        scaled = got * vectors[1:2, :]
        grad = tokens[r, :].astype(F32) + inv * (
            scaled - unit * jnp.mean(scaled * unit, axis=-1, keepdims=True)
        )
        small_grads[1:2, :] = small_grads[1:2, :] + jnp.sum(got * unit, axis=0, keepdims=True)
        mixed[r, :] = grad
        tokens[r, :] = grad.astype(BF16)
        return 0

    lax.fori_loop(0, blocks, second_back, 0)
    result = pltpu.make_async_copy(second, out_ref, out_sems.at[2])
    result.start()
    go(*EVENTS["second_back"])

    out_w = w_out[0].reshape(width, width)
    acc_out[0:width, :] = dot(context[...], tokens[...], 1, 0)
    lowered = dot(out_w, tokens[...], 1, 1).astype(BF16)
    fetch.wait()
    for h in range(heads):
        r = slice(h * head_dim, (h + 1) * head_dim)
        low = lowered[r]
        exact = context[r, :].astype(F32) + both_g[r, :].astype(F32)
        delta = jnp.sum(low.astype(F32) * exact, axis=0, keepdims=True)
        extra[1, h : h + 1, :] = -delta
        context[r, :] = low
    w_out[0] = acc_out[0:width, :].astype(BF16).reshape(deep, 2, rows, width)
    go(*EVENTS["context_back"])

    def backward_head(h):
        g, off = offsets(h)
        q_rows = pl.ds(aligned(off, 64), head_dim)
        k_rows = pl.ds(aligned(off + 128, 64), head_dim)
        v_rows = pl.ds(aligned(off + 256, 64), head_dim)
        query = qkv[g, q_rows, :]
        all_keys = qkv[g, k_rows, :]
        all_vals = qkv[g, v_rows, :]
        back = context[pl.ds(aligned(h * head_dim, 64), head_dim), :]
        ask = jnp.concatenate([query, splits(extra[0, pl.ds(h, 1), :], 1.0)], 0)
        back_ask = jnp.concatenate([back, splits(extra[1, pl.ds(h, 1), :], 0.0)], 0)
        query_grad = None
        for j in range(tiles):
            cut = slice(j * tile, (j + 1) * tile)
            keys = all_keys[:, cut]
            lift = key_extra[:, cut]
            probs = jnp.exp(dot(jnp.concatenate([keys, lift], 0), ask, 0, 0))
            gap = dot(jnp.concatenate([all_vals[:, cut], lift], 0), back_ask, 0, 0)
            score_grad = (probs * gap).astype(BF16)
            part = dot(keys, score_grad, 1, 0)
            query_grad = part if query_grad is None else query_grad + part
            qkv[g, k_rows, cut] = dot(query, score_grad, 1, 1).astype(BF16)
            qkv[g, v_rows, cut] = dot(back, probs.astype(BF16), 1, 1).astype(BF16)
        qkv[g, q_rows, :] = (query_grad * scale).astype(BF16)

    def in_grad(pair):
        weight = dot(
            normed[...], qkv[pair // 2, pl.ds(aligned((pair % 2) * 384, 128), 384), :], 0, 1
        )
        w_ff[pair // 2, :, :, :, pl.ds(aligned((pair % 2) * 384, 128), 384)] = weight.astype(
            BF16
        ).reshape(deep, 2, rows, 384)

    def each_back(h, _):
        backward_head(h)

        @pl.when(h % 2 == 1)
        def _():
            in_grad(h // 2)

        for at, events in EVENTS["backward"].items():

            @pl.when(h == at)
            def _(events=events):
                go(*events)

        return 0

    lax.fori_loop(0, heads, each_back, 0)
    result.wait()
    again = pltpu.make_async_copy(patches_ref, second, out_sems.at[3])
    again.start()
    go(*EVENTS["attention_back"])
    again.wait()

    def first_norm_back(i, _):
        for at, events in EVENTS["last"].items():

            @pl.when(i == at)
            def _(events=events):
                go(*events)

        r = rows_of(i)
        got = dot(qkv[0, :, r], w_in[0].reshape(width, width), 0, 1)
        for g in range(1, groups):
            got = got + dot(qkv[g, :, r], w_in[g].reshape(width, width), 0, 1)
        resid = second[r, :].astype(F32) + task_row()
        inv = lax.rsqrt(jnp.mean(resid * resid, axis=-1, keepdims=True) + EPS)
        unit = resid * inv
        scaled = got * vectors[0:1, :]
        grad = mixed[r, :] + inv * (
            scaled - unit * jnp.mean(scaled * unit, axis=-1, keepdims=True)
        )
        small_grads[0:1, :] = small_grads[0:1, :] + jnp.sum(got * unit, axis=0, keepdims=True)
        small_grads[7:8, :] = small_grads[7:8, :] + jnp.sum(grad, axis=0, keepdims=True)
        acc_out[r, :] = grad
        return 0

    lax.fori_loop(0, blocks, first_norm_back, 0)
    grad_out = pltpu.make_async_copy(acc_out, grad_ref, out_sems.at[4])
    grad_out.start()
    for k in range(tasks_held):
        small_grads[2 + k : 3 + k, :] = small_grads[7:8, :] * chosen[k]

    member_buf[p.rep] = small_grads[...]
    member_copies = [
        send(
            member_buf.at[p.rep], member_buf.at[p.rep],
            member_sems.at[0, step - 1], member_sems.at[1, step - 1], p.member(step),
        )
        for step in range(1, reps)
    ]
    for copy in member_copies:
        copy.start()
    go(*EVENTS["tail_one"])
    for copy in member_copies:
        copy.wait_recv()
    summed = member_buf[0]
    for i in range(1, reps):
        summed = summed + member_buf[i]
    peer_out[...] = jnp.zeros_like(peer_out)
    for f in range(group):
        peer_out[f, :, 0:shard] = summed[:, f * shard : (f + 1) * shard]
    peer_copies = []
    for step in range(1, group):
        target = lax.rem(p.pos + step, group)
        peer_copies.append(
            send(
                peer_out.at[target], peer_buf.at[p.pos],
                peer_sems.at[0, step - 1], peer_sems.at[1, step - 1], p.peer(step),
            )
        )
    for copy in peer_copies:
        copy.start()
    peer_buf[p.pos] = peer_out[p.pos]
    go(*EVENTS["tail_two"])
    for copy in peer_copies:
        copy.wait_recv()
    summed = peer_buf[0]
    for i in range(1, group):
        summed = summed + peer_buf[i]
    small_grads[:, 0:128] = summed
    ends = [
        pltpu.make_async_copy(small_grads.at[:, pl.ds(0, 128)], done_small, out_sems.at[5])
    ]
    ends[0].start()
    go(*EVENTS["tail_three"])
    for i, (_, done, _) in enumerate(grads):
        copy = pltpu.make_async_copy(results[i], done, out_sems.at[6 + i])
        copy.start()
        ends.append(copy)
    for copy in small_copies + member_copies + peer_copies:
        copy.wait_send()
    for copy in ends:
        copy.wait()
    grad_out.wait()


def fits(reps, group, args):
    patches, w_query, w_gate, w_down = args[0], args[3], args[7], args[9]
    return (
        reps == 4
        and group == 8
        and patches.shape == (1, 1024, 768)
        and w_query.shape == (96, 768)
        and w_gate.shape == (96, 2048)
        and w_down.shape == (256, 768)
    )


def ending(config, *refs):
    groups, group, rows, held = config
    sources, small = refs[:6], refs[6]
    targets, (one, two, table) = refs[7:16], refs[16:19]
    in_sems, out_sems = refs[19:21]
    held_out, held_grad, from_in, from_gate, from_up, from_down = refs[21:27]
    made = refs[27:34]
    parts = 4
    span = held_out.shape[0] // parts
    brought, copies = [], []
    middles = (from_in, from_gate, from_up, from_down)
    whole = []
    for i in range(parts):
        r = pl.ds(i * span, span)
        for k, middle in enumerate((held_out, held_grad)):
            at = 4 + 2 * i + k
            whole.append(
                (
                    pltpu.make_async_copy(sources[k].at[r], middle.at[r], in_sems.at[at]),
                    pltpu.make_async_copy(middle.at[r], targets[k].at[0, r], out_sems.at[at]),
                )
            )
            whole[-1][0].start()
    for i, (source, middle) in enumerate(zip(sources[2:], middles)):
        brought.append(pltpu.make_async_copy(source, middle, in_sems.at[i]))
        brought[-1].start()

    def finish(i):
        copies.append(pltpu.make_async_copy(made[i], targets[2 + i], out_sems.at[12 + i]))
        copies[-1].start()

    def pass_on(count):
        for _ in range(count):
            first, then = whole.pop(0)
            first.wait()
            then.start()
            copies.append(then)

    brought[0].wait()
    for i in range(3):
        pass_on(1)
        for g in range(groups):
            for core in range(2):
                start = core * 384 + i * 128
                to = g * 256 + core * 128
                made[i][:, to : to + 128] = from_in[g, :, start : start + 128].astype(F32)
        finish(i)
    made[3][...] = from_in[groups].astype(F32)
    finish(3)
    for k, source in enumerate((from_gate, from_up)):
        brought[1 + k].wait()
        for j in range(2):
            for f in range(group):
                to = f * 256 + j * 128
                made[4 + k][:, to : to + 128] = source[j, :, f * 128 : (f + 1) * 128].astype(F32)
        finish(4 + k)
        pass_on(2)
    brought[3].wait()
    half = from_down.shape[1]
    for j in range(2):
        made[6][j * half : (j + 1) * half, :] = from_down[j].astype(F32)
    finish(6)
    pass_on(len(whole))
    one[...] = small[0, :rows]
    two[...] = small[1, :rows]
    table[...] = small[2 : 2 + held, :rows]
    for copy in copies:
        copy.wait()


def fused(
    reps, group, patches, lengths, tasks, w_query, w_key, w_value, w_out, w_gate, w_up, w_down,
    gain_attn, gain_mlp, task_table, cotangent,
):
    count, width = patches.shape[1:]
    rows, hidden = w_gate.shape
    held = task_table.shape[1]
    deep = group // PAIR
    groups = width // 256
    down_rows = w_down.shape[0] // 2

    def of(rows, columns, x_first, row_parts=0):
        half = columns // 2
        shapes = [(rows, columns)]
        if row_parts:
            rows, half = rows // 2 // row_parts, columns
        for _ in range(max(row_parts, 1)):
            shapes.append((deep, 2, rows, half))
            if x_first:
                shapes.append((deep, 2, rows // 2, half))
                shapes.append((deep, rows // 2, half))
                shapes.append((deep - 1, rows // 2, half))
            else:
                shapes.append((deep, rows, half))
                shapes.append((deep - 1, rows, half))
                shapes.append((rows, half))
        return [pltpu.VMEM(shape, BF16) for shape in shapes]

    red_bufs = []
    for j in range(2):
        red_bufs += of(rows, hidden // 2, True)
        red_bufs += of(rows, hidden // 2, False)
        red_bufs += of(down_rows, width, True)
    red_bufs += of(rows, width, True)
    for pair in range(2 * groups):
        red_bufs += of(rows, width // 2, False, LAST_PARTS if pair == 2 * groups - 1 else 1)
    sums = 7 + 2 * groups
    chunks = sum(PARTS)
    scratch = [
        pltpu.VMEM((groups, deep, 2, rows, width), BF16),
        pltpu.VMEM((1, deep, 2, rows, width), BF16),
        pltpu.VMEM((4, deep, 2, rows, hidden // 2), BF16),
        pltpu.VMEM((2, deep, 2, down_rows, width), BF16),
        pltpu.VMEM((count, width), BF16),
        pltpu.VMEM((groups, width, count), BF16),
        pltpu.VMEM((width, count), BF16),
        pltpu.VMEM((2, 16, count), F32),
        pltpu.VMEM((count, width), F32),
        pltpu.VMEM((count, width), BF16),
        pltpu.VMEM((count, width), BF16),
        pltpu.VMEM((count, 512), BF16),
        pltpu.VMEM((count, 1024), BF16),
        pltpu.VMEM((count, width), F32),
        pltpu.VMEM((count, width), F32),
        pltpu.VMEM((16, count), BF16),
        pltpu.VMEM((16, width), F32),
        pltpu.VMEM((group, 16, 128), BF16),
        pltpu.VMEM((8, width), F32),
        pltpu.VMEM((reps, 8, width), F32),
        pltpu.VMEM((group, 8, 128), F32),
        pltpu.VMEM((group, 8, 128), F32),
        pltpu.SemaphoreType.DMA((groups * 4 + 1 + 14,)),
        pltpu.SemaphoreType.DMA((chunks, 2, deep - 1)),
        pltpu.SemaphoreType.DMA((chunks, 2, 3)),
        pltpu.SemaphoreType.DMA((2, group - 1)),
        pltpu.SemaphoreType.DMA((2, reps - 1)),
        pltpu.SemaphoreType.DMA((2, group - 1)),
        pltpu.SemaphoreType.DMA((sums + LAST_PARTS - 1, 2, deep + 4)),
        pltpu.SemaphoreType.DMA((10 + sums,)),
        *red_bufs,
    ]
    shape = jax.ShapeDtypeStruct
    smem = pl.BlockSpec(memory_space=pltpu.SMEM)
    anywhere = pl.BlockSpec(memory_space=pl.ANY)
    config = (reps, group, count, width, HEADS, hidden, held)
    output, grad, done_in, done_gate, done_up, done_down, done_small, _ = pl.pallas_call(
        functools.partial(layer, config),
        out_shape=[
            shape((count, width), BF16),
            shape((count, width), F32),
            shape((groups + 1, rows, width), BF16),
            shape((2, rows, hidden // 2), BF16),
            shape((2, rows, hidden // 2), BF16),
            shape((2, down_rows, width), BF16),
            shape((8, 128), F32),
            shape((width, count), BF16),
        ],
        in_specs=[smem, smem] + [pl.BlockSpec(memory_space=pltpu.VMEM)] * 3 + [anywhere] * 9,
        out_specs=[anywhere] * 8,
        scratch_shapes=scratch,
        compiler_params=pltpu.CompilerParams(
            collective_id=0, has_side_effects=True, vmem_limit_bytes=62 * 1024 * 1024
        ),
        name="layer",
    )(
        lengths, tasks, gain_attn[None], gain_mlp[None], task_table.T, patches[0], cotangent[0],
        w_query, w_key, w_value, w_out, w_gate, w_up, w_down,
    )
    lane = pl.BlockSpec(memory_space=pltpu.VMEM)
    sizes = [(rows, width)] * 4 + [(rows, hidden)] * 2 + [(2 * down_rows, width)]
    results = pl.pallas_call(
        functools.partial(ending, (groups, group, rows, held)),
        out_shape=[
            shape((1, count, width), BF16),
            shape((1, count, width), F32),
            *[shape(size, F32) for size in sizes],
            shape((rows,), F32),
            shape((rows,), F32),
            shape((held, rows), F32),
        ],
        in_specs=[anywhere] * 6 + [lane],
        out_specs=[anywhere] * 9 + [lane] * 3,
        scratch_shapes=[
            pltpu.SemaphoreType.DMA((12,)),
            pltpu.SemaphoreType.DMA((19,)),
            pltpu.VMEM((count, width), BF16),
            pltpu.VMEM((count, width), F32),
            pltpu.VMEM((groups + 1, rows, width), BF16),
            pltpu.VMEM((2, rows, hidden // 2), BF16),
            pltpu.VMEM((2, rows, hidden // 2), BF16),
            pltpu.VMEM((2, down_rows, width), BF16),
            *[pltpu.VMEM(size, F32) for size in sizes],
        ],
        compiler_params=pltpu.CompilerParams(vmem_limit_bytes=62 * 1024 * 1024),
        name="ending",
    )(output, grad, done_in, done_gate, done_up, done_down, done_small)
    return (*results[:11], results[11].T)


def solution(mesh):
    in_specs = (
        P(("rep", "fsdp"), None, None),
        P(("rep", "fsdp")),
        P(("rep", "fsdp")),
        P("fsdp", None),
        P("fsdp", None),
        P("fsdp", None),
        P("fsdp", None),
        P("fsdp", None),
        P("fsdp", None),
        P("fsdp", None),
        P("fsdp"),
        P("fsdp"),
        P("fsdp", None),
        P(("rep", "fsdp"), None, None),
    )
    out_specs = (
        P(("rep", "fsdp"), None, None),
        P(("rep", "fsdp"), None, None),
        P("fsdp", None),
        P("fsdp", None),
        P("fsdp", None),
        P("fsdp", None),
        P("fsdp", None),
        P("fsdp", None),
        P("fsdp", None),
        P("fsdp"),
        P("fsdp"),
        P("fsdp", None),
    )
    reps, group = mesh.shape["rep"], mesh.shape["fsdp"]

    def per_device(*args):
        if fits(reps, group, args):
            return fused(reps, group, *args)
        return plain(*args)

    return jax.shard_map(
        per_device, mesh=mesh, in_specs=in_specs, out_specs=out_specs, check_vma=False
    )
```
